32 devices in a mesh: dp: 8 (over z, y), fsdp: 4 (over x, core).
Axes of the slice: x: 2, y: 2, z: 4, core: 2. Of those that a mesh axis runs over, the one named last changes fastest.
Arguments:
- qkv_codes: bfloat16 [8, 4, 128, 3, 896], P('dp', 'fsdp'), may hold values from -4 to 4, as said below
- block_scales: bfloat16 [8, 4, 128, 3, 7], P('dp', 'fsdp'), may hold values from 0.25 to 2
- home_segments: int32 [8, 4, 128], P('dp', 'fsdp'), may hold values from -1 to 131, as said below
- kept_rows: int32 [8, 4], P('dp', 'fsdp'), may hold values from 32 to 64, as said below
- pack_list: int32 [8, 4, 4, 3], P(None, 'fsdp'), may hold values from 0 to 112, as said below
- w_out: bfloat16 [896, 1792], P('fsdp'), may hold values from -0.1875 to 0.1875
- cotangent: bfloat16 [8, 4, 128, 1792], P('dp', 'fsdp'), may hold values from -4 to 4
Outputs:
- output: bfloat16 [8, 4, 128, 1792], P('dp', 'fsdp')
- grad_codes: bfloat16 [8, 4, 128, 3, 896], P('dp', 'fsdp')
- grad_w_out: float32 [8, 896, 1792], P('dp', 'fsdp')
The draws below stay inside these ranges and needn't reach their ends.
Inputs may be any that keep to these rules, and one draw needn't show every extreme that they name: Rows below kept_rows are whole images or the first part of one, and stay in place; the first image of every device has at least 3 rows. `pack_list`: one table for each fsdp index, the same on all its dp devices. Entry [s, d] describes the one whole image that dp index s sends to s + offset(d), offsets +1, -1, +2, -2, always inside the axis; length 0 means none, with the other entries 0. Lengths run from 3 to 16 and reach 16. Sent images lie at or above the source's kept_rows without intersection; placed images lie at or above the target's kept_rows without intersection, below 128. `home_segments`: kept rows carry their image number, runs of equal numbers; rows of the image sent in direction d carry 128 + d; other rows -1. `qkv_codes`: every entry is a value of the e4m3 8-bit float format.
All inputs are finite; a program needn't handle non-finite values.
Results may differ from the reference program's by a relative error of at most 0.02.
Values may be sent and summed in bfloat16 or wider, within the bound.
A program may use at most 64 MiB of HBM per device.

```python
import math
import jax
import jax.numpy as jnp
from jax import lax

D = 1792
HD = 112
HEADS = 8
ROWS = 128
HW = 896
NB = 7
SLOT = 16
N_DP = 8
N_FSDP = 4


def pack_tables(key):
    key_keep, key_send, key_length, key_images = jax.random.split(key, 4)
    steps_away = (1, -1, 2, -2)
    kept = jax.random.randint(key_keep, (N_DP, N_FSDP), ROWS // 4, ROWS // 2 + 1)
    kept = kept.at[0].set(ROWS // 2).at[1].set(ROWS // 4).at[2].set(ROWS // 2)
    source = jnp.arange(N_DP)[:, None, None]
    direction = jnp.arange(4)[None, None, :]
    target = source + jnp.array(steps_away, jnp.int32)[None, None, :]
    allowed = ((target >= 0) & (target < N_DP)).astype(jnp.int32)
    forced = (source == 0) & (direction == 0) | (source == 1) & (direction == 1) | (source == 0) & (direction == 2) | (source == 2)
    sending = jax.random.randint(key_send, (N_DP, N_FSDP, 4), 0, 2)
    sending = jnp.where(forced, 1, sending) * allowed
    length = jax.random.randint(key_length, (N_DP, N_FSDP, 4), 3, SLOT + 1)
    full_slot = (source == 0) & (direction == 0) | (source == 2) & (direction < 3)
    length = jnp.where(full_slot, SLOT, length) * sending
    home_start = kept[:, :, None] + jnp.cumsum(length, axis=-1) - length
    arriving = jnp.stack([jnp.roll(length[:, :, route], steps_away[route], axis=0) for route in range(4)], axis=-1)
    placed = kept[:, :, None] + jnp.cumsum(arriving, axis=-1) - arriving
    landing = jnp.stack([jnp.roll(placed[:, :, route], -steps_away[route], axis=0) for route in range(4)], axis=-1)
    present = length > 0
    table = jnp.stack([jnp.where(present, home_start, 0), length, jnp.where(present, landing, 0)], axis=-1)
    row_index = jnp.arange(ROWS)[None, None, :]
    starts = (jax.random.randint(key_images, (N_DP, N_FSDP, ROWS), 0, 12) == 0) & (row_index >= 3)
    image_ids = jnp.cumsum(starts.astype(jnp.int32), axis=-1)
    home_ids = jnp.where(row_index < kept[:, :, None], image_ids, -1)
    for route in range(4):
        begin_row = home_start[:, :, route:route + 1]
        inside = (row_index >= begin_row) & (row_index < begin_row + length[:, :, route:route + 1])
        home_ids = jnp.where(inside, ROWS + route, home_ids)
    return (kept.astype(jnp.int32), table.astype(jnp.int32), home_ids.astype(jnp.int32))


def draw_kept_rows(key, part):
    tables = pack_tables(key)
    return tables[0]


def draw_pack_list(key, part):
    tables = pack_tables(key)
    return tables[1]


def draw_home_segments(key, part):
    tables = pack_tables(key)
    return tables[2]


def small_code(sign_bits, power_index, mantissa):
    powers = jnp.array([0.125, 0.25, 0.5, 1.0, 2.0], jnp.float32)
    signs = 2.0 * sign_bits.astype(jnp.float32) - 1.0
    return signs * powers[power_index] * (1.0 + mantissa.astype(jnp.float32) / 8.0)


def draw_qkv_codes(key, part):
    key = jax.random.fold_in(key, 11)
    shape = (N_DP, N_FSDP, ROWS, 3, HW)
    key_sign, key_first, key_second, key_mant = jax.random.split(key, 4)
    sign_bits = jax.random.randint(key_sign, shape, 0, 2)
    mantissa = jax.random.randint(key_mant, shape, 0, 8)
    power_index = jax.random.randint(key_first, shape, 0, 3) + jax.random.randint(key_second, shape, 0, 3)
    codes = small_code(sign_bits, power_index, mantissa)
    return codes.astype(jnp.bfloat16)


def draw_block_scales(key, part):
    key = jax.random.fold_in(key, 12)
    shape = (N_DP, N_FSDP, ROWS, 3, NB)
    scales = jnp.exp(jax.random.uniform(key, shape, jnp.float32, jnp.log(0.25), jnp.log(2.0)))
    return scales.astype(jnp.bfloat16)


def levels(key, shape, pieces, low, largest):
    factor_of = 1.0
    for dim, parts in pieces:
        heights = jax.random.uniform(jax.random.fold_in(jax.random.fold_in(key, 6), dim), (parts,), jnp.float32, low / len(pieces), largest / len(pieces))
        factor_of = factor_of * jnp.repeat(jnp.exp(heights), shape[dim] // parts).reshape((-1,) + (1,) * (len(shape) - 1 - dim))
    return factor_of


def noise(key, extent, deviation, limit, cuts=(), kind=jnp.bfloat16):
    values = deviation * jax.random.normal(key, extent, jnp.float32)
    if cuts:
        values = values * levels(key, extent, cuts, -0.22, 0.18)
    return jnp.clip(values, -limit, limit).astype(kind)


def setup_inputs(seed: int = 0) -> dict:
    key_list = jax.random.split(jax.random.key(seed), 8)
    qkv_codes = draw_qkv_codes(jax.random.fold_in(key_list[7], 71), 0)
    block_scales = draw_block_scales(jax.random.fold_in(key_list[7], 71), 0)
    home_segments = draw_home_segments(jax.random.fold_in(key_list[7], 71), 0)
    kept_rows = draw_kept_rows(jax.random.fold_in(key_list[7], 71), 0)
    pack_list = draw_pack_list(jax.random.fold_in(key_list[7], 71), 0)
    w_out = noise(key_list[5], (HW, D), HW ** -0.5, 0.1875, ((0, 4),))
    cotangent = noise(key_list[6], (N_DP, N_FSDP, ROWS, D), 0.25, 4.0, ((0, 8), (1, 4)))
    return {"qkv_codes": qkv_codes, "block_scales": block_scales, "home_segments": home_segments, "kept_rows": kept_rows, "pack_list": pack_list, "w_out": w_out, "cotangent": cotangent}


offsets = (1, -1, 2, -2)

def dequantize(codes, scales):
    count = codes.shape[0]
    blocks = scales.shape[-1]
    scaled = codes.astype(jnp.float32).reshape(count, 3, blocks, -1) * scales.astype(jnp.float32)[..., None]
    return scaled.reshape(count, 3, -1).astype(jnp.bfloat16)

def local_layer(codes, scales, labels, w_full, grad_out):
    count = codes.shape[0]
    factor = 1.0 / math.sqrt(HD)
    values = dequantize(codes, scales)
    query = values[:, 0].reshape(count, HEADS, HD).astype(jnp.float32)
    keys = values[:, 1].reshape(count, HEADS, HD).astype(jnp.float32)
    value_rows = values[:, 2].reshape(count, HEADS, HD).astype(jnp.float32)
    scores = jnp.einsum('qhd,khd->hqk', query, keys) * factor
    same = labels[:, None] == labels[None, :]
    scores = jnp.where(same[None], scores, -jnp.inf)
    top = lax.optimization_barrier(jnp.max(scores, axis=-1, keepdims=True))
    weights = jnp.exp(scores - top)
    probs = weights / lax.optimization_barrier(jnp.sum(weights, axis=-1, keepdims=True))
    probs_b = probs.astype(jnp.bfloat16).astype(jnp.float32)
    context = jnp.einsum('hqk,khd->qhd', probs_b, value_rows).reshape(count, HW).astype(jnp.bfloat16)
    output = jnp.dot(context, w_full, preferred_element_type=jnp.float32).astype(jnp.bfloat16)
    grad_context = lax.dot_general(grad_out, w_full, (((1,), (1,)), ((), ())), preferred_element_type=jnp.float32)
    grad_context = grad_context.astype(jnp.bfloat16).reshape(count, HEADS, HD).astype(jnp.float32)
    grad_probs = jnp.einsum('qhd,khd->hqk', grad_context, value_rows)
    total = lax.optimization_barrier(jnp.sum(probs * grad_probs, axis=-1, keepdims=True))
    grad_scores = (probs * (grad_probs - total) * factor).astype(jnp.bfloat16).astype(jnp.float32)
    grad_query = jnp.einsum('hqk,khd->qhd', grad_scores, keys)
    grad_keys = jnp.einsum('hqk,qhd->khd', grad_scores, query)
    grad_values = jnp.einsum('hqk,qhd->khd', probs_b, grad_context)
    grads = jnp.stack([grad_query, grad_keys, grad_values], axis=1).reshape(count, 3, -1)
    blocks = scales.shape[-1]
    grads = (grads.reshape(count, 3, blocks, -1) * scales.astype(jnp.float32)[..., None]).reshape(count, 3, -1)
    term = lax.dot_general(context, grad_out, (((0,), (0,)), ((), ())), preferred_element_type=jnp.float32)
    return (output, grads.astype(jnp.bfloat16), term)

def pad_rows(array, fill):
    extra = jnp.full((array.shape[0], SLOT) + array.shape[2:], fill, array.dtype)
    return jnp.concatenate([array, extra], axis=1)

def corner(device, at_row, ndim):
    return (device.astype(jnp.int32), at_row.astype(jnp.int32)) + (jnp.int32(0),) * (ndim - 2)

def take_rows(buffer, device, at_row):
    return lax.dynamic_slice(buffer, corner(device, at_row, buffer.ndim), (1, SLOT) + buffer.shape[2:])

def place_rows(buffer, piece, device, at_row, length):
    old = take_rows(buffer, device, at_row)
    present = (jnp.arange(SLOT) < length).reshape((1, SLOT) + (1,) * (buffer.ndim - 2))
    return lax.dynamic_update_slice(buffer, jnp.where(present, piece, old), corner(device, at_row, buffer.ndim))

def balance_group(items):
    codes, scales, segments, kept, table = items
    inside = jnp.arange(ROWS)[None, :] < kept[:, None]
    start_codes = pad_rows(jnp.where(inside[:, :, None, None], codes, jnp.zeros_like(codes)), 0)
    start_scales = pad_rows(jnp.where(inside[:, :, None, None], scales, jnp.zeros_like(scales)), 0)
    start_labels = pad_rows(jnp.where(inside, segments, -1).astype(jnp.int32), -1)
    home_codes = pad_rows(codes, 0)
    home_scales = pad_rows(scales, 0)
    moved_by = jnp.array(offsets, jnp.int32)

    def step(index, state):
        bal_codes, bal_scales, labels = state
        index = index.astype(jnp.int32)
        source = index // 4
        route = index % 4
        entry = table[source, route]
        target = jnp.clip(source + moved_by[route], 0, N_DP - 1)
        bal_codes = place_rows(bal_codes, take_rows(home_codes, source, entry[0]), target, entry[2], entry[1])
        bal_scales = place_rows(bal_scales, take_rows(home_scales, source, entry[0]), target, entry[2], entry[1])
        marks = jnp.full((1, SLOT), 100000, jnp.int32) + route
        labels = place_rows(labels, marks, target, entry[2], entry[1])
        return (bal_codes, bal_scales, labels)
    bal_codes, bal_scales, labels = lax.fori_loop(0, N_DP * 4, step, (start_codes, start_scales, start_labels))
    return (bal_codes[:, :ROWS], bal_scales[:, :ROWS], labels[:, :ROWS])

def return_group(items):
    grads, kept, table = items
    inside = jnp.arange(ROWS)[None, :] < kept[:, None]
    home = pad_rows(jnp.where(inside[:, :, None, None], grads, jnp.zeros_like(grads)), 0)
    source_rows = pad_rows(grads, 0)
    moved_by = jnp.array(offsets, jnp.int32)

    def step(index, home):
        index = index.astype(jnp.int32)
        source = index // 4
        route = index % 4
        entry = table[source, route]
        target = jnp.clip(source + moved_by[route], 0, N_DP - 1)
        return place_rows(home, take_rows(source_rows, target, entry[2]), source, entry[0], entry[1])
    home = lax.fori_loop(0, N_DP * 4, step, home)
    return home[:, :ROWS]

def by_group(array):
    return jnp.swapaxes(array, 0, 1)

def reference(qkv_codes, block_scales, home_segments, kept_rows, pack_list, w_out, cotangent):
    bal_codes, bal_scales, labels = lax.map(balance_group, (by_group(qkv_codes), by_group(block_scales), by_group(home_segments), by_group(kept_rows), by_group(pack_list)))

    def per_device(total, item):
        codes, scales, marks, grad_out = item
        output, grads, term = local_layer(codes, scales, marks, w_out, grad_out)
        rounded = lax.optimization_barrier(term.astype(jnp.bfloat16))
        return (total + rounded.astype(jnp.float32), (output, grads))

    def per_data(item):
        total, (outputs, grads) = lax.scan(per_device, jnp.zeros((HW, D), jnp.float32), item)
        return (outputs, grads, total)
    outputs, grads, grad_w = lax.map(per_data, (by_group(bal_codes), by_group(bal_scales), by_group(labels), cotangent))
    home_grads = lax.map(return_group, (by_group(grads), by_group(kept_rows), by_group(pack_list)))
    return (outputs, by_group(home_grads), grad_w)
```

```python
import functools
import math

import jax
import jax.numpy as jnp
from jax import lax
from jax.experimental import pallas as pl
from jax.experimental.pallas import tpu as pltpu
from jax.sharding import PartitionSpec as P

HEADS = 8


offsets = (1, -1, 2, -2)


def shifted(block, axis, distance):
    devices = range(lax.axis_size(axis))
    route = [(i - distance, i) for i in devices if i - distance in devices]
    return lax.ppermute(block, axis, route)


def dequantize(codes, scales):
    count = codes.shape[0]
    blocks = scales.shape[-1]
    scaled = (
        codes.astype(jnp.float32).reshape(count, 3, blocks, -1)
        * scales.astype(jnp.float32)[..., None]
    )
    return scaled.reshape(count, 3, -1).astype(jnp.bfloat16)


def local_layer(codes, scales, labels, w_full, grad_out):
    count = codes.shape[0]
    width = w_full.shape[0]
    head_size = width // HEADS
    factor = 1.0 / math.sqrt(head_size)
    values = dequantize(codes, scales)
    query = values[:, 0].reshape(count, HEADS, head_size)
    keys = values[:, 1].reshape(count, HEADS, head_size)
    value_rows = values[:, 2].reshape(count, HEADS, head_size)
    scores = jnp.einsum("qhd,khd->hqk", query, keys, preferred_element_type=jnp.float32) * factor
    same = labels[:, None] == labels[None, :]
    scores = jnp.where(same[None], scores, -jnp.inf)
    top = jnp.max(scores, axis=-1, keepdims=True)
    weights = jnp.exp(scores - top)
    probs = weights / jnp.sum(weights, axis=-1, keepdims=True)
    probs_b = probs.astype(jnp.bfloat16)
    context = jnp.einsum("hqk,khd->qhd", probs_b, value_rows, preferred_element_type=jnp.float32)
    context = context.reshape(count, width).astype(jnp.bfloat16)
    output = jnp.dot(context, w_full, preferred_element_type=jnp.float32).astype(jnp.bfloat16)
    grad_context = lax.dot_general(
        grad_out, w_full, (((1,), (1,)), ((), ())), preferred_element_type=jnp.float32
    )
    grad_context = grad_context.astype(jnp.bfloat16).reshape(count, HEADS, head_size)
    grad_probs = jnp.einsum(
        "qhd,khd->hqk", grad_context, value_rows, preferred_element_type=jnp.float32
    )
    total = jnp.sum(probs * grad_probs, axis=-1, keepdims=True)
    grad_scores = (probs * (grad_probs - total) * factor).astype(jnp.bfloat16)
    grad_query = jnp.einsum("hqk,khd->qhd", grad_scores, keys, preferred_element_type=jnp.float32)
    grad_keys = jnp.einsum("hqk,qhd->khd", grad_scores, query, preferred_element_type=jnp.float32)
    grad_values = jnp.einsum(
        "hqk,qhd->khd", probs_b, grad_context, preferred_element_type=jnp.float32
    )
    grads = jnp.stack([grad_query, grad_keys, grad_values], axis=1).reshape(count, 3, -1)
    blocks = scales.shape[-1]
    grads = (grads.reshape(count, 3, blocks, -1) * scales.astype(jnp.float32)[..., None]).reshape(
        count, 3, -1
    )
    return (output, grads.astype(jnp.bfloat16), context)


def pad_rows(array, extra_rows, fill):
    extra = jnp.full((extra_rows,) + array.shape[1:], fill, array.dtype)
    return jnp.concatenate([array, extra], axis=0)


def cut_rows(buffer, at_row, length, slot):
    piece = lax.dynamic_slice_in_dim(buffer, at_row, slot, 0)
    present = (jnp.arange(slot) < length).reshape((slot,) + (1,) * (buffer.ndim - 1))
    return jnp.where(present, piece, jnp.zeros_like(piece))


def put_rows(buffer, piece, at_row, length):
    slot = piece.shape[0]
    old = lax.dynamic_slice_in_dim(buffer, at_row, slot, 0)
    present = (jnp.arange(slot) < length).reshape((slot,) + (1,) * (buffer.ndim - 1))
    return lax.dynamic_update_slice_in_dim(buffer, jnp.where(present, piece, old), at_row, 0)


def local(qkv_codes, block_scales, home_segments, kept_rows, pack_list, w_out, cotangent):
    position = lax.axis_index("dp")
    group_size = lax.axis_size("dp")
    codes = qkv_codes[0, 0]
    scales = block_scales[0, 0]
    segments = home_segments[0, 0]
    kept = kept_rows[0, 0]
    table = pack_list[:, 0]
    grad_out = cotangent[0, 0]
    row_count = codes.shape[0]
    slot = row_count // 8
    w_full = lax.all_gather(w_out, "fsdp", axis=0, tiled=True)
    inside = jnp.arange(row_count) < kept
    own_entries = lax.dynamic_index_in_dim(table, position, 0, keepdims=False)
    home_codes = pad_rows(codes, slot, 0)
    home_scales = pad_rows(scales, slot, 0)
    sent_codes = [
        cut_rows(home_codes, own_entries[route, 0], own_entries[route, 1], slot)
        for route in range(4)
    ]
    sent_scales = [
        cut_rows(home_scales, own_entries[route, 0], own_entries[route, 1], slot)
        for route in range(4)
    ]
    received = [
        shifted((sent_codes[route], sent_scales[route]), "dp", offsets[route]) for route in range(4)
    ]
    landing = []
    arrived = []
    for route in range(4):
        source = position - offsets[route]
        allowed = (source >= 0) & (source < group_size)
        entries = lax.dynamic_index_in_dim(
            table, jnp.clip(source, 0, group_size - 1), 0, keepdims=False
        )
        arrived.append(jnp.where(allowed, entries[route, 1], 0))
        landing.append(entries[route, 2])
    bal_codes = pad_rows(jnp.where(inside[:, None, None], codes, jnp.zeros_like(codes)), slot, 0)
    bal_scales = pad_rows(jnp.where(inside[:, None, None], scales, jnp.zeros_like(scales)), slot, 0)
    labels = pad_rows(jnp.where(inside, segments, -1), slot, -1)
    for route in range(4):
        bal_codes = put_rows(bal_codes, received[route][0], landing[route], arrived[route])
        bal_scales = put_rows(bal_scales, received[route][1], landing[route], arrived[route])
        marks = jnp.full((slot,), 100000 + route, jnp.int32)
        labels = put_rows(labels, marks, landing[route], arrived[route])
    output, grads, context = local_layer(
        bal_codes[:row_count], bal_scales[:row_count], labels[:row_count], w_full, grad_out
    )
    grads_padded = pad_rows(grads, slot, 0)
    going_back = [
        cut_rows(grads_padded, landing[route], arrived[route], slot) for route in range(4)
    ]
    returned = [shifted(going_back[route], "dp", -offsets[route]) for route in range(4)]
    home_grads = pad_rows(jnp.where(inside[:, None, None], grads, jnp.zeros_like(grads)), slot, 0)
    for route in range(4):
        home_grads = put_rows(
            home_grads, returned[route], own_entries[route, 0], own_entries[route, 1]
        )
    grad_codes = home_grads[:row_count]
    term = lax.dot_general(
        context, grad_out, (((0,), (0,)), ((), ())), preferred_element_type=jnp.float32
    )
    grad_w = lax.psum_scatter(
        term.astype(jnp.bfloat16), "fsdp", scatter_dimension=0, tiled=True
    ).astype(jnp.float32)
    return (output[None, None], grad_codes[None, None], grad_w[None])


BF = jnp.bfloat16
F32 = jnp.float32
PAIR = 256


def iota(shape, dim):
    return lax.broadcasted_iota(jnp.int32, shape, dim)


def hot(mask):
    return mask.astype(F32).astype(BF)


def mm(a, b, dims=((1,), (0,))):
    return lax.dot_general(a, b, (dims, ((), ())), preferred_element_type=F32)


def window(block, share):
    low = block * share // 128 * 128
    high = -(-(block + 1) * share // 128) * 128
    return low, high


def heads_kernel(
    groups, share, width,
    table, kept_ref, seg_ref, x_ref, w_ref, cot_ref,
    out_ref, grad_ref, gw_ref,
    img_send, img_recv, w_pad, cot_all, bal, qkv, scl, probs,
    ctx_send, ctx_all, gc_send, gc_in, part_send, part_in, x_send, x_in,
    packed, nat, back_send, back_recv,
    cot_s, cot_r, fwd_s, fwd_r, img_s, img_r, ctx_s, ctx_r, gc_s, gc_r,
    part_s, part_r, xs_s, xs_r, back_s, back_r,
):
    pos = lax.axis_index("dp")
    me = lax.axis_index("fsdp")
    sib = me + 1 - 2 * (me % 2)
    cross = (me + 2) % 4
    diag = (sib + 2) % 4
    peer = (me, sib, cross, diag)
    rows = cot_ref.shape[0]
    slot = img_send.shape[0] // 4
    feats = 3 * width
    model = cot_ref.shape[1]
    half = model // 2
    head = width // HEADS
    factor = 1.0 / math.sqrt(head)

    def remote(src, dst, s, r, where):
        return pltpu.make_async_remote_copy(
            src_ref=src, dst_ref=dst, send_sem=s, recv_sem=r,
            device_id=where, device_id_type=pl.DeviceIdType.MESH,
        )

    def at_dp(index):
        return (index, me)

    def at_fsdp(index):
        return (pos, index)

    img_recv[...] = jnp.zeros_like(img_recv)
    back_recv[...] = jnp.zeros_like(back_recv)

    barrier = pltpu.get_barrier_semaphore()
    for r in (1, 2, 3):
        pl.semaphore_signal(barrier, inc=1, device_id=at_fsdp(peer[r]),
                            device_id_type=pl.DeviceIdType.MESH)
    valid_to = [(pos + o >= 0) & (pos + o < groups) for o in offsets]
    valid_from = [(pos - o >= 0) & (pos - o < groups) for o in offsets]
    for d in range(4):
        @pl.when(valid_to[d])
        def _(d=d):
            pl.semaphore_signal(barrier, inc=1, device_id=at_dp(pos + offsets[d]),
                                device_id_type=pl.DeviceIdType.MESH)
    pl.semaphore_wait(barrier, 3 + jnp.minimum(pos, 2) + jnp.minimum(groups - 1 - pos, 2))

    hr = rows // 2
    cot_out = []
    for c in range(2):
        part = pl.ds(c * hr, hr)
        cot_out.append(remote(cot_ref.at[part], cot_all.at[1, part], cot_s.at[c], cot_r.at[c],
                              at_fsdp(cross)))
    cot_sib = remote(cot_ref, cot_all.at[0], cot_s.at[2], cot_r.at[2], at_fsdp(sib))
    cot_out[0].start()
    cot_out[1].start()
    cot_sib.start()
    forward = [
        remote(cot_all.at[1, pl.ds(c * hr, hr)], cot_all.at[2, pl.ds(c * hr, hr)],
               fwd_s.at[c], fwd_r.at[c], at_fsdp(sib))
        for c in range(2)
    ]

    kept = kept_ref[0, 0]
    r64 = iota((4 * slot, rows), 0)
    c64 = iota((4 * slot, rows), 1)

    def selection(starts, lengths):
        mask = jnp.zeros((4 * slot, rows), F32)
        for d in range(4):
            step = r64 - d * slot
            ok = (step >= 0) & (step < lengths[d]) & (step < slot) & (c64 == starts[d] + step)
            mask = mask + ok.astype(F32)
        return mask.astype(BF)

    own_start = [table[pos, 3 * d] for d in range(4)]
    own_len = [table[pos, 3 * d + 1] for d in range(4)]
    landing, arrived = [], []
    for d in range(4):
        src = jnp.clip(pos - offsets[d], 0, groups - 1)
        landing.append(table[src, 3 * d + 2])
        arrived.append(jnp.where(valid_from[d], table[src, 3 * d + 1], 0))
    img_send[...] = mm(selection(own_start, own_len), x_ref[...]).astype(BF)
    images = []
    for d in range(4):
        part = pl.ds(d * slot, slot)
        images.append(remote(img_send.at[part], img_recv.at[part], img_s.at[d], img_r.at[d],
                             at_dp(jnp.clip(pos + offsets[d], 0, groups - 1))))

        @pl.when(valid_to[d])
        def _(d=d):
            images[d].start()

    w_pad[0:share] = w_ref[...]
    w_pad[share:PAIR] = jnp.zeros((PAIR - share, model), BF)
    gc_in[0] = mm(cot_ref[...], w_pad[...], ((1,), (1,))).astype(BF)

    rr = iota((rows, rows), 0)
    cc = iota((rows, rows), 1)
    keep_hot = hot((rr == cc) & (rr < kept))

    def placing(starts, lengths):
        r_ = iota((rows, 4 * slot), 0)
        c_ = iota((rows, 4 * slot), 1)
        mask = jnp.zeros((rows, 4 * slot), F32)
        for d in range(4):
            step = c_ - d * slot
            ok = (step >= 0) & (step < lengths[d]) & (step < slot) & (r_ == starts[d] + step)
            mask = mask + ok.astype(F32)
        return mask.astype(BF)

    row_id = iota((1, rows), 1)
    marks = jnp.where(row_id < kept, seg_ref[...], -1)
    for d in range(4):
        here = (row_id >= landing[d]) & (row_id < landing[d] + arrived[d])
        marks = jnp.where(here, 100000 + d, marks)
    marks_row = jnp.broadcast_to(marks.astype(F32), (rows, rows))
    marks_col = jnp.sum(jnp.where(rr == cc, marks_row, 0.0), axis=1, keepdims=True)
    same = marks_col == marks_row
    bias = jnp.where(same, 0.0, -jnp.inf)
    bias2 = jnp.concatenate([bias, bias], axis=0)

    for d in range(4):
        @pl.when(valid_from[d])
        def _(d=d):
            images[d].wait_recv()
    place = placing(landing, arrived)
    bal[...] = (mm(keep_hot, x_ref[...]) + mm(place, img_recv[...])).astype(BF)

    lanes = iota((1, PAIR), 1)
    first = hot(lanes < head)
    second = hot(lanes >= head)
    for j in range(4):
        low, high = window(j, share)
        pick = hot((iota((high - low, PAIR), 0) + low == iota((high - low, PAIR), 1) + j * share)
                   & (iota((high - low, PAIR), 1) < share))
        block = (iota((128, PAIR), 1) + j * share) // 128
        for m in range(3):
            values = mm(bal[:, m * width + low:m * width + high], pick)
            spread = hot((iota((128, PAIR), 0) == block + m * (width // 128))
                         & (iota((128, PAIR), 1) < share))
            scale = mm(bal[:, feats:feats + 128], spread)
            scl[m * 4 + j] = scale.astype(BF)
            qkv[m * 4 + j] = (values * scale).astype(BF)

    def stack(x):
        return jnp.concatenate([x * first, x * second], axis=0)

    def wide(x):
        return jnp.concatenate([x[:rows], x[rows:]], axis=1)

    ctx_out = [None] * 4
    for r in (2, 3, 1, 0):
        j = peer[r]
        scores = mm(stack(qkv[j]), qkv[4 + j], ((1,), (1,))) * factor + bias2
        top = jnp.max(scores, axis=-1, keepdims=True)
        weights = jnp.exp(scores - top)
        p = weights / jnp.sum(weights, axis=-1, keepdims=True)
        probs[r] = p
        ctx = mm(wide(p.astype(BF)), stack(qkv[8 + j])).astype(BF)
        if r == 0:
            ctx_all[0] = ctx
        else:
            ctx_send[r] = ctx
            ctx_out[r] = remote(ctx_send.at[r], ctx_all.at[r], ctx_s.at[r], ctx_r.at[r],
                                at_fsdp(j))
            ctx_out[r].start()

    gc_out = [None] * 4

    def send_gc(r):
        gc_send[r] = mm(cot_all[r - 1], w_pad[...], ((1,), (1,))).astype(BF)
        gc_out[r] = remote(gc_send.at[r], gc_in.at[r], gc_s.at[r], gc_r.at[r], at_fsdp(peer[r]))
        gc_out[r].start()

    cot_sib.wait_recv()
    for c in range(2):
        cot_out[c].wait_recv()
        forward[c].start()
    send_gc(2)
    send_gc(1)
    for c in range(2):
        forward[c].wait_recv()
    send_gc(3)

    def product(r, c):
        return mm(ctx_all[r], w_pad[:, c * half:(c + 1) * half])

    sent = []
    crossing = []
    ctx_out[3].wait_recv()
    for c in range(2):
        part_send[c] = product(3, c).astype(BF)
        sent.append(remote(part_send.at[c], part_in.at[c], part_s.at[c], part_r.at[c],
                           at_fsdp(sib)))
        sent[c].start()
    ctx_out[2].wait_recv()
    for c in range(2):
        own = product(2, c)
        sent[c].wait_recv()
        x_send[c] = (own + part_in[c].astype(F32)).astype(BF)
        crossing.append(remote(x_send.at[c], x_in.at[c], xs_s.at[c], xs_r.at[c], at_fsdp(cross)))
        crossing[c].start()
    ctx_out[1].wait_recv()
    for c in range(2):
        part_send[2 + c] = product(1, c).astype(BF)
        sent.append(remote(part_send.at[2 + c], part_in.at[2 + c], part_s.at[2 + c],
                           part_r.at[2 + c], at_fsdp(sib)))
        sent[2 + c].start()

    for r in (0, 1, 2, 3):
        j = peer[r]
        if r:
            gc_out[r].wait_recv()
        p = probs[r]
        gstack = stack(gc_in[r])
        gp = mm(gstack, qkv[8 + j], ((1,), (1,)))
        total = jnp.sum(p * gp, axis=-1, keepdims=True)
        gs = (p * (gp - total) * factor).astype(BF)
        gq = mm(wide(gs), stack(qkv[4 + j]))
        gk = mm(gs, stack(qkv[j]), ((0,), (0,)))
        gv = mm(p.astype(BF), gstack, ((0,), (0,)))
        for m, g in enumerate((gq, gk, gv)):
            packed[m * 4 + j] = (g * scl[m * 4 + j].astype(F32)).astype(BF)
    for m in range(3):
        blocks = [None] * (width // 128)
        for j in range(4):
            low, high = window(j, share)
            spread = hot((iota((PAIR, high - low), 1) + low
                          == iota((PAIR, high - low), 0) + j * share)
                         & (iota((PAIR, high - low), 0) < share))
            piece = mm(packed[m * 4 + j], spread)
            for b in range((high - low) // 128):
                add = piece[:, b * 128:(b + 1) * 128]
                at = low // 128 + b
                blocks[at] = add if blocks[at] is None else blocks[at] + add
        for b in range(width // 128):
            nat[:, m * width + b * 128:m * width + (b + 1) * 128] = blocks[b].astype(BF)

    back_send[...] = mm(selection(landing, arrived), nat[...]).astype(BF)
    returns = []
    for d in range(4):
        part = pl.ds(d * slot, slot)
        returns.append(remote(back_send.at[part], back_recv.at[part], back_s.at[d], back_r.at[d],
                              at_dp(jnp.clip(pos - offsets[d], 0, groups - 1))))

        @pl.when(valid_from[d])
        def _(d=d):
            returns[d].start()

    acc = mm(ctx_all[0], cot_ref[...], ((0,), (0,)))
    for r in (1, 2, 3):
        acc = acc + mm(ctx_all[r], cot_all[r - 1], ((0,), (0,)))
    gw_ref[...] = acc[:share]

    for d in range(4):
        @pl.when(valid_to[d])
        def _(d=d):
            returns[d].wait_recv()
    grad_ref[...] = (mm(keep_hot, nat[...])
                     + mm(placing(own_start, own_len), back_recv[...])).astype(BF)

    for c in range(2):
        own = product(0, c)
        sent[2 + c].wait_recv()
        crossing[c].wait_recv()
        out_ref[:, c * half:(c + 1) * half] = (
            own + part_in[2 + c].astype(F32) + x_in[c].astype(F32)
        ).astype(BF)

    for copy in cot_out + [cot_sib] + forward + ctx_out[1:] + gc_out[1:] + sent + crossing:
        copy.wait_send()
    for d in range(4):
        @pl.when(valid_to[d])
        def _(d=d):
            images[d].wait_send()

        @pl.when(valid_from[d])
        def _(d=d):
            returns[d].wait_send()


def local_by_heads(qkv_codes, block_scales, home_segments, kept_rows, pack_list, w_out, cotangent):
    groups = lax.axis_size("dp")
    rows = qkv_codes.shape[2]
    width = qkv_codes.shape[4]
    model = w_out.shape[1]
    share = w_out.shape[0]
    slot = rows // 8
    feats = 3 * width
    scales = block_scales[0, 0].reshape(rows, -1)
    scales = jnp.pad(scales, ((0, 0), (0, 128 - scales.shape[1])))
    x = jnp.concatenate([qkv_codes[0, 0].reshape(rows, feats), scales], axis=1)
    vmem = pl.BlockSpec(memory_space=pltpu.VMEM)
    smem = pl.BlockSpec(memory_space=pltpu.SMEM)
    dma = pltpu.SemaphoreType.DMA
    half = model // 2
    out, grads, gw = pl.pallas_call(
        functools.partial(heads_kernel, groups, share, width),
        out_shape=(
            jax.ShapeDtypeStruct((rows, model), BF),
            jax.ShapeDtypeStruct((rows, feats), BF),
            jax.ShapeDtypeStruct((share, model), F32),
        ),
        in_specs=[smem, smem, vmem, vmem, vmem, vmem],
        out_specs=(vmem, vmem, vmem),
        scratch_shapes=[
            pltpu.VMEM((4 * slot, feats + 128), BF),
            pltpu.VMEM((4 * slot, feats + 128), BF),
            pltpu.VMEM((PAIR, model), BF),
            pltpu.VMEM((3, rows, model), BF),
            pltpu.VMEM((rows, feats + 128), BF),
            pltpu.VMEM((12, rows, PAIR), BF),
            pltpu.VMEM((12, rows, PAIR), BF),
            pltpu.VMEM((4, 2 * rows, rows), F32),
            pltpu.VMEM((4, rows, PAIR), BF),
            pltpu.VMEM((4, rows, PAIR), BF),
            pltpu.VMEM((4, rows, PAIR), BF),
            pltpu.VMEM((4, rows, PAIR), BF),
            pltpu.VMEM((4, rows, half), BF),
            pltpu.VMEM((4, rows, half), BF),
            pltpu.VMEM((2, rows, half), BF),
            pltpu.VMEM((2, rows, half), BF),
            pltpu.VMEM((12, rows, PAIR), BF),
            pltpu.VMEM((rows, feats), BF),
            pltpu.VMEM((4 * slot, feats), BF),
            pltpu.VMEM((4 * slot, feats), BF),
            dma((3,)), dma((3,)), dma((2,)), dma((2,)), dma((4,)), dma((4,)),
            dma((4,)), dma((4,)), dma((4,)), dma((4,)), dma((4,)), dma((4,)),
            dma((2,)), dma((2,)), dma((4,)), dma((4,)),
        ],
        compiler_params=pltpu.CompilerParams(
            collective_id=0, has_side_effects=True, vmem_limit_bytes=48 * 1024 * 1024
        ),
        cost_estimate=pl.CostEstimate(
            flops=8 * rows * width * model, bytes_accessed=8 * 1024 * 1024, transcendentals=0
        ),
        name="attention_by_heads",
    )(
        pack_list[:, 0].reshape(groups, 12),
        kept_rows,
        home_segments[0],
        x,
        w_out,
        cotangent[0, 0],
    )
    return (out[None, None], grads.reshape(1, 1, rows, 3, width), gw[None])


def solution(mesh):
    fast = mesh.shape["fsdp"] == 4
    return jax.shard_map(
        local_by_heads if fast else local,
        mesh=mesh,
        in_specs=(
            P("dp", "fsdp", None, None, None),
            P("dp", "fsdp", None, None, None),
            P("dp", "fsdp", None),
            P("dp", "fsdp"),
            P(None, "fsdp", None, None),
            P("fsdp", None),
            P("dp", "fsdp", None, None),
        ),
        out_specs=(
            P("dp", "fsdp", None, None),
            P("dp", "fsdp", None, None, None),
            P("dp", "fsdp", None),
        ),
        check_vma=False,
    )
```

```python
import functools
import math

import jax
import jax.numpy as jnp
from jax import lax
from jax.experimental import pallas as pl
from jax.experimental.pallas import tpu as pltpu
from jax.sharding import PartitionSpec as P

HEADS = 8


offsets = (1, -1, 2, -2)


def shifted(block, axis, distance):
    devices = range(lax.axis_size(axis))
    route = [(i - distance, i) for i in devices if i - distance in devices]
    return lax.ppermute(block, axis, route)


def dequantize(codes, scales):
    count = codes.shape[0]
    blocks = scales.shape[-1]
    scaled = (
        codes.astype(jnp.float32).reshape(count, 3, blocks, -1)
        * scales.astype(jnp.float32)[..., None]
    )
    return scaled.reshape(count, 3, -1).astype(jnp.bfloat16)


def local_layer(codes, scales, labels, w_full, grad_out):
    count = codes.shape[0]
    width = w_full.shape[0]
    head_size = width // HEADS
    factor = 1.0 / math.sqrt(head_size)
    values = dequantize(codes, scales)
    query = values[:, 0].reshape(count, HEADS, head_size)
    keys = values[:, 1].reshape(count, HEADS, head_size)
    value_rows = values[:, 2].reshape(count, HEADS, head_size)
    scores = jnp.einsum("qhd,khd->hqk", query, keys, preferred_element_type=jnp.float32) * factor
    same = labels[:, None] == labels[None, :]
    scores = jnp.where(same[None], scores, -jnp.inf)
    top = jnp.max(scores, axis=-1, keepdims=True)
    weights = jnp.exp(scores - top)
    probs = weights / jnp.sum(weights, axis=-1, keepdims=True)
    probs_b = probs.astype(jnp.bfloat16)
    context = jnp.einsum("hqk,khd->qhd", probs_b, value_rows, preferred_element_type=jnp.float32)
    context = context.reshape(count, width).astype(jnp.bfloat16)
    output = jnp.dot(context, w_full, preferred_element_type=jnp.float32).astype(jnp.bfloat16)
    grad_context = lax.dot_general(
        grad_out, w_full, (((1,), (1,)), ((), ())), preferred_element_type=jnp.float32
    )
    grad_context = grad_context.astype(jnp.bfloat16).reshape(count, HEADS, head_size)
    grad_probs = jnp.einsum(
        "qhd,khd->hqk", grad_context, value_rows, preferred_element_type=jnp.float32
    )
    total = jnp.sum(probs * grad_probs, axis=-1, keepdims=True)
    grad_scores = (probs * (grad_probs - total) * factor).astype(jnp.bfloat16)
    grad_query = jnp.einsum("hqk,khd->qhd", grad_scores, keys, preferred_element_type=jnp.float32)
    grad_keys = jnp.einsum("hqk,qhd->khd", grad_scores, query, preferred_element_type=jnp.float32)
    grad_values = jnp.einsum(
        "hqk,qhd->khd", probs_b, grad_context, preferred_element_type=jnp.float32
    )
    grads = jnp.stack([grad_query, grad_keys, grad_values], axis=1).reshape(count, 3, -1)
    blocks = scales.shape[-1]
    grads = (grads.reshape(count, 3, blocks, -1) * scales.astype(jnp.float32)[..., None]).reshape(
        count, 3, -1
    )
    return (output, grads.astype(jnp.bfloat16), context)


def pad_rows(array, extra_rows, fill):
    extra = jnp.full((extra_rows,) + array.shape[1:], fill, array.dtype)
    return jnp.concatenate([array, extra], axis=0)


def cut_rows(buffer, at_row, length, slot):
    piece = lax.dynamic_slice_in_dim(buffer, at_row, slot, 0)
    present = (jnp.arange(slot) < length).reshape((slot,) + (1,) * (buffer.ndim - 1))
    return jnp.where(present, piece, jnp.zeros_like(piece))


def put_rows(buffer, piece, at_row, length):
    slot = piece.shape[0]
    old = lax.dynamic_slice_in_dim(buffer, at_row, slot, 0)
    present = (jnp.arange(slot) < length).reshape((slot,) + (1,) * (buffer.ndim - 1))
    return lax.dynamic_update_slice_in_dim(buffer, jnp.where(present, piece, old), at_row, 0)


def local(qkv_codes, block_scales, home_segments, kept_rows, pack_list, w_out, cotangent):
    position = lax.axis_index("dp")
    group_size = lax.axis_size("dp")
    codes = qkv_codes[0, 0]
    scales = block_scales[0, 0]
    segments = home_segments[0, 0]
    kept = kept_rows[0, 0]
    table = pack_list[:, 0]
    grad_out = cotangent[0, 0]
    row_count = codes.shape[0]
    slot = row_count // 8
    w_full = lax.all_gather(w_out, "fsdp", axis=0, tiled=True)
    inside = jnp.arange(row_count) < kept
    own_entries = lax.dynamic_index_in_dim(table, position, 0, keepdims=False)
    home_codes = pad_rows(codes, slot, 0)
    home_scales = pad_rows(scales, slot, 0)
    sent_codes = [
        cut_rows(home_codes, own_entries[route, 0], own_entries[route, 1], slot)
        for route in range(4)
    ]
    sent_scales = [
        cut_rows(home_scales, own_entries[route, 0], own_entries[route, 1], slot)
        for route in range(4)
    ]
    received = [
        shifted((sent_codes[route], sent_scales[route]), "dp", offsets[route]) for route in range(4)
    ]
    landing = []
    arrived = []
    for route in range(4):
        source = position - offsets[route]
        allowed = (source >= 0) & (source < group_size)
        entries = lax.dynamic_index_in_dim(
            table, jnp.clip(source, 0, group_size - 1), 0, keepdims=False
        )
        arrived.append(jnp.where(allowed, entries[route, 1], 0))
        landing.append(entries[route, 2])
    bal_codes = pad_rows(jnp.where(inside[:, None, None], codes, jnp.zeros_like(codes)), slot, 0)
    bal_scales = pad_rows(jnp.where(inside[:, None, None], scales, jnp.zeros_like(scales)), slot, 0)
    labels = pad_rows(jnp.where(inside, segments, -1), slot, -1)
    for route in range(4):
        bal_codes = put_rows(bal_codes, received[route][0], landing[route], arrived[route])
        bal_scales = put_rows(bal_scales, received[route][1], landing[route], arrived[route])
        marks = jnp.full((slot,), 100000 + route, jnp.int32)
        labels = put_rows(labels, marks, landing[route], arrived[route])
    output, grads, context = local_layer(
        bal_codes[:row_count], bal_scales[:row_count], labels[:row_count], w_full, grad_out
    )
    grads_padded = pad_rows(grads, slot, 0)
    going_back = [
        cut_rows(grads_padded, landing[route], arrived[route], slot) for route in range(4)
    ]
    returned = [shifted(going_back[route], "dp", -offsets[route]) for route in range(4)]
    home_grads = pad_rows(jnp.where(inside[:, None, None], grads, jnp.zeros_like(grads)), slot, 0)
    for route in range(4):
        home_grads = put_rows(
            home_grads, returned[route], own_entries[route, 0], own_entries[route, 1]
        )
    grad_codes = home_grads[:row_count]
    term = lax.dot_general(
        context, grad_out, (((0,), (0,)), ((), ())), preferred_element_type=jnp.float32
    )
    grad_w = lax.psum_scatter(
        term.astype(jnp.bfloat16), "fsdp", scatter_dimension=0, tiled=True
    ).astype(jnp.float32)
    return (output[None, None], grad_codes[None, None], grad_w[None])


BF = jnp.bfloat16
F32 = jnp.float32
PAIR = 256


def iota(shape, dim):
    return lax.broadcasted_iota(jnp.int32, shape, dim)


def hot(mask):
    return mask.astype(F32).astype(BF)


def mm(a, b, dims=((1,), (0,))):
    return lax.dot_general(a, b, (dims, ((), ())), preferred_element_type=F32)


def window(block, share):
    low = block * share // 128 * 128
    high = -(-(block + 1) * share // 128) * 128
    return low, high


def heads_kernel(
    groups, share, width,
    table, kept_ref, seg_ref, scales_ref, codes_hbm, w_hbm, cot_hbm,
    out_ref, grad_ref, gw_ref,
    codes, cot_ref, tall, scal, load_s, img_send, img_recv, w_pad, cot_all, bal, qkv, scl, probs,
    ctx_send, ctx_all, gc_send, gc_in, part_send, part_in, x_send, x_in,
    packed, nat, back_send, back_recv,
    cot_s, cot_r, fwd_s, fwd_r, img_s, img_r, ctx_s, ctx_r, gc_s, gc_r,
    part_s, part_r, xs_s, xs_r, back_s, back_r,
):
    pos = lax.axis_index("dp")
    me = lax.axis_index("fsdp")
    sib = me + 1 - 2 * (me % 2)
    cross = (me + 2) % 4
    diag = (sib + 2) % 4
    peer = (me, sib, cross, diag)
    rows = cot_ref.shape[0]
    slot = img_send.shape[0] // 4
    feats = 3 * width
    model = cot_ref.shape[1]
    half = model // 2
    head = width // HEADS
    factor = 1.0 / math.sqrt(head)

    def remote(src, dst, s, r, where):
        return pltpu.make_async_remote_copy(
            src_ref=src, dst_ref=dst, send_sem=s, recv_sem=r,
            device_id=where, device_id_type=pl.DeviceIdType.MESH,
        )

    def at_dp(index):
        return (index, me)

    def at_fsdp(index):
        return (pos, index)

    loads = [
        pltpu.make_async_copy(codes_hbm, codes, load_s.at[0]),
        pltpu.make_async_copy(w_hbm, w_pad.at[pl.ds(0, share)], load_s.at[1]),
        pltpu.make_async_copy(cot_hbm, cot_ref, load_s.at[2]),
    ]
    for load in loads:
        load.start()
    img_recv[...] = jnp.zeros_like(img_recv)
    back_recv[...] = jnp.zeros_like(back_recv)

    barrier = pltpu.get_barrier_semaphore()
    for r in (1, 2, 3):
        pl.semaphore_signal(barrier, inc=1, device_id=at_fsdp(peer[r]),
                            device_id_type=pl.DeviceIdType.MESH)
    valid_to = [(pos + o >= 0) & (pos + o < groups) for o in offsets]
    valid_from = [(pos - o >= 0) & (pos - o < groups) for o in offsets]
    for d in range(4):
        @pl.when(valid_to[d])
        def _(d=d):
            pl.semaphore_signal(barrier, inc=1, device_id=at_dp(pos + offsets[d]),
                                device_id_type=pl.DeviceIdType.MESH)
    pl.semaphore_wait(barrier, 3 + jnp.minimum(pos, 2) + jnp.minimum(groups - 1 - pos, 2))

    hr = rows // 2
    cot_out = []
    for c in range(2):
        part = pl.ds(c * hr, hr)
        cot_out.append(remote(cot_hbm.at[part], cot_all.at[1, part], cot_s.at[c], cot_r.at[c],
                              at_fsdp(cross)))
    cot_sib = remote(cot_hbm, cot_all.at[0], cot_s.at[2], cot_r.at[2], at_fsdp(sib))
    cot_out[0].start()
    cot_out[1].start()
    cot_sib.start()
    forward = [
        remote(cot_all.at[1, pl.ds(c * hr, hr)], cot_all.at[2, pl.ds(c * hr, hr)],
               fwd_s.at[c], fwd_r.at[c], at_fsdp(sib))
        for c in range(2)
    ]

    kept = kept_ref[0, 0]
    r64 = iota((4 * slot, rows), 0)
    c64 = iota((4 * slot, rows), 1)

    def selection(starts, lengths):
        mask = jnp.zeros((4 * slot, rows), F32)
        for d in range(4):
            step = r64 - d * slot
            ok = (step >= 0) & (step < lengths[d]) & (step < slot) & (c64 == starts[d] + step)
            mask = mask + ok.astype(F32)
        return mask.astype(BF)

    own_start = [table[0, d, pos] for d in range(4)]
    own_len = [table[1, d, pos] for d in range(4)]
    landing, arrived = [], []
    for d in range(4):
        src = jnp.clip(pos - offsets[d], 0, groups - 1)
        landing.append(table[2, d, src])
        arrived.append(jnp.where(valid_from[d], table[1, d, src], 0))
    tall[...] = jnp.zeros_like(tall)
    for m in range(3):
        tall[m * 8:m * 8 + scales_ref.shape[1]] = scales_ref[m].astype(F32)
    rr = iota((rows, rows), 0)
    cc = iota((rows, rows), 1)
    scal[...] = mm(hot(rr == cc), tall[...].astype(BF), ((1,), (1,))).astype(BF)
    loads[0].wait()
    chosen = selection(own_start, own_len)
    for m in range(3):
        img_send[:, m * width:(m + 1) * width] = mm(chosen, codes[m]).astype(BF)
    img_send[:, feats:] = mm(chosen, scal[...]).astype(BF)
    images = []
    for d in range(4):
        part = pl.ds(d * slot, slot)
        images.append(remote(img_send.at[part], img_recv.at[part], img_s.at[d], img_r.at[d],
                             at_dp(jnp.clip(pos + offsets[d], 0, groups - 1))))

        @pl.when(valid_to[d])
        def _(d=d):
            images[d].start()

    loads[1].wait()
    loads[2].wait()
    w_pad[share:PAIR] = jnp.zeros((PAIR - share, model), BF)
    gc_in[0] = mm(cot_ref[...], w_pad[...], ((1,), (1,))).astype(BF)

    keep_hot = hot((rr == cc) & (rr < kept))

    def placing(starts, lengths):
        r_ = iota((rows, 4 * slot), 0)
        c_ = iota((rows, 4 * slot), 1)
        mask = jnp.zeros((rows, 4 * slot), F32)
        for d in range(4):
            step = c_ - d * slot
            ok = (step >= 0) & (step < lengths[d]) & (step < slot) & (r_ == starts[d] + step)
            mask = mask + ok.astype(F32)
        return mask.astype(BF)

    row_id = iota((1, rows), 1)
    marks = jnp.where(row_id < kept, seg_ref[...], -1)
    for d in range(4):
        here = (row_id >= landing[d]) & (row_id < landing[d] + arrived[d])
        marks = jnp.where(here, 100000 + d, marks)
    marks_row = jnp.broadcast_to(marks.astype(F32), (rows, rows))
    marks_col = jnp.sum(jnp.where(rr == cc, marks_row, 0.0), axis=1, keepdims=True)
    same = marks_col == marks_row
    bias = jnp.where(same, 0.0, -jnp.inf)
    bias2 = jnp.concatenate([bias, bias], axis=0)

    for d in range(4):
        @pl.when(valid_from[d])
        def _(d=d):
            images[d].wait_recv()
    place = placing(landing, arrived)
    for m in range(3):
        part = slice(m * width, (m + 1) * width)
        bal[:, part] = (mm(keep_hot, codes[m]) + mm(place, img_recv[:, part])).astype(BF)
    bal[:, feats:] = (mm(keep_hot, scal[...]) + mm(place, img_recv[:, feats:])).astype(BF)

    lanes = iota((1, PAIR), 1)
    first = hot(lanes < head)
    second = hot(lanes >= head)
    for j in range(4):
        low, high = window(j, share)
        pick = hot((iota((high - low, PAIR), 0) + low == iota((high - low, PAIR), 1) + j * share)
                   & (iota((high - low, PAIR), 1) < share))
        block = (iota((128, PAIR), 1) + j * share) // 128
        for m in range(3):
            values = mm(bal[:, m * width + low:m * width + high], pick)
            spread = hot((iota((128, PAIR), 0) == block + m * 8)
                         & (iota((128, PAIR), 1) < share))
            scale = mm(bal[:, feats:feats + 128], spread)
            scl[m * 4 + j] = scale.astype(BF)
            qkv[m * 4 + j] = (values * scale).astype(BF)

    def stack(x):
        return jnp.concatenate([x * first, x * second], axis=0)

    def wide(x):
        return jnp.concatenate([x[:rows], x[rows:]], axis=1)

    ctx_out = [None] * 4
    for r in (2, 3, 1, 0):
        j = peer[r]
        scores = mm(stack(qkv[j]), qkv[4 + j], ((1,), (1,))) * factor + bias2
        top = jnp.max(scores, axis=-1, keepdims=True)
        weights = jnp.exp(scores - top)
        p = weights / jnp.sum(weights, axis=-1, keepdims=True)
        probs[r] = p
        ctx = mm(wide(p.astype(BF)), stack(qkv[8 + j])).astype(BF)
        if r == 0:
            ctx_all[0] = ctx
        else:
            ctx_send[r] = ctx
            ctx_out[r] = remote(ctx_send.at[r], ctx_all.at[r], ctx_s.at[r], ctx_r.at[r],
                                at_fsdp(j))
            ctx_out[r].start()

    gc_out = [None] * 4

    def send_gc(r):
        gc_send[r] = mm(cot_all[r - 1], w_pad[...], ((1,), (1,))).astype(BF)
        gc_out[r] = remote(gc_send.at[r], gc_in.at[r], gc_s.at[r], gc_r.at[r], at_fsdp(peer[r]))
        gc_out[r].start()

    cot_sib.wait_recv()
    for c in range(2):
        cot_out[c].wait_recv()
        forward[c].start()
    send_gc(2)
    send_gc(1)
    for c in range(2):
        forward[c].wait_recv()
    send_gc(3)

    def product(r, c):
        return mm(ctx_all[r], w_pad[:, c * half:(c + 1) * half])

    sent = []
    crossing = []
    ctx_out[3].wait_recv()
    for c in range(2):
        part_send[c] = product(3, c).astype(BF)
        sent.append(remote(part_send.at[c], part_in.at[c], part_s.at[c], part_r.at[c],
                           at_fsdp(sib)))
        sent[c].start()
    ctx_out[2].wait_recv()
    for c in range(2):
        own = product(2, c)
        sent[c].wait_recv()
        x_send[c] = (own + part_in[c].astype(F32)).astype(BF)
        crossing.append(remote(x_send.at[c], x_in.at[c], xs_s.at[c], xs_r.at[c], at_fsdp(cross)))
        crossing[c].start()
    ctx_out[1].wait_recv()
    for c in range(2):
        part_send[2 + c] = product(1, c).astype(BF)
        sent.append(remote(part_send.at[2 + c], part_in.at[2 + c], part_s.at[2 + c],
                           part_r.at[2 + c], at_fsdp(sib)))
        sent[2 + c].start()

    for r in (0, 1, 2, 3):
        j = peer[r]
        if r:
            gc_out[r].wait_recv()
        p = probs[r]
        gstack = stack(gc_in[r])
        gp = mm(gstack, qkv[8 + j], ((1,), (1,)))
        total = jnp.sum(p * gp, axis=-1, keepdims=True)
        gs = (p * (gp - total) * factor).astype(BF)
        gq = mm(wide(gs), stack(qkv[4 + j]))
        gk = mm(gs, stack(qkv[j]), ((0,), (0,)))
        gv = mm(p.astype(BF), gstack, ((0,), (0,)))
        for m, g in enumerate((gq, gk, gv)):
            packed[m * 4 + j] = (g * scl[m * 4 + j].astype(F32)).astype(BF)
    for m in range(3):
        blocks = [None] * (width // 128)
        for j in range(4):
            low, high = window(j, share)
            spread = hot((iota((PAIR, high - low), 1) + low
                          == iota((PAIR, high - low), 0) + j * share)
                         & (iota((PAIR, high - low), 0) < share))
            piece = mm(packed[m * 4 + j], spread)
            for b in range((high - low) // 128):
                add = piece[:, b * 128:(b + 1) * 128]
                at = low // 128 + b
                blocks[at] = add if blocks[at] is None else blocks[at] + add
        for b in range(width // 128):
            nat[:, m * width + b * 128:m * width + (b + 1) * 128] = blocks[b].astype(BF)

    back_send[...] = mm(selection(landing, arrived), nat[...]).astype(BF)
    returns = []
    for d in range(4):
        part = pl.ds(d * slot, slot)
        returns.append(remote(back_send.at[part], back_recv.at[part], back_s.at[d], back_r.at[d],
                              at_dp(jnp.clip(pos - offsets[d], 0, groups - 1))))

        @pl.when(valid_from[d])
        def _(d=d):
            returns[d].start()

    acc = mm(ctx_all[0], cot_ref[...], ((0,), (0,)))
    for r in (1, 2, 3):
        acc = acc + mm(ctx_all[r], cot_all[r - 1], ((0,), (0,)))
    gw_ref[...] = acc[:share]

    for d in range(4):
        @pl.when(valid_to[d])
        def _(d=d):
            returns[d].wait_recv()
    place = placing(own_start, own_len)
    for m in range(3):
        part = slice(m * width, (m + 1) * width)
        grad_ref[m] = (mm(keep_hot, nat[:, part]) + mm(place, back_recv[:, part])).astype(BF)

    for c in range(2):
        own = product(0, c)
        sent[2 + c].wait_recv()
        crossing[c].wait_recv()
        out_ref[:, c * half:(c + 1) * half] = (
            own + part_in[2 + c].astype(F32) + x_in[c].astype(F32)
        ).astype(BF)

    for copy in cot_out + [cot_sib] + forward + ctx_out[1:] + gc_out[1:] + sent + crossing:
        copy.wait_send()
    for d in range(4):
        @pl.when(valid_to[d])
        def _(d=d):
            images[d].wait_send()

        @pl.when(valid_from[d])
        def _(d=d):
            returns[d].wait_send()


def write_out(a, b, c, a_out, b_out, c_out, sems):
    copies = [
        pltpu.make_async_copy(src, dst, sems.at[i])
        for i, (src, dst) in enumerate(((a, a_out), (b, b_out), (c, c_out)))
    ]
    for copy in copies:
        copy.start()
    for copy in copies:
        copy.wait()


def local_by_heads(qkv_codes, block_scales, home_segments, kept_rows, pack_list, w_out, cotangent):
    groups = lax.axis_size("dp")
    rows = qkv_codes.shape[2]
    width = qkv_codes.shape[4]
    model = w_out.shape[1]
    share = w_out.shape[0]
    slot = rows // 8
    feats = 3 * width
    vmem = pl.BlockSpec(memory_space=pltpu.VMEM)
    hbm = pl.BlockSpec(memory_space=pltpu.HBM)
    smem = pl.BlockSpec(memory_space=pltpu.SMEM)
    dma = pltpu.SemaphoreType.DMA
    half = model // 2
    out, grads, gw = pl.pallas_call(
        functools.partial(heads_kernel, groups, share, width),
        out_shape=(
            jax.ShapeDtypeStruct((rows, model), BF),
            jax.ShapeDtypeStruct((3, rows, width), BF),
            jax.ShapeDtypeStruct((share, model), F32),
        ),
        in_specs=[smem, smem, vmem, vmem, hbm, hbm, hbm],
        out_specs=(vmem, vmem, vmem),
        scratch_shapes=[
            pltpu.VMEM((3, rows, width), BF),
            pltpu.VMEM((rows, model), BF),
            pltpu.VMEM((128, rows), F32),
            pltpu.VMEM((rows, 128), BF),
            dma((3,)),
            pltpu.VMEM((4 * slot, feats + 128), BF),
            pltpu.VMEM((4 * slot, feats + 128), BF),
            pltpu.VMEM((PAIR, model), BF),
            pltpu.VMEM((3, rows, model), BF),
            pltpu.VMEM((rows, feats + 128), BF),
            pltpu.VMEM((12, rows, PAIR), BF),
            pltpu.VMEM((12, rows, PAIR), BF),
            pltpu.VMEM((4, 2 * rows, rows), F32),
            pltpu.VMEM((4, rows, PAIR), BF),
            pltpu.VMEM((4, rows, PAIR), BF),
            pltpu.VMEM((4, rows, PAIR), BF),
            pltpu.VMEM((4, rows, PAIR), BF),
            pltpu.VMEM((4, rows, half), BF),
            pltpu.VMEM((4, rows, half), BF),
            pltpu.VMEM((2, rows, half), BF),
            pltpu.VMEM((2, rows, half), BF),
            pltpu.VMEM((12, rows, PAIR), BF),
            pltpu.VMEM((rows, feats), BF),
            pltpu.VMEM((4 * slot, feats), BF),
            pltpu.VMEM((4 * slot, feats), BF),
            dma((3,)), dma((3,)), dma((2,)), dma((2,)), dma((4,)), dma((4,)),
            dma((4,)), dma((4,)), dma((4,)), dma((4,)), dma((4,)), dma((4,)),
            dma((2,)), dma((2,)), dma((4,)), dma((4,)),
        ],
        compiler_params=pltpu.CompilerParams(
            collective_id=0, has_side_effects=True, vmem_limit_bytes=48 * 1024 * 1024
        ),
        cost_estimate=pl.CostEstimate(
            flops=8 * rows * width * model, bytes_accessed=8 * 1024 * 1024, transcendentals=0
        ),
        name="attention_by_heads",
    )(
        jnp.transpose(pack_list[:, 0], (2, 1, 0)),
        kept_rows,
        home_segments[0],
        jnp.transpose(block_scales[0, 0], (1, 2, 0)),
        jnp.transpose(qkv_codes[0, 0], (1, 0, 2)),
        w_out,
        cotangent[0, 0],
    )
    results = (out, grads, gw)
    out, grads, gw = pl.pallas_call(
        write_out,
        out_shape=tuple(jax.ShapeDtypeStruct(a.shape, a.dtype) for a in results),
        in_specs=[vmem] * 3,
        out_specs=(hbm,) * 3,
        scratch_shapes=[dma((3,))],
        compiler_params=pltpu.CompilerParams(vmem_limit_bytes=4 * 1024 * 1024),
        name="write_out",
    )(*results)
    return (out[None, None], jnp.transpose(grads, (1, 0, 2))[None, None], gw[None])


def solution(mesh):
    fast = mesh.shape["fsdp"] == 4
    return jax.shard_map(
        local_by_heads if fast else local,
        mesh=mesh,
        in_specs=(
            P("dp", "fsdp", None, None, None),
            P("dp", "fsdp", None, None, None),
            P("dp", "fsdp", None),
            P("dp", "fsdp"),
            P(None, "fsdp", None, None),
            P("fsdp", None),
            P("dp", "fsdp", None, None),
        ),
        out_specs=(
            P("dp", "fsdp", None, None),
            P("dp", "fsdp", None, None, None),
            P("dp", "fsdp", None),
        ),
        check_vma=False,
    )
```

```python
import functools
import math

import jax
import jax.numpy as jnp
from jax import lax
from jax.experimental import pallas as pl
from jax.experimental.pallas import tpu as pltpu
from jax.sharding import PartitionSpec as P

HEADS = 8


offsets = (1, -1, 2, -2)


def shifted(block, axis, distance):
    devices = range(lax.axis_size(axis))
    route = [(i - distance, i) for i in devices if i - distance in devices]
    return lax.ppermute(block, axis, route)


def dequantize(codes, scales):
    count = codes.shape[0]
    blocks = scales.shape[-1]
    scaled = (
        codes.astype(jnp.float32).reshape(count, 3, blocks, -1)
        * scales.astype(jnp.float32)[..., None]
    )
    return scaled.reshape(count, 3, -1).astype(jnp.bfloat16)


def local_layer(codes, scales, labels, w_full, grad_out):
    count = codes.shape[0]
    width = w_full.shape[0]
    head_size = width // HEADS
    factor = 1.0 / math.sqrt(head_size)
    values = dequantize(codes, scales)
    query = values[:, 0].reshape(count, HEADS, head_size)
    keys = values[:, 1].reshape(count, HEADS, head_size)
    value_rows = values[:, 2].reshape(count, HEADS, head_size)
    scores = jnp.einsum("qhd,khd->hqk", query, keys, preferred_element_type=jnp.float32) * factor
    same = labels[:, None] == labels[None, :]
    scores = jnp.where(same[None], scores, -jnp.inf)
    top = jnp.max(scores, axis=-1, keepdims=True)
    weights = jnp.exp(scores - top)
    probs = weights / jnp.sum(weights, axis=-1, keepdims=True)
    probs_b = probs.astype(jnp.bfloat16)
    context = jnp.einsum("hqk,khd->qhd", probs_b, value_rows, preferred_element_type=jnp.float32)
    context = context.reshape(count, width).astype(jnp.bfloat16)
    output = jnp.dot(context, w_full, preferred_element_type=jnp.float32).astype(jnp.bfloat16)
    grad_context = lax.dot_general(
        grad_out, w_full, (((1,), (1,)), ((), ())), preferred_element_type=jnp.float32
    )
    grad_context = grad_context.astype(jnp.bfloat16).reshape(count, HEADS, head_size)
    grad_probs = jnp.einsum(
        "qhd,khd->hqk", grad_context, value_rows, preferred_element_type=jnp.float32
    )
    total = jnp.sum(probs * grad_probs, axis=-1, keepdims=True)
    grad_scores = (probs * (grad_probs - total) * factor).astype(jnp.bfloat16)
    grad_query = jnp.einsum("hqk,khd->qhd", grad_scores, keys, preferred_element_type=jnp.float32)
    grad_keys = jnp.einsum("hqk,qhd->khd", grad_scores, query, preferred_element_type=jnp.float32)
    grad_values = jnp.einsum(
        "hqk,qhd->khd", probs_b, grad_context, preferred_element_type=jnp.float32
    )
    grads = jnp.stack([grad_query, grad_keys, grad_values], axis=1).reshape(count, 3, -1)
    blocks = scales.shape[-1]
    grads = (grads.reshape(count, 3, blocks, -1) * scales.astype(jnp.float32)[..., None]).reshape(
        count, 3, -1
    )
    return (output, grads.astype(jnp.bfloat16), context)


def pad_rows(array, extra_rows, fill):
    extra = jnp.full((extra_rows,) + array.shape[1:], fill, array.dtype)
    return jnp.concatenate([array, extra], axis=0)


def cut_rows(buffer, at_row, length, slot):
    piece = lax.dynamic_slice_in_dim(buffer, at_row, slot, 0)
    present = (jnp.arange(slot) < length).reshape((slot,) + (1,) * (buffer.ndim - 1))
    return jnp.where(present, piece, jnp.zeros_like(piece))


def put_rows(buffer, piece, at_row, length):
    slot = piece.shape[0]
    old = lax.dynamic_slice_in_dim(buffer, at_row, slot, 0)
    present = (jnp.arange(slot) < length).reshape((slot,) + (1,) * (buffer.ndim - 1))
    return lax.dynamic_update_slice_in_dim(buffer, jnp.where(present, piece, old), at_row, 0)


def local(qkv_codes, block_scales, home_segments, kept_rows, pack_list, w_out, cotangent):
    position = lax.axis_index("dp")
    group_size = lax.axis_size("dp")
    codes = qkv_codes[0, 0]
    scales = block_scales[0, 0]
    segments = home_segments[0, 0]
    kept = kept_rows[0, 0]
    table = pack_list[:, 0]
    grad_out = cotangent[0, 0]
    row_count = codes.shape[0]
    slot = row_count // 8
    w_full = lax.all_gather(w_out, "fsdp", axis=0, tiled=True)
    inside = jnp.arange(row_count) < kept
    own_entries = lax.dynamic_index_in_dim(table, position, 0, keepdims=False)
    home_codes = pad_rows(codes, slot, 0)
    home_scales = pad_rows(scales, slot, 0)
    sent_codes = [
        cut_rows(home_codes, own_entries[route, 0], own_entries[route, 1], slot)
        for route in range(4)
    ]
    sent_scales = [
        cut_rows(home_scales, own_entries[route, 0], own_entries[route, 1], slot)
        for route in range(4)
    ]
    received = [
        shifted((sent_codes[route], sent_scales[route]), "dp", offsets[route]) for route in range(4)
    ]
    landing = []
    arrived = []
    for route in range(4):
        source = position - offsets[route]
        allowed = (source >= 0) & (source < group_size)
        entries = lax.dynamic_index_in_dim(
            table, jnp.clip(source, 0, group_size - 1), 0, keepdims=False
        )
        arrived.append(jnp.where(allowed, entries[route, 1], 0))
        landing.append(entries[route, 2])
    bal_codes = pad_rows(jnp.where(inside[:, None, None], codes, jnp.zeros_like(codes)), slot, 0)
    bal_scales = pad_rows(jnp.where(inside[:, None, None], scales, jnp.zeros_like(scales)), slot, 0)
    labels = pad_rows(jnp.where(inside, segments, -1), slot, -1)
    for route in range(4):
        bal_codes = put_rows(bal_codes, received[route][0], landing[route], arrived[route])
        bal_scales = put_rows(bal_scales, received[route][1], landing[route], arrived[route])
        marks = jnp.full((slot,), 100000 + route, jnp.int32)
        labels = put_rows(labels, marks, landing[route], arrived[route])
    output, grads, context = local_layer(
        bal_codes[:row_count], bal_scales[:row_count], labels[:row_count], w_full, grad_out
    )
    grads_padded = pad_rows(grads, slot, 0)
    going_back = [
        cut_rows(grads_padded, landing[route], arrived[route], slot) for route in range(4)
    ]
    returned = [shifted(going_back[route], "dp", -offsets[route]) for route in range(4)]
    home_grads = pad_rows(jnp.where(inside[:, None, None], grads, jnp.zeros_like(grads)), slot, 0)
    for route in range(4):
        home_grads = put_rows(
            home_grads, returned[route], own_entries[route, 0], own_entries[route, 1]
        )
    grad_codes = home_grads[:row_count]
    term = lax.dot_general(
        context, grad_out, (((0,), (0,)), ((), ())), preferred_element_type=jnp.float32
    )
    grad_w = lax.psum_scatter(
        term.astype(jnp.bfloat16), "fsdp", scatter_dimension=0, tiled=True
    ).astype(jnp.float32)
    return (output[None, None], grad_codes[None, None], grad_w[None])


BF = jnp.bfloat16
F32 = jnp.float32
PAIR = 256


def iota(shape, dim):
    return lax.broadcasted_iota(jnp.int32, shape, dim)


def hot(mask):
    return mask.astype(F32).astype(BF)


def mm(a, b, dims=((1,), (0,))):
    return lax.dot_general(a, b, (dims, ((), ())), preferred_element_type=F32)


def window(block, share):
    low = block * share // 128 * 128
    high = -(-(block + 1) * share // 128) * 128
    return low, high


def heads_kernel(
    groups, share, width,
    table, kept_ref, seg_ref, scales_ref, codes_hbm, w_hbm, cot_hbm,
    out_ref, grad_ref, gw_ref,
    codes, cot_ref, tall, scal, load_s, img_send, img_recv, w_pad, cot_all, bal, qkv, scl, probs,
    ctx_send, ctx_all, gc_send, gc_in, part_send, part_in, x_send, x_in,
    packed, nat, back_send, back_recv,
    cot_s, cot_r, fwd_s, fwd_r, img_s, img_r, ctx_s, ctx_r, gc_s, gc_r,
    part_s, part_r, xs_s, xs_r, back_s, back_r,
):
    pos = lax.axis_index("dp")
    me = lax.axis_index("fsdp")
    sib = me + 1 - 2 * (me % 2)
    cross = (me + 2) % 4
    diag = (sib + 2) % 4
    peer = (me, sib, cross, diag)
    rows = cot_ref.shape[0]
    slot = img_send.shape[0] // 4
    feats = 3 * width
    model = cot_ref.shape[1]
    half = model // 2
    head = width // HEADS
    factor = 1.0 / math.sqrt(head)

    def remote(src, dst, s, r, where):
        return pltpu.make_async_remote_copy(
            src_ref=src, dst_ref=dst, send_sem=s, recv_sem=r,
            device_id=where, device_id_type=pl.DeviceIdType.MESH,
        )

    def at_dp(index):
        return (index, me)

    def at_fsdp(index):
        return (pos, index)

    loads = [
        pltpu.make_async_copy(codes_hbm, codes, load_s.at[0]),
        pltpu.make_async_copy(w_hbm, w_pad.at[pl.ds(0, share)], load_s.at[1]),
        pltpu.make_async_copy(cot_hbm, cot_ref, load_s.at[2]),
    ]
    for load in loads:
        load.start()
    img_recv[...] = jnp.zeros_like(img_recv)
    back_recv[...] = jnp.zeros_like(back_recv)

    barrier = pltpu.get_barrier_semaphore()
    for r in (1, 2, 3):
        pl.semaphore_signal(barrier, inc=1, device_id=at_fsdp(peer[r]),
                            device_id_type=pl.DeviceIdType.MESH)
    valid_to = [(pos + o >= 0) & (pos + o < groups) for o in offsets]
    valid_from = [(pos - o >= 0) & (pos - o < groups) for o in offsets]
    for d in range(4):
        @pl.when(valid_to[d])
        def _(d=d):
            pl.semaphore_signal(barrier, inc=1, device_id=at_dp(pos + offsets[d]),
                                device_id_type=pl.DeviceIdType.MESH)
    pl.semaphore_wait(barrier, 3 + jnp.minimum(pos, 2) + jnp.minimum(groups - 1 - pos, 2))

    hr = rows // 2
    cot_out = []
    for c in range(2):
        part = pl.ds(c * hr, hr)
        cot_out.append(remote(cot_hbm.at[part], cot_all.at[1, part], cot_s.at[c], cot_r.at[c],
                              at_fsdp(cross)))
    cot_sib = remote(cot_hbm, cot_all.at[0], cot_s.at[2], cot_r.at[2], at_fsdp(sib))
    cot_out[0].start()
    cot_out[1].start()
    cot_sib.start()
    forward = [
        remote(cot_all.at[1, pl.ds(c * hr, hr)], cot_all.at[2, pl.ds(c * hr, hr)],
               fwd_s.at[c], fwd_r.at[c], at_fsdp(sib))
        for c in range(2)
    ]

    kept = kept_ref[0, 0]
    r64 = iota((4 * slot, rows), 0)
    c64 = iota((4 * slot, rows), 1)

    def selection(starts, lengths):
        mask = jnp.zeros((4 * slot, rows), F32)
        for d in range(4):
            step = r64 - d * slot
            ok = (step >= 0) & (step < lengths[d]) & (step < slot) & (c64 == starts[d] + step)
            mask = mask + ok.astype(F32)
        return mask.astype(BF)

    own_start = [table[0, d, pos] for d in range(4)]
    own_len = [table[1, d, pos] for d in range(4)]
    landing, arrived = [], []
    for d in range(4):
        src = jnp.clip(pos - offsets[d], 0, groups - 1)
        landing.append(table[2, d, src])
        arrived.append(jnp.where(valid_from[d], table[1, d, src], 0))
    tall[...] = jnp.zeros_like(tall)
    for m in range(3):
        tall[m * 8:m * 8 + scales_ref.shape[1]] = scales_ref[m].astype(F32)
    rr = iota((rows, rows), 0)
    cc = iota((rows, rows), 1)
    scal[...] = mm(hot(rr == cc), tall[...].astype(BF), ((1,), (1,))).astype(BF)
    loads[0].wait()
    chosen = selection(own_start, own_len)
    for m in range(3):
        img_send[:, m * width:(m + 1) * width] = mm(chosen, codes[m]).astype(BF)
    img_send[:, feats:] = mm(chosen, scal[...]).astype(BF)
    images = []
    for d in range(4):
        part = pl.ds(d * slot, slot)
        images.append(remote(img_send.at[part], img_recv.at[part], img_s.at[d], img_r.at[d],
                             at_dp(jnp.clip(pos + offsets[d], 0, groups - 1))))

        @pl.when(valid_to[d])
        def _(d=d):
            images[d].start()

    loads[1].wait()
    loads[2].wait()
    w_pad[share:PAIR] = jnp.zeros((PAIR - share, model), BF)
    gc_in[0] = mm(cot_ref[...], w_pad[...], ((1,), (1,))).astype(BF)

    keep_hot = hot((rr == cc) & (rr < kept))

    def placing(starts, lengths):
        r_ = iota((rows, 4 * slot), 0)
        c_ = iota((rows, 4 * slot), 1)
        mask = jnp.zeros((rows, 4 * slot), F32)
        for d in range(4):
            step = c_ - d * slot
            ok = (step >= 0) & (step < lengths[d]) & (step < slot) & (r_ == starts[d] + step)
            mask = mask + ok.astype(F32)
        return mask.astype(BF)

    row_id = iota((1, rows), 1)
    marks = jnp.where(row_id < kept, seg_ref[...], -1)
    for d in range(4):
        here = (row_id >= landing[d]) & (row_id < landing[d] + arrived[d])
        marks = jnp.where(here, 100000 + d, marks)
    marks_row = jnp.broadcast_to(marks.astype(F32), (rows, rows))
    marks_col = jnp.sum(jnp.where(rr == cc, marks_row, 0.0), axis=1, keepdims=True)
    same = marks_col == marks_row
    bias = jnp.where(same, 0.0, -jnp.inf)
    bias2 = jnp.concatenate([bias, bias], axis=0)

    for d in range(4):
        @pl.when(valid_from[d])
        def _(d=d):
            images[d].wait_recv()
    place = placing(landing, arrived)
    for m in range(3):
        part = slice(m * width, (m + 1) * width)
        bal[:, part] = (mm(keep_hot, codes[m]) + mm(place, img_recv[:, part])).astype(BF)
    bal[:, feats:] = (mm(keep_hot, scal[...]) + mm(place, img_recv[:, feats:])).astype(BF)

    lanes = iota((1, PAIR), 1)
    first = hot(lanes < head)
    second = hot(lanes >= head)
    for j in range(4):
        low, high = window(j, share)
        pick = hot((iota((high - low, PAIR), 0) + low == iota((high - low, PAIR), 1) + j * share)
                   & (iota((high - low, PAIR), 1) < share))
        block = (iota((128, PAIR), 1) + j * share) // 128
        for m in range(3):
            values = mm(bal[:, m * width + low:m * width + high], pick)
            spread = hot((iota((128, PAIR), 0) == block + m * 8)
                         & (iota((128, PAIR), 1) < share))
            scale = mm(bal[:, feats:feats + 128], spread)
            scl[m * 4 + j] = scale.astype(BF)
            qkv[m * 4 + j] = (values * scale).astype(BF)

    def stack(x):
        return jnp.concatenate([x * first, x * second], axis=0)

    def wide(x):
        return jnp.concatenate([x[:rows], x[rows:]], axis=1)

    ctx_out = [None] * 4
    for r in (2, 3, 1, 0):
        j = peer[r]
        scores = mm(stack(qkv[j]), qkv[4 + j], ((1,), (1,))) * factor + bias2
        top = jnp.max(scores, axis=-1, keepdims=True)
        weights = jnp.exp(scores - top)
        p = weights / jnp.sum(weights, axis=-1, keepdims=True)
        probs[r] = p
        ctx = mm(wide(p.astype(BF)), stack(qkv[8 + j])).astype(BF)
        if r == 0:
            ctx_all[0] = ctx
        else:
            ctx_send[r] = ctx
            ctx_out[r] = remote(ctx_send.at[r], ctx_all.at[r], ctx_s.at[r], ctx_r.at[r],
                                at_fsdp(j))
            ctx_out[r].start()

    gc_out = [None] * 4

    def send_gc(r):
        gc_send[r] = mm(cot_all[r - 1], w_pad[...], ((1,), (1,))).astype(BF)
        gc_out[r] = remote(gc_send.at[r], gc_in.at[r], gc_s.at[r], gc_r.at[r], at_fsdp(peer[r]))
        gc_out[r].start()

    cot_sib.wait_recv()
    for c in range(2):
        cot_out[c].wait_recv()
        forward[c].start()
    send_gc(2)
    send_gc(1)
    for c in range(2):
        forward[c].wait_recv()
    send_gc(3)

    def product(r, c):
        return mm(ctx_all[r], w_pad[:, c * half:(c + 1) * half])

    sent = []
    crossing = []
    ctx_out[3].wait_recv()
    for c in range(2):
        part_send[c] = product(3, c).astype(BF)
        sent.append(remote(part_send.at[c], part_in.at[c], part_s.at[c], part_r.at[c],
                           at_fsdp(sib)))
        sent[c].start()
    ctx_out[2].wait_recv()
    for c in range(2):
        own = product(2, c)
        sent[c].wait_recv()
        x_send[c] = (own + part_in[c].astype(F32)).astype(BF)
        crossing.append(remote(x_send.at[c], x_in.at[c], xs_s.at[c], xs_r.at[c], at_fsdp(cross)))
        crossing[c].start()
    ctx_out[1].wait_recv()
    for c in range(2):
        part_send[2 + c] = product(1, c).astype(BF)
        sent.append(remote(part_send.at[2 + c], part_in.at[2 + c], part_s.at[2 + c],
                           part_r.at[2 + c], at_fsdp(sib)))
        sent[2 + c].start()

    for r in (0, 1, 2, 3):
        j = peer[r]
        if r:
            gc_out[r].wait_recv()
        p = probs[r]
        gstack = stack(gc_in[r])
        gp = mm(gstack, qkv[8 + j], ((1,), (1,)))
        total = jnp.sum(p * gp, axis=-1, keepdims=True)
        gs = (p * (gp - total) * factor).astype(BF)
        gq = mm(wide(gs), stack(qkv[4 + j]))
        gk = mm(gs, stack(qkv[j]), ((0,), (0,)))
        gv = mm(p.astype(BF), gstack, ((0,), (0,)))
        for m, g in enumerate((gq, gk, gv)):
            packed[m * 4 + j] = (g * scl[m * 4 + j].astype(F32)).astype(BF)
    for m in range(3):
        blocks = [None] * (width // 128)
        for j in range(4):
            low, high = window(j, share)
            spread = hot((iota((PAIR, high - low), 1) + low
                          == iota((PAIR, high - low), 0) + j * share)
                         & (iota((PAIR, high - low), 0) < share))
            piece = mm(packed[m * 4 + j], spread)
            for b in range((high - low) // 128):
                add = piece[:, b * 128:(b + 1) * 128]
                at = low // 128 + b
                blocks[at] = add if blocks[at] is None else blocks[at] + add
        for b in range(width // 128):
            nat[:, m * width + b * 128:m * width + (b + 1) * 128] = blocks[b].astype(BF)

    back_send[...] = mm(selection(landing, arrived), nat[...]).astype(BF)
    returns = []
    for d in range(4):
        part = pl.ds(d * slot, slot)
        returns.append(remote(back_send.at[part], back_recv.at[part], back_s.at[d], back_r.at[d],
                              at_dp(jnp.clip(pos - offsets[d], 0, groups - 1))))

        @pl.when(valid_from[d])
        def _(d=d):
            returns[d].start()

    acc = mm(ctx_all[0], cot_ref[...], ((0,), (0,)))
    for r in (1, 2, 3):
        acc = acc + mm(ctx_all[r], cot_all[r - 1], ((0,), (0,)))
    gw_ref[...] = acc[:share]

    for d in range(4):
        @pl.when(valid_to[d])
        def _(d=d):
            returns[d].wait_recv()
    place = placing(own_start, own_len)
    for m in range(3):
        part = slice(m * width, (m + 1) * width)
        grad_ref[m] = (mm(keep_hot, nat[:, part]) + mm(place, back_recv[:, part])).astype(BF)

    for c in range(2):
        own = product(0, c)
        sent[2 + c].wait_recv()
        crossing[c].wait_recv()
        out_ref[:, c * half:(c + 1) * half] = (
            own + part_in[2 + c].astype(F32) + x_in[c].astype(F32)
        ).astype(BF)

    for copy in cot_out + [cot_sib] + forward + ctx_out[1:] + gc_out[1:] + sent + crossing:
        copy.wait_send()
    for d in range(4):
        @pl.when(valid_to[d])
        def _(d=d):
            images[d].wait_send()

        @pl.when(valid_from[d])
        def _(d=d):
            returns[d].wait_send()


def write_out(a, b, c, a_out, b_out, c_out, sems):
    copies = [
        pltpu.make_async_copy(src, dst, sems.at[i])
        for i, (src, dst) in enumerate(((a, a_out), (b, b_out), (c, c_out)))
    ]
    for copy in copies:
        copy.start()
    for copy in copies:
        copy.wait()


def local_by_heads(qkv_codes, block_scales, home_segments, kept_rows, pack_list, w_out, cotangent):
    groups = lax.axis_size("dp")
    rows = qkv_codes.shape[2]
    width = qkv_codes.shape[4]
    model = w_out.shape[1]
    share = w_out.shape[0]
    slot = rows // 8
    feats = 3 * width
    vmem = pl.BlockSpec(memory_space=pltpu.VMEM)
    hbm = pl.BlockSpec(memory_space=pltpu.HBM)
    smem = pl.BlockSpec(memory_space=pltpu.SMEM)
    dma = pltpu.SemaphoreType.DMA
    half = model // 2
    out, grads, gw = pl.pallas_call(
        functools.partial(heads_kernel, groups, share, width),
        out_shape=(
            pltpu.VMEM((rows, model), BF),
            pltpu.VMEM((3, rows, width), BF),
            pltpu.VMEM((share, model), F32),
        ),
        in_specs=[smem, smem, vmem, vmem, hbm, hbm, hbm],
        out_specs=(vmem, vmem, vmem),
        scratch_shapes=[
            pltpu.VMEM((3, rows, width), BF),
            pltpu.VMEM((rows, model), BF),
            pltpu.VMEM((128, rows), F32),
            pltpu.VMEM((rows, 128), BF),
            dma((3,)),
            pltpu.VMEM((4 * slot, feats + 128), BF),
            pltpu.VMEM((4 * slot, feats + 128), BF),
            pltpu.VMEM((PAIR, model), BF),
            pltpu.VMEM((3, rows, model), BF),
            pltpu.VMEM((rows, feats + 128), BF),
            pltpu.VMEM((12, rows, PAIR), BF),
            pltpu.VMEM((12, rows, PAIR), BF),
            pltpu.VMEM((4, 2 * rows, rows), F32),
            pltpu.VMEM((4, rows, PAIR), BF),
            pltpu.VMEM((4, rows, PAIR), BF),
            pltpu.VMEM((4, rows, PAIR), BF),
            pltpu.VMEM((4, rows, PAIR), BF),
            pltpu.VMEM((4, rows, half), BF),
            pltpu.VMEM((4, rows, half), BF),
            pltpu.VMEM((2, rows, half), BF),
            pltpu.VMEM((2, rows, half), BF),
            pltpu.VMEM((12, rows, PAIR), BF),
            pltpu.VMEM((rows, feats), BF),
            pltpu.VMEM((4 * slot, feats), BF),
            pltpu.VMEM((4 * slot, feats), BF),
            dma((3,)), dma((3,)), dma((2,)), dma((2,)), dma((4,)), dma((4,)),
            dma((4,)), dma((4,)), dma((4,)), dma((4,)), dma((4,)), dma((4,)),
            dma((2,)), dma((2,)), dma((4,)), dma((4,)),
        ],
        compiler_params=pltpu.CompilerParams(
            collective_id=0, has_side_effects=True, vmem_limit_bytes=58 * 1024 * 1024
        ),
        cost_estimate=pl.CostEstimate(
            flops=8 * rows * width * model, bytes_accessed=8 * 1024 * 1024, transcendentals=0
        ),
        name="attention_by_heads",
    )(
        jnp.transpose(pack_list[:, 0], (2, 1, 0)),
        kept_rows,
        home_segments[0],
        jnp.transpose(block_scales[0, 0], (1, 2, 0)),
        jnp.transpose(qkv_codes[0, 0], (1, 0, 2)),
        w_out,
        cotangent[0, 0],
    )
    results = (out, grads, gw)
    out, grads, gw = pl.pallas_call(
        write_out,
        out_shape=tuple(jax.ShapeDtypeStruct(a.shape, a.dtype) for a in results),
        in_specs=[vmem] * 3,
        out_specs=(hbm,) * 3,
        scratch_shapes=[dma((3,))],
        compiler_params=pltpu.CompilerParams(vmem_limit_bytes=4 * 1024 * 1024),
        name="write_out",
    )(*results)
    return (out[None, None], jnp.transpose(grads, (1, 0, 2))[None, None], gw[None])


def solution(mesh):
    fast = mesh.shape["fsdp"] == 4
    return jax.shard_map(
        local_by_heads if fast else local,
        mesh=mesh,
        in_specs=(
            P("dp", "fsdp", None, None, None),
            P("dp", "fsdp", None, None, None),
            P("dp", "fsdp", None),
            P("dp", "fsdp"),
            P(None, "fsdp", None, None),
            P("fsdp", None),
            P("dp", "fsdp", None, None),
        ),
        out_specs=(
            P("dp", "fsdp", None, None),
            P("dp", "fsdp", None, None, None),
            P("dp", "fsdp", None),
        ),
        check_vma=False,
    )
```

```python
import functools
import math

import jax
import jax.numpy as jnp
from jax import lax
from jax.experimental import pallas as pl
from jax.experimental.pallas import tpu as pltpu
from jax.sharding import PartitionSpec as P

HEADS = 8


offsets = (1, -1, 2, -2)


def shifted(block, axis, distance):
    devices = range(lax.axis_size(axis))
    route = [(i - distance, i) for i in devices if i - distance in devices]
    return lax.ppermute(block, axis, route)


def dequantize(codes, scales):
    count = codes.shape[0]
    blocks = scales.shape[-1]
    scaled = (
        codes.astype(jnp.float32).reshape(count, 3, blocks, -1)
        * scales.astype(jnp.float32)[..., None]
    )
    return scaled.reshape(count, 3, -1).astype(jnp.bfloat16)


def local_layer(codes, scales, labels, w_full, grad_out):
    count = codes.shape[0]
    width = w_full.shape[0]
    head_size = width // HEADS
    factor = 1.0 / math.sqrt(head_size)
    values = dequantize(codes, scales)
    query = values[:, 0].reshape(count, HEADS, head_size)
    keys = values[:, 1].reshape(count, HEADS, head_size)
    value_rows = values[:, 2].reshape(count, HEADS, head_size)
    scores = jnp.einsum("qhd,khd->hqk", query, keys, preferred_element_type=jnp.float32) * factor
    same = labels[:, None] == labels[None, :]
    scores = jnp.where(same[None], scores, -jnp.inf)
    top = jnp.max(scores, axis=-1, keepdims=True)
    weights = jnp.exp(scores - top)
    probs = weights / jnp.sum(weights, axis=-1, keepdims=True)
    probs_b = probs.astype(jnp.bfloat16)
    context = jnp.einsum("hqk,khd->qhd", probs_b, value_rows, preferred_element_type=jnp.float32)
    context = context.reshape(count, width).astype(jnp.bfloat16)
    output = jnp.dot(context, w_full, preferred_element_type=jnp.float32).astype(jnp.bfloat16)
    grad_context = lax.dot_general(
        grad_out, w_full, (((1,), (1,)), ((), ())), preferred_element_type=jnp.float32
    )
    grad_context = grad_context.astype(jnp.bfloat16).reshape(count, HEADS, head_size)
    grad_probs = jnp.einsum(
        "qhd,khd->hqk", grad_context, value_rows, preferred_element_type=jnp.float32
    )
    total = jnp.sum(probs * grad_probs, axis=-1, keepdims=True)
    grad_scores = (probs * (grad_probs - total) * factor).astype(jnp.bfloat16)
    grad_query = jnp.einsum("hqk,khd->qhd", grad_scores, keys, preferred_element_type=jnp.float32)
    grad_keys = jnp.einsum("hqk,qhd->khd", grad_scores, query, preferred_element_type=jnp.float32)
    grad_values = jnp.einsum(
        "hqk,qhd->khd", probs_b, grad_context, preferred_element_type=jnp.float32
    )
    grads = jnp.stack([grad_query, grad_keys, grad_values], axis=1).reshape(count, 3, -1)
    blocks = scales.shape[-1]
    grads = (grads.reshape(count, 3, blocks, -1) * scales.astype(jnp.float32)[..., None]).reshape(
        count, 3, -1
    )
    return (output, grads.astype(jnp.bfloat16), context)


def pad_rows(array, extra_rows, fill):
    extra = jnp.full((extra_rows,) + array.shape[1:], fill, array.dtype)
    return jnp.concatenate([array, extra], axis=0)


def cut_rows(buffer, at_row, length, slot):
    piece = lax.dynamic_slice_in_dim(buffer, at_row, slot, 0)
    present = (jnp.arange(slot) < length).reshape((slot,) + (1,) * (buffer.ndim - 1))
    return jnp.where(present, piece, jnp.zeros_like(piece))


def put_rows(buffer, piece, at_row, length):
    slot = piece.shape[0]
    old = lax.dynamic_slice_in_dim(buffer, at_row, slot, 0)
    present = (jnp.arange(slot) < length).reshape((slot,) + (1,) * (buffer.ndim - 1))
    return lax.dynamic_update_slice_in_dim(buffer, jnp.where(present, piece, old), at_row, 0)


def local(qkv_codes, block_scales, home_segments, kept_rows, pack_list, w_out, cotangent):
    position = lax.axis_index("dp")
    group_size = lax.axis_size("dp")
    codes = qkv_codes[0, 0]
    scales = block_scales[0, 0]
    segments = home_segments[0, 0]
    kept = kept_rows[0, 0]
    table = pack_list[:, 0]
    grad_out = cotangent[0, 0]
    row_count = codes.shape[0]
    slot = row_count // 8
    w_full = lax.all_gather(w_out, "fsdp", axis=0, tiled=True)
    inside = jnp.arange(row_count) < kept
    own_entries = lax.dynamic_index_in_dim(table, position, 0, keepdims=False)
    home_codes = pad_rows(codes, slot, 0)
    home_scales = pad_rows(scales, slot, 0)
    sent_codes = [
        cut_rows(home_codes, own_entries[route, 0], own_entries[route, 1], slot)
        for route in range(4)
    ]
    sent_scales = [
        cut_rows(home_scales, own_entries[route, 0], own_entries[route, 1], slot)
        for route in range(4)
    ]
    received = [
        shifted((sent_codes[route], sent_scales[route]), "dp", offsets[route]) for route in range(4)
    ]
    landing = []
    arrived = []
    for route in range(4):
        source = position - offsets[route]
        allowed = (source >= 0) & (source < group_size)
        entries = lax.dynamic_index_in_dim(
            table, jnp.clip(source, 0, group_size - 1), 0, keepdims=False
        )
        arrived.append(jnp.where(allowed, entries[route, 1], 0))
        landing.append(entries[route, 2])
    bal_codes = pad_rows(jnp.where(inside[:, None, None], codes, jnp.zeros_like(codes)), slot, 0)
    bal_scales = pad_rows(jnp.where(inside[:, None, None], scales, jnp.zeros_like(scales)), slot, 0)
    labels = pad_rows(jnp.where(inside, segments, -1), slot, -1)
    for route in range(4):
        bal_codes = put_rows(bal_codes, received[route][0], landing[route], arrived[route])
        bal_scales = put_rows(bal_scales, received[route][1], landing[route], arrived[route])
        marks = jnp.full((slot,), 100000 + route, jnp.int32)
        labels = put_rows(labels, marks, landing[route], arrived[route])
    output, grads, context = local_layer(
        bal_codes[:row_count], bal_scales[:row_count], labels[:row_count], w_full, grad_out
    )
    grads_padded = pad_rows(grads, slot, 0)
    going_back = [
        cut_rows(grads_padded, landing[route], arrived[route], slot) for route in range(4)
    ]
    returned = [shifted(going_back[route], "dp", -offsets[route]) for route in range(4)]
    home_grads = pad_rows(jnp.where(inside[:, None, None], grads, jnp.zeros_like(grads)), slot, 0)
    for route in range(4):
        home_grads = put_rows(
            home_grads, returned[route], own_entries[route, 0], own_entries[route, 1]
        )
    grad_codes = home_grads[:row_count]
    term = lax.dot_general(
        context, grad_out, (((0,), (0,)), ((), ())), preferred_element_type=jnp.float32
    )
    grad_w = lax.psum_scatter(
        term.astype(jnp.bfloat16), "fsdp", scatter_dimension=0, tiled=True
    ).astype(jnp.float32)
    return (output[None, None], grad_codes[None, None], grad_w[None])


BF = jnp.bfloat16
F32 = jnp.float32
PAIR = 256


def iota(shape, dim):
    return lax.broadcasted_iota(jnp.int32, shape, dim)


def hot(mask):
    return mask.astype(F32).astype(BF)


def mm(a, b, dims=((1,), (0,))):
    return lax.dot_general(a, b, (dims, ((), ())), preferred_element_type=F32)


def window(block, share):
    low = block * share // 128 * 128
    high = -(-(block + 1) * share // 128) * 128
    return low, high


def heads_kernel(
    groups, share, width,
    table, kept_ref, seg_ref, scales_ref, codes_hbm, w_hbm, cot_hbm,
    out_ref, grad_ref, gw_ref,
    codes, tall, scal, img_send, img_recv, w_all, cot_all, bal, qkv, scl, probs,
    ctx_own, ctx_all, packed, nat, back_send, back_recv,
    load_s, cot_s, cot_r, fwd_s, fwd_r, img_s, img_r, ctx_s, ctx_r, back_s, back_r,
    wsib_s, wsib_r, wx_s, wx_r, wq_s, wq_r, wf_s, wf_r,
):
    pos = lax.axis_index("dp")
    me = lax.axis_index("fsdp")
    sib = me + 1 - 2 * (me % 2)
    cross = (me + 2) % 4
    diag = (sib + 2) % 4
    peer = (me, sib, cross, diag)
    quad = pos % 4
    rows = cot_hbm.shape[0]
    slot = img_send.shape[0] // 4
    feats = 3 * width
    model = cot_hbm.shape[1]
    head = width // HEADS
    factor = 1.0 / math.sqrt(head)

    def remote(src, dst, s, r, where):
        return pltpu.make_async_remote_copy(
            src_ref=src, dst_ref=dst, send_sem=s, recv_sem=r,
            device_id=where, device_id_type=pl.DeviceIdType.MESH,
        )

    def at_dp(index):
        return (index, me)

    def at_fsdp(index):
        return (pos, index)

    loads = [
        pltpu.make_async_copy(codes_hbm, codes, load_s.at[0]),
        pltpu.make_async_copy(w_hbm, w_all.at[0, pl.ds(0, share)], load_s.at[1]),
        pltpu.make_async_copy(cot_hbm, cot_all.at[0], load_s.at[2]),
    ]
    for load in loads:
        load.start()
    img_recv[...] = jnp.zeros_like(img_recv)
    back_recv[...] = jnp.zeros_like(back_recv)

    barrier = pltpu.get_barrier_semaphore()
    for r in (1, 2, 3):
        pl.semaphore_signal(barrier, inc=1, device_id=at_fsdp(peer[r]),
                            device_id_type=pl.DeviceIdType.MESH)
    valid_to = [(pos + o >= 0) & (pos + o < groups) for o in offsets]
    valid_from = [(pos - o >= 0) & (pos - o < groups) for o in offsets]
    for d in range(4):
        @pl.when(valid_to[d])
        def _(d=d):
            pl.semaphore_signal(barrier, inc=1, device_id=at_dp(pos + offsets[d]),
                                device_id_type=pl.DeviceIdType.MESH)
    far = pos + 3 - 2 * quad
    outer = (quad == 0) | (quad == 3)

    @pl.when(outer)
    def _():
        pl.semaphore_signal(barrier, inc=1, device_id=at_dp(far),
                            device_id_type=pl.DeviceIdType.MESH)
    pl.semaphore_wait(barrier, 3 + jnp.minimum(pos, 2) + jnp.minimum(groups - 1 - pos, 2)
                      + outer.astype(jnp.int32))

    tiles = model // 128
    cuts = [tiles * i // 4 * 128 for i in range(5)]

    def columns(ref, r, i):
        return ref.at[r, pl.ds(0, share), pl.ds(cuts[i], cuts[i + 1] - cuts[i])]

    w_sib = remote(w_hbm, w_all.at[1, pl.ds(0, share)], wsib_s, wsib_r, at_fsdp(sib))
    w_cross = [
        remote(w_hbm.at[:, pl.ds(cuts[i], cuts[i + 1] - cuts[i])], columns(w_all, 2, i),
               wx_s.at[i], wx_r.at[i], at_fsdp(cross))
        for i in range(4)
    ]
    w_quad = [
        [remote(columns(w_all, 2, i), columns(w_all, 2, i), wq_s.at[4 * i + p], wq_r.at[i],
                at_dp(pos - quad + p)) for p in range(4)]
        for i in range(4)
    ]
    w_fwd = [
        remote(columns(w_all, 2, i), columns(w_all, 3, i), wf_s.at[i], wf_r.at[i], at_fsdp(sib))
        for i in range(4)
    ]
    for i in range(4):
        @pl.when(quad == i)
        def _(i=i):
            w_cross[i].start()
    w_sib.start()

    hr = rows // 2
    cot_out = [
        remote(cot_hbm.at[pl.ds(c * hr, hr)], cot_all.at[2, pl.ds(c * hr, hr)],
               cot_s.at[c], cot_r.at[c], at_fsdp(cross))
        for c in range(2)
    ]
    cot_sib = remote(cot_hbm, cot_all.at[1], cot_s.at[2], cot_r.at[2], at_fsdp(sib))
    forward = [
        remote(cot_all.at[2, pl.ds(c * hr, hr)], cot_all.at[3, pl.ds(c * hr, hr)],
               fwd_s.at[c], fwd_r.at[c], at_fsdp(sib))
        for c in range(2)
    ]

    kept = kept_ref[0, 0]
    r64 = iota((4 * slot, rows), 0)
    c64 = iota((4 * slot, rows), 1)

    def selection(starts, lengths):
        mask = jnp.zeros((4 * slot, rows), F32)
        for d in range(4):
            step = r64 - d * slot
            ok = (step >= 0) & (step < lengths[d]) & (step < slot) & (c64 == starts[d] + step)
            mask = mask + ok.astype(F32)
        return mask.astype(BF)

    own_start = [table[0, d, pos] for d in range(4)]
    own_len = [table[1, d, pos] for d in range(4)]
    landing, arrived = [], []
    for d in range(4):
        src = jnp.clip(pos - offsets[d], 0, groups - 1)
        landing.append(table[2, d, src])
        arrived.append(jnp.where(valid_from[d], table[1, d, src], 0))
    tall[...] = jnp.zeros_like(tall)
    for m in range(3):
        tall[m * 8:m * 8 + scales_ref.shape[1]] = scales_ref[m].astype(F32)
    rr = iota((rows, rows), 0)
    cc = iota((rows, rows), 1)
    scal[...] = mm(hot(rr == cc), tall[...].astype(BF), ((1,), (1,))).astype(BF)
    loads[0].wait()
    chosen = selection(own_start, own_len)
    for m in range(3):
        img_send[:, m * width:(m + 1) * width] = mm(chosen, codes[m]).astype(BF)
    img_send[:, feats:] = mm(chosen, scal[...]).astype(BF)
    images = []
    for d in range(4):
        part = pl.ds(d * slot, slot)
        images.append(remote(img_send.at[part], img_recv.at[part], img_s.at[d], img_r.at[d],
                             at_dp(jnp.clip(pos + offsets[d], 0, groups - 1))))

        @pl.when(valid_to[d])
        def _(d=d):
            images[d].start()

    loads[1].wait()
    loads[2].wait()
    for r in range(4):
        w_all[r, share:PAIR] = jnp.zeros((PAIR - share, model), BF)
    gc_own = mm(cot_all[0], w_all[0], ((1,), (1,))).astype(BF)

    keep_hot = hot((rr == cc) & (rr < kept))

    def placing(starts, lengths):
        r_ = iota((rows, 4 * slot), 0)
        c_ = iota((rows, 4 * slot), 1)
        mask = jnp.zeros((rows, 4 * slot), F32)
        for d in range(4):
            step = c_ - d * slot
            ok = (step >= 0) & (step < lengths[d]) & (step < slot) & (r_ == starts[d] + step)
            mask = mask + ok.astype(F32)
        return mask.astype(BF)

    row_id = iota((1, rows), 1)
    marks = jnp.where(row_id < kept, seg_ref[...], -1)
    for d in range(4):
        here = (row_id >= landing[d]) & (row_id < landing[d] + arrived[d])
        marks = jnp.where(here, 100000 + d, marks)
    marks_row = jnp.broadcast_to(marks.astype(F32), (rows, rows))
    marks_col = jnp.sum(jnp.where(rr == cc, marks_row, 0.0), axis=1, keepdims=True)
    same = marks_col == marks_row
    bias = jnp.where(same, 0.0, -jnp.inf)
    bias2 = jnp.concatenate([bias, bias], axis=0)

    for i in range(4):
        @pl.when(quad == i)
        def _(i=i):
            w_cross[i].wait_recv()
            for p in range(4):
                if p != i:
                    w_quad[i][p].start()
            w_fwd[i].start()
    for copy in cot_out + [cot_sib]:
        copy.start()

    for d in range(4):
        @pl.when(valid_from[d])
        def _(d=d):
            images[d].wait_recv()
    place = placing(landing, arrived)
    for m in range(3):
        part = slice(m * width, (m + 1) * width)
        bal[:, part] = (mm(keep_hot, codes[m]) + mm(place, img_recv[:, part])).astype(BF)
    bal[:, feats:] = (mm(keep_hot, scal[...]) + mm(place, img_recv[:, feats:])).astype(BF)

    lanes = iota((1, PAIR), 1)
    first = hot(lanes < head)
    second = hot(lanes >= head)
    for j in range(4):
        low, high = window(j, share)
        pick = hot((iota((high - low, PAIR), 0) + low == iota((high - low, PAIR), 1) + j * share)
                   & (iota((high - low, PAIR), 1) < share))
        block = (iota((128, PAIR), 1) + j * share) // 128
        for m in range(3):
            values = mm(bal[:, m * width + low:m * width + high], pick)
            spread = hot((iota((128, PAIR), 0) == block + m * 8)
                         & (iota((128, PAIR), 1) < share))
            scale = mm(bal[:, feats:feats + 128], spread)
            scl[m * 4 + j] = scale.astype(BF)
            qkv[m * 4 + j] = (values * scale).astype(BF)

    def stack(x):
        return jnp.concatenate([x * first, x * second], axis=0)

    def wide(x):
        return jnp.concatenate([x[:rows], x[rows:]], axis=1)

    ctx_out = [None] * 4
    for r in (2, 3, 1, 0):
        j = peer[r]
        scores = mm(stack(qkv[j]), qkv[4 + j], ((1,), (1,))) * factor + bias2
        top = jnp.max(scores, axis=-1, keepdims=True)
        weights = jnp.exp(scores - top)
        p = weights / jnp.sum(weights, axis=-1, keepdims=True)
        probs[r] = p
        ctx = mm(wide(p.astype(BF)), stack(qkv[8 + j])).astype(BF)
        ctx_own[r] = ctx
        if r == 0:
            ctx_all[0] = ctx
        else:
            ctx_out[r] = remote(ctx_own.at[r], ctx_all.at[r], ctx_s.at[r], ctx_r.at[r],
                                at_fsdp(j))
            ctx_out[r].start()

    def backward(r, gc):
        j = peer[r]
        p = probs[r]
        gstack = stack(gc)
        gp = mm(gstack, qkv[8 + j], ((1,), (1,)))
        total = jnp.sum(p * gp, axis=-1, keepdims=True)
        gs = (p * (gp - total) * factor).astype(BF)
        gq = mm(wide(gs), stack(qkv[4 + j]))
        gk = mm(gs, stack(qkv[j]), ((0,), (0,)))
        gv = mm(p.astype(BF), gstack, ((0,), (0,)))
        for m, g in enumerate((gq, gk, gv)):
            packed[m * 4 + j] = (g * scl[m * 4 + j].astype(F32)).astype(BF)

    def gradient(r):
        return mm(cot_all[0], w_all[r], ((1,), (1,))).astype(BF)

    backward(0, gc_own)
    w_sib.wait_recv()
    backward(1, gradient(1))
    for i in range(4):
        @pl.when(quad != i)
        def _(i=i):
            w_quad[i][i].wait_recv()
            w_fwd[i].start()
    backward(2, gradient(2))
    for i in range(4):
        w_fwd[i].wait_recv()
    backward(3, gradient(3))
    for m in range(3):
        blocks = [None] * (width // 128)
        for j in range(4):
            low, high = window(j, share)
            spread = hot((iota((PAIR, high - low), 1) + low
                          == iota((PAIR, high - low), 0) + j * share)
                         & (iota((PAIR, high - low), 0) < share))
            piece = mm(packed[m * 4 + j], spread)
            for b in range((high - low) // 128):
                add = piece[:, b * 128:(b + 1) * 128]
                at = low // 128 + b
                blocks[at] = add if blocks[at] is None else blocks[at] + add
        for b in range(width // 128):
            nat[:, m * width + b * 128:m * width + (b + 1) * 128] = blocks[b].astype(BF)

    back_send[...] = mm(selection(landing, arrived), nat[...]).astype(BF)
    returns = []
    for d in range(4):
        part = pl.ds(d * slot, slot)
        returns.append(remote(back_send.at[part], back_recv.at[part], back_s.at[d], back_r.at[d],
                              at_dp(jnp.clip(pos - offsets[d], 0, groups - 1))))

        @pl.when(valid_from[d])
        def _(d=d):
            returns[d].start()

    out_ref[...] = mm(jnp.concatenate([ctx_own[r] for r in range(4)], axis=1),
                      w_all[...].reshape(4 * PAIR, model)).astype(BF)

    for c in range(2):
        cot_out[c].wait_recv()
        forward[c].start()
    cot_sib.wait_recv()
    for r in (1, 2, 3):
        ctx_out[r].wait_recv()
    for c in range(2):
        forward[c].wait_recv()
    gw_ref[...] = mm(ctx_all[...].reshape(4 * rows, PAIR), cot_all[...].reshape(4 * rows, model),
                     ((0,), (0,)))[:share]

    for d in range(4):
        @pl.when(valid_to[d])
        def _(d=d):
            returns[d].wait_recv()
    place = placing(own_start, own_len)
    for m in range(3):
        part = slice(m * width, (m + 1) * width)
        grad_ref[m] = (mm(keep_hot, nat[:, part]) + mm(place, back_recv[:, part])).astype(BF)

    for copy in cot_out + [cot_sib, w_sib] + forward + w_fwd + ctx_out[1:]:
        copy.wait_send()
    for i in range(4):
        @pl.when(quad == i)
        def _(i=i):
            w_cross[i].wait_send()
            for p in range(4):
                if p != i:
                    w_quad[i][p].wait_send()
    for d in range(4):
        @pl.when(valid_to[d])
        def _(d=d):
            images[d].wait_send()

        @pl.when(valid_from[d])
        def _(d=d):
            returns[d].wait_send()


def write_out(a, b, c, a_out, b_out, c_out, sems):
    copies = [
        pltpu.make_async_copy(src, dst, sems.at[i])
        for i, (src, dst) in enumerate(((a, a_out), (b, b_out), (c, c_out)))
    ]
    for copy in copies:
        copy.start()
    for copy in copies:
        copy.wait()


def local_by_heads(qkv_codes, block_scales, home_segments, kept_rows, pack_list, w_out, cotangent):
    groups = lax.axis_size("dp")
    rows = qkv_codes.shape[2]
    width = qkv_codes.shape[4]
    model = w_out.shape[1]
    share = w_out.shape[0]
    slot = rows // 8
    feats = 3 * width
    vmem = pl.BlockSpec(memory_space=pltpu.VMEM)
    hbm = pl.BlockSpec(memory_space=pltpu.HBM)
    smem = pl.BlockSpec(memory_space=pltpu.SMEM)
    dma = pltpu.SemaphoreType.DMA
    out, grads, gw = pl.pallas_call(
        functools.partial(heads_kernel, groups, share, width),
        out_shape=(
            pltpu.VMEM((rows, model), BF),
            pltpu.VMEM((3, rows, width), BF),
            pltpu.VMEM((share, model), F32),
        ),
        in_specs=[smem, smem, vmem, vmem, hbm, hbm, hbm],
        out_specs=(vmem, vmem, vmem),
        scratch_shapes=[
            pltpu.VMEM((3, rows, width), BF),
            pltpu.VMEM((128, rows), F32),
            pltpu.VMEM((rows, 128), BF),
            pltpu.VMEM((4 * slot, feats + 128), BF),
            pltpu.VMEM((4 * slot, feats + 128), BF),
            pltpu.VMEM((4, PAIR, model), BF),
            pltpu.VMEM((4, rows, model), BF),
            pltpu.VMEM((rows, feats + 128), BF),
            pltpu.VMEM((12, rows, PAIR), BF),
            pltpu.VMEM((12, rows, PAIR), BF),
            pltpu.VMEM((4, 2 * rows, rows), F32),
            pltpu.VMEM((4, rows, PAIR), BF),
            pltpu.VMEM((4, rows, PAIR), BF),
            pltpu.VMEM((12, rows, PAIR), BF),
            pltpu.VMEM((rows, feats), BF),
            pltpu.VMEM((4 * slot, feats), BF),
            pltpu.VMEM((4 * slot, feats), BF),
            dma((3,)), dma((3,)), dma((3,)), dma((2,)), dma((2,)), dma((4,)), dma((4,)),
            dma((4,)), dma((4,)), dma((4,)), dma((4,)),
            dma, dma, dma((4,)), dma((4,)), dma((16,)), dma((4,)), dma((4,)), dma((4,)),
        ],
        compiler_params=pltpu.CompilerParams(
            collective_id=0, has_side_effects=True, vmem_limit_bytes=58 * 1024 * 1024
        ),
        cost_estimate=pl.CostEstimate(
            flops=8 * rows * width * model, bytes_accessed=8 * 1024 * 1024, transcendentals=0
        ),
        name="attention_by_heads",
    )(
        jnp.transpose(pack_list[:, 0], (2, 1, 0)),
        kept_rows,
        home_segments[0],
        jnp.transpose(block_scales[0, 0], (1, 2, 0)),
        jnp.transpose(qkv_codes[0, 0], (1, 0, 2)),
        w_out,
        cotangent[0, 0],
    )
    results = (out, grads, gw)
    out, grads, gw = pl.pallas_call(
        write_out,
        out_shape=tuple(jax.ShapeDtypeStruct(a.shape, a.dtype) for a in results),
        in_specs=[vmem] * 3,
        out_specs=(hbm,) * 3,
        scratch_shapes=[dma((3,))],
        compiler_params=pltpu.CompilerParams(vmem_limit_bytes=4 * 1024 * 1024),
        name="write_out",
    )(*results)
    return (out[None, None], jnp.transpose(grads, (1, 0, 2))[None, None], gw[None])


def solution(mesh):
    fast = mesh.shape["fsdp"] == 4 and mesh.shape["dp"] % 4 == 0
    return jax.shard_map(
        local_by_heads if fast else local,
        mesh=mesh,
        in_specs=(
            P("dp", "fsdp", None, None, None),
            P("dp", "fsdp", None, None, None),
            P("dp", "fsdp", None),
            P("dp", "fsdp"),
            P(None, "fsdp", None, None),
            P("fsdp", None),
            P("dp", "fsdp", None, None),
        ),
        out_specs=(
            P("dp", "fsdp", None, None),
            P("dp", "fsdp", None, None, None),
            P("dp", "fsdp", None),
        ),
        check_vma=False,
    )
```

```python
import functools
import math

import jax
import jax.numpy as jnp
from jax import lax
from jax.experimental import pallas as pl
from jax.experimental.pallas import tpu as pltpu
from jax.sharding import PartitionSpec as P

HEADS = 8


offsets = (1, -1, 2, -2)


def shifted(block, axis, distance):
    devices = range(lax.axis_size(axis))
    route = [(i - distance, i) for i in devices if i - distance in devices]
    return lax.ppermute(block, axis, route)


def dequantize(codes, scales):
    count = codes.shape[0]
    blocks = scales.shape[-1]
    scaled = (
        codes.astype(jnp.float32).reshape(count, 3, blocks, -1)
        * scales.astype(jnp.float32)[..., None]
    )
    return scaled.reshape(count, 3, -1).astype(jnp.bfloat16)


def local_layer(codes, scales, labels, w_full, grad_out):
    count = codes.shape[0]
    width = w_full.shape[0]
    head_size = width // HEADS
    factor = 1.0 / math.sqrt(head_size)
    values = dequantize(codes, scales)
    query = values[:, 0].reshape(count, HEADS, head_size)
    keys = values[:, 1].reshape(count, HEADS, head_size)
    value_rows = values[:, 2].reshape(count, HEADS, head_size)
    scores = jnp.einsum("qhd,khd->hqk", query, keys, preferred_element_type=jnp.float32) * factor
    same = labels[:, None] == labels[None, :]
    scores = jnp.where(same[None], scores, -jnp.inf)
    top = jnp.max(scores, axis=-1, keepdims=True)
    weights = jnp.exp(scores - top)
    probs = weights / jnp.sum(weights, axis=-1, keepdims=True)
    probs_b = probs.astype(jnp.bfloat16)
    context = jnp.einsum("hqk,khd->qhd", probs_b, value_rows, preferred_element_type=jnp.float32)
    context = context.reshape(count, width).astype(jnp.bfloat16)
    output = jnp.dot(context, w_full, preferred_element_type=jnp.float32).astype(jnp.bfloat16)
    grad_context = lax.dot_general(
        grad_out, w_full, (((1,), (1,)), ((), ())), preferred_element_type=jnp.float32
    )
    grad_context = grad_context.astype(jnp.bfloat16).reshape(count, HEADS, head_size)
    grad_probs = jnp.einsum(
        "qhd,khd->hqk", grad_context, value_rows, preferred_element_type=jnp.float32
    )
    total = jnp.sum(probs * grad_probs, axis=-1, keepdims=True)
    grad_scores = (probs * (grad_probs - total) * factor).astype(jnp.bfloat16)
    grad_query = jnp.einsum("hqk,khd->qhd", grad_scores, keys, preferred_element_type=jnp.float32)
    grad_keys = jnp.einsum("hqk,qhd->khd", grad_scores, query, preferred_element_type=jnp.float32)
    grad_values = jnp.einsum(
        "hqk,qhd->khd", probs_b, grad_context, preferred_element_type=jnp.float32
    )
    grads = jnp.stack([grad_query, grad_keys, grad_values], axis=1).reshape(count, 3, -1)
    blocks = scales.shape[-1]
    grads = (grads.reshape(count, 3, blocks, -1) * scales.astype(jnp.float32)[..., None]).reshape(
        count, 3, -1
    )
    return (output, grads.astype(jnp.bfloat16), context)


def pad_rows(array, extra_rows, fill):
    extra = jnp.full((extra_rows,) + array.shape[1:], fill, array.dtype)
    return jnp.concatenate([array, extra], axis=0)


def cut_rows(buffer, at_row, length, slot):
    piece = lax.dynamic_slice_in_dim(buffer, at_row, slot, 0)
    present = (jnp.arange(slot) < length).reshape((slot,) + (1,) * (buffer.ndim - 1))
    return jnp.where(present, piece, jnp.zeros_like(piece))


def put_rows(buffer, piece, at_row, length):
    slot = piece.shape[0]
    old = lax.dynamic_slice_in_dim(buffer, at_row, slot, 0)
    present = (jnp.arange(slot) < length).reshape((slot,) + (1,) * (buffer.ndim - 1))
    return lax.dynamic_update_slice_in_dim(buffer, jnp.where(present, piece, old), at_row, 0)


def local(qkv_codes, block_scales, home_segments, kept_rows, pack_list, w_out, cotangent):
    position = lax.axis_index("dp")
    group_size = lax.axis_size("dp")
    codes = qkv_codes[0, 0]
    scales = block_scales[0, 0]
    segments = home_segments[0, 0]
    kept = kept_rows[0, 0]
    table = pack_list[:, 0]
    grad_out = cotangent[0, 0]
    row_count = codes.shape[0]
    slot = row_count // 8
    w_full = lax.all_gather(w_out, "fsdp", axis=0, tiled=True)
    inside = jnp.arange(row_count) < kept
    own_entries = lax.dynamic_index_in_dim(table, position, 0, keepdims=False)
    home_codes = pad_rows(codes, slot, 0)
    home_scales = pad_rows(scales, slot, 0)
    sent_codes = [
        cut_rows(home_codes, own_entries[route, 0], own_entries[route, 1], slot)
        for route in range(4)
    ]
    sent_scales = [
        cut_rows(home_scales, own_entries[route, 0], own_entries[route, 1], slot)
        for route in range(4)
    ]
    received = [
        shifted((sent_codes[route], sent_scales[route]), "dp", offsets[route]) for route in range(4)
    ]
    landing = []
    arrived = []
    for route in range(4):
        source = position - offsets[route]
        allowed = (source >= 0) & (source < group_size)
        entries = lax.dynamic_index_in_dim(
            table, jnp.clip(source, 0, group_size - 1), 0, keepdims=False
        )
        arrived.append(jnp.where(allowed, entries[route, 1], 0))
        landing.append(entries[route, 2])
    bal_codes = pad_rows(jnp.where(inside[:, None, None], codes, jnp.zeros_like(codes)), slot, 0)
    bal_scales = pad_rows(jnp.where(inside[:, None, None], scales, jnp.zeros_like(scales)), slot, 0)
    labels = pad_rows(jnp.where(inside, segments, -1), slot, -1)
    for route in range(4):
        bal_codes = put_rows(bal_codes, received[route][0], landing[route], arrived[route])
        bal_scales = put_rows(bal_scales, received[route][1], landing[route], arrived[route])
        marks = jnp.full((slot,), 100000 + route, jnp.int32)
        labels = put_rows(labels, marks, landing[route], arrived[route])
    output, grads, context = local_layer(
        bal_codes[:row_count], bal_scales[:row_count], labels[:row_count], w_full, grad_out
    )
    grads_padded = pad_rows(grads, slot, 0)
    going_back = [
        cut_rows(grads_padded, landing[route], arrived[route], slot) for route in range(4)
    ]
    returned = [shifted(going_back[route], "dp", -offsets[route]) for route in range(4)]
    home_grads = pad_rows(jnp.where(inside[:, None, None], grads, jnp.zeros_like(grads)), slot, 0)
    for route in range(4):
        home_grads = put_rows(
            home_grads, returned[route], own_entries[route, 0], own_entries[route, 1]
        )
    grad_codes = home_grads[:row_count]
    term = lax.dot_general(
        context, grad_out, (((0,), (0,)), ((), ())), preferred_element_type=jnp.float32
    )
    grad_w = lax.psum_scatter(
        term.astype(jnp.bfloat16), "fsdp", scatter_dimension=0, tiled=True
    ).astype(jnp.float32)
    return (output[None, None], grad_codes[None, None], grad_w[None])


BF = jnp.bfloat16
F32 = jnp.float32
PAIR = 256


def iota(shape, dim):
    return lax.broadcasted_iota(jnp.int32, shape, dim)


def hot(mask):
    return mask.astype(F32).astype(BF)


def mm(a, b, dims=((1,), (0,))):
    return lax.dot_general(a, b, (dims, ((), ())), preferred_element_type=F32)


def window(block, share):
    low = block * share // 128 * 128
    high = -(-(block + 1) * share // 128) * 128
    return low, high


def heads_kernel(
    groups, share, width,
    table, kept_ref, seg_ref, scales_ref, codes_hbm, w_hbm, cot_hbm,
    out_ref, grad_ref, gw_ref,
    codes, tall, scal, img_send, img_recv, w_all, cot_all, bal, qkv, scl, probs,
    ctx_own, ctx_all, packed, nat, back_send, back_recv,
    load_s, cot_s, cot_r, fwd_s, fwd_r, img_s, img_r, ctx_s, ctx_r, back_s, back_r,
    wsib_s, wsib_r, wx_s, wx_r, wq_s, wq_r, wf_s, wf_r,
):
    pos = lax.axis_index("dp")
    me = lax.axis_index("fsdp")
    sib = me + 1 - 2 * (me % 2)
    cross = (me + 2) % 4
    diag = (sib + 2) % 4
    peer = (me, sib, cross, diag)
    quad = pos % 4
    rows = cot_hbm.shape[0]
    slot = img_send.shape[0] // 4
    feats = 3 * width
    model = cot_hbm.shape[1]
    head = width // HEADS
    factor = 1.0 / math.sqrt(head)

    def remote(src, dst, s, r, where):
        return pltpu.make_async_remote_copy(
            src_ref=src, dst_ref=dst, send_sem=s, recv_sem=r,
            device_id=where, device_id_type=pl.DeviceIdType.MESH,
        )

    def at_dp(index):
        return (index, me)

    def at_fsdp(index):
        return (pos, index)

    loads = [
        pltpu.make_async_copy(codes_hbm, codes, load_s.at[0]),
        pltpu.make_async_copy(w_hbm, w_all.at[0, pl.ds(0, share)], load_s.at[1]),
        pltpu.make_async_copy(cot_hbm, cot_all.at[0], load_s.at[2]),
    ]
    for load in loads:
        load.start()
    img_recv[...] = jnp.zeros_like(img_recv)
    back_recv[...] = jnp.zeros_like(back_recv)

    barrier = pltpu.get_barrier_semaphore()
    for r in (1, 2, 3):
        pl.semaphore_signal(barrier, inc=1, device_id=at_fsdp(peer[r]),
                            device_id_type=pl.DeviceIdType.MESH)
    valid_to = [(pos + o >= 0) & (pos + o < groups) for o in offsets]
    valid_from = [(pos - o >= 0) & (pos - o < groups) for o in offsets]
    for d in range(4):
        @pl.when(valid_to[d])
        def _(d=d):
            pl.semaphore_signal(barrier, inc=1, device_id=at_dp(pos + offsets[d]),
                                device_id_type=pl.DeviceIdType.MESH)
    far = pos + 3 - 2 * quad
    outer = (quad == 0) | (quad == 3)

    @pl.when(outer)
    def _():
        pl.semaphore_signal(barrier, inc=1, device_id=at_dp(far),
                            device_id_type=pl.DeviceIdType.MESH)
    pl.semaphore_wait(barrier, 3 + jnp.minimum(pos, 2) + jnp.minimum(groups - 1 - pos, 2)
                      + outer.astype(jnp.int32))

    tiles = model // 128
    cuts = [tiles * i // 4 * 128 for i in range(5)]

    split = share // 2 // 16 * 16
    bands = ((0, split), (split, share - split))
    pieces = [(i, c) for i in range(4) for c in range(2)]

    def columns(ref, i, c):
        return ref.at[pl.ds(*bands[c]), pl.ds(cuts[i], cuts[i + 1] - cuts[i])]

    w_sib = remote(w_hbm, w_all.at[1, pl.ds(0, share)], wsib_s, wsib_r, at_fsdp(sib))
    w_cross = {
        (i, c): remote(columns(w_hbm, i, c), columns(w_all.at[2], i, c),
                       wx_s.at[2 * i + c], wx_r.at[2 * i + c], at_fsdp(cross))
        for i, c in pieces
    }
    w_quad = {
        (i, c, p): remote(columns(w_all.at[2], i, c), columns(w_all.at[2], i, c),
                          wq_s.at[8 * i + 4 * c + p], wq_r.at[2 * i + c], at_dp(pos - quad + p))
        for i, c in pieces for p in range(4)
    }
    w_fwd = {
        (i, c): remote(columns(w_all.at[2], i, c), columns(w_all.at[3], i, c),
                       wf_s.at[2 * i + c], wf_r.at[2 * i + c], at_fsdp(sib))
        for i, c in pieces
    }
    for i in range(4):
        @pl.when(quad == i)
        def _(i=i):
            w_cross[i, 0].start()
            w_cross[i, 1].start()
    w_sib.start()

    hr = rows // 2
    cot_out = [
        remote(cot_hbm.at[pl.ds(c * hr, hr)], cot_all.at[2, pl.ds(c * hr, hr)],
               cot_s.at[c], cot_r.at[c], at_fsdp(cross))
        for c in range(2)
    ]
    cot_sib = remote(cot_hbm, cot_all.at[1], cot_s.at[2], cot_r.at[2], at_fsdp(sib))
    forward = [
        remote(cot_all.at[2, pl.ds(c * hr, hr)], cot_all.at[3, pl.ds(c * hr, hr)],
               fwd_s.at[c], fwd_r.at[c], at_fsdp(sib))
        for c in range(2)
    ]

    kept = kept_ref[0, 0]
    r64 = iota((4 * slot, rows), 0)
    c64 = iota((4 * slot, rows), 1)

    def selection(starts, lengths):
        mask = jnp.zeros((4 * slot, rows), F32)
        for d in range(4):
            step = r64 - d * slot
            ok = (step >= 0) & (step < lengths[d]) & (step < slot) & (c64 == starts[d] + step)
            mask = mask + ok.astype(F32)
        return mask.astype(BF)

    own_start = [table[0, d, pos] for d in range(4)]
    own_len = [table[1, d, pos] for d in range(4)]
    landing, arrived = [], []
    for d in range(4):
        src = jnp.clip(pos - offsets[d], 0, groups - 1)
        landing.append(table[2, d, src])
        arrived.append(jnp.where(valid_from[d], table[1, d, src], 0))
    tall[...] = jnp.zeros_like(tall)
    for m in range(3):
        tall[m * 8:m * 8 + scales_ref.shape[1]] = scales_ref[m].astype(F32)
    rr = iota((rows, rows), 0)
    cc = iota((rows, rows), 1)
    scal[...] = mm(hot(rr == cc), tall[...].astype(BF), ((1,), (1,))).astype(BF)
    loads[0].wait()
    chosen = selection(own_start, own_len)
    for m in range(3):
        img_send[:, m * width:(m + 1) * width] = mm(chosen, codes[m]).astype(BF)
    img_send[:, feats:] = mm(chosen, scal[...]).astype(BF)
    images = []
    for d in range(4):
        part = pl.ds(d * slot, slot)
        images.append(remote(img_send.at[part], img_recv.at[part], img_s.at[d], img_r.at[d],
                             at_dp(jnp.clip(pos + offsets[d], 0, groups - 1))))

        @pl.when(valid_to[d])
        def _(d=d):
            images[d].start()

    def hand_on(c):
        for i in range(4):
            @pl.when(quad == i)
            def _(i=i):
                w_cross[i, c].wait_recv()
                for p in range(4):
                    if p != i:
                        w_quad[i, c, p].start()
                w_fwd[i, c].start()

    hand_on(0)

    loads[1].wait()
    loads[2].wait()
    for r in range(4):
        w_all[r, share:PAIR] = jnp.zeros((PAIR - share, model), BF)
    gc_own = mm(cot_all[0], w_all[0], ((1,), (1,))).astype(BF)

    keep = iota((rows, 1), 0) < kept
    lanes = iota((1, PAIR), 1)
    first = hot(lanes < head)
    second = hot(lanes >= head)
    picks = []
    spreads = [None] * 12
    for j in range(4):
        low, high = window(j, share)
        picks.append(hot((iota((high - low, PAIR), 0) + low
                          == iota((high - low, PAIR), 1) + j * share)
                         & (iota((high - low, PAIR), 1) < share)))
        block = jnp.where(lanes < share, (lanes + j * share) // 128, -128)
        for m in range(3):
            spreads[m * 4 + j] = hot(iota((128, PAIR), 0) == block + m * 8)

    def placing(starts, lengths):
        r_ = iota((rows, 4 * slot), 0)
        c_ = iota((rows, 4 * slot), 1)
        mask = jnp.zeros((rows, 4 * slot), F32)
        for d in range(4):
            step = c_ - d * slot
            ok = (step >= 0) & (step < lengths[d]) & (step < slot) & (r_ == starts[d] + step)
            mask = mask + ok.astype(F32)
        return mask.astype(BF)

    row_id = iota((1, rows), 1)
    marks = jnp.where(row_id < kept, seg_ref[...], -1)
    for d in range(4):
        here = (row_id >= landing[d]) & (row_id < landing[d] + arrived[d])
        marks = jnp.where(here, 100000 + d, marks)
    marks_row = jnp.broadcast_to(marks.astype(F32), (rows, rows))
    marks_col = jnp.sum(jnp.where(rr == cc, marks_row, 0.0), axis=1, keepdims=True)
    same = marks_col == marks_row
    bias = jnp.where(same, 0.0, -jnp.inf)
    bias2 = jnp.concatenate([bias, bias], axis=0)

    hand_on(1)
    for copy in cot_out + [cot_sib]:
        copy.start()

    for d in range(4):
        @pl.when(valid_from[d])
        def _(d=d):
            images[d].wait_recv()
    place = placing(landing, arrived)
    for m in range(3):
        part = slice(m * width, (m + 1) * width)
        bal[:, part] = jnp.where(keep, codes[m], mm(place, img_recv[:, part]).astype(BF))
    bal[:, feats:] = jnp.where(keep, scal[...], mm(place, img_recv[:, feats:]).astype(BF))

    for j in range(4):
        low, high = window(j, share)
        for m in range(3):
            values = mm(bal[:, m * width + low:m * width + high], picks[j])
            scale = mm(bal[:, feats:feats + 128], spreads[m * 4 + j])
            scl[m * 4 + j] = scale.astype(BF)
            qkv[m * 4 + j] = (values * scale).astype(BF)

    def stack(x):
        return jnp.concatenate([x * first, x * second], axis=0)

    def wide(x):
        return jnp.concatenate([x[:rows], x[rows:]], axis=1)

    w_sib.wait_recv()
    ctx_out = [None] * 4
    for r in range(4):
        j = peer[r]
        scores = mm(stack(qkv[j]), qkv[4 + j], ((1,), (1,))) * factor + bias2
        top = jnp.max(scores, axis=-1, keepdims=True)
        weights = jnp.exp(scores - top)
        p = weights / jnp.sum(weights, axis=-1, keepdims=True)
        probs[r] = p
        ctx = mm(wide(p.astype(BF)), stack(qkv[8 + j])).astype(BF)
        ctx_own[r] = ctx
        if r == 0:
            ctx_all[0] = ctx
        else:
            ctx_out[r] = remote(ctx_own.at[r], ctx_all.at[r], ctx_s.at[r], ctx_r.at[r],
                                at_fsdp(j))

    def backward(r, gc):
        j = peer[r]
        p = probs[r]
        gstack = stack(gc)
        gp = mm(gstack, qkv[8 + j], ((1,), (1,)))
        total = jnp.sum(p * gp, axis=-1, keepdims=True)
        gs = (p * (gp - total) * factor).astype(BF)
        gq = mm(wide(gs), stack(qkv[4 + j]))
        gk = mm(gs, stack(qkv[j]), ((0,), (0,)))
        gv = mm(p.astype(BF), gstack, ((0,), (0,)))
        for m, g in enumerate((gq, gk, gv)):
            packed[m * 4 + j] = (g * scl[m * 4 + j].astype(F32)).astype(BF)

    def gradient(r):
        return mm(cot_all[0], w_all[r], ((1,), (1,))).astype(BF)

    backward(0, gc_own)
    backward(1, gradient(1))
    for r in (1, 2, 3):
        ctx_out[r].start()
    for i, c in sorted(pieces, key=lambda piece: piece[1]):
        @pl.when(quad != i)
        def _(i=i, c=c):
            w_quad[i, c, i].wait_recv()
            w_fwd[i, c].start()
    for piece in pieces:
        w_fwd[piece].wait_recv()
    backward(2, gradient(2))
    backward(3, gradient(3))
    for m in range(3):
        blocks = [None] * (width // 128)
        for j in range(4):
            low, high = window(j, share)
            spread = hot((iota((PAIR, high - low), 1) + low
                          == iota((PAIR, high - low), 0) + j * share)
                         & (iota((PAIR, high - low), 0) < share))
            piece = mm(packed[m * 4 + j], spread)
            for b in range((high - low) // 128):
                add = piece[:, b * 128:(b + 1) * 128]
                at = low // 128 + b
                blocks[at] = add if blocks[at] is None else blocks[at] + add
        for b in range(width // 128):
            nat[:, m * width + b * 128:m * width + (b + 1) * 128] = blocks[b].astype(BF)

    back_send[...] = mm(selection(landing, arrived), nat[...]).astype(BF)
    returns = []
    for d in range(4):
        part = pl.ds(d * slot, slot)
        returns.append(remote(back_send.at[part], back_recv.at[part], back_s.at[d], back_r.at[d],
                              at_dp(jnp.clip(pos - offsets[d], 0, groups - 1))))

        @pl.when(valid_from[d])
        def _(d=d):
            returns[d].start()

    out_ref[...] = mm(jnp.concatenate([ctx_own[r] for r in range(4)], axis=1),
                      w_all[...].reshape(4 * PAIR, model)).astype(BF)

    for c in range(2):
        cot_out[c].wait_recv()
        forward[c].start()
    cot_sib.wait_recv()
    for r in (1, 2, 3):
        ctx_out[r].wait_recv()
    for c in range(2):
        forward[c].wait_recv()
    gw_ref[...] = mm(ctx_all[...].reshape(4 * rows, PAIR), cot_all[...].reshape(4 * rows, model),
                     ((0,), (0,)))[:share]

    for d in range(4):
        @pl.when(valid_to[d])
        def _(d=d):
            returns[d].wait_recv()
    place = placing(own_start, own_len)
    for m in range(3):
        part = slice(m * width, (m + 1) * width)
        grad_ref[m] = jnp.where(keep, nat[:, part], mm(place, back_recv[:, part]).astype(BF))

    for copy in cot_out + [cot_sib, w_sib] + forward + list(w_fwd.values()) + ctx_out[1:]:
        copy.wait_send()
    for i in range(4):
        @pl.when(quad == i)
        def _(i=i):
            for c in range(2):
                w_cross[i, c].wait_send()
                for p in range(4):
                    if p != i:
                        w_quad[i, c, p].wait_send()
    for d in range(4):
        @pl.when(valid_to[d])
        def _(d=d):
            images[d].wait_send()

        @pl.when(valid_from[d])
        def _(d=d):
            returns[d].wait_send()


def write_out(a, b, c, a_out, b_out, c_out, sems):
    copies = [
        pltpu.make_async_copy(src, dst, sems.at[i])
        for i, (src, dst) in enumerate(((a, a_out), (b, b_out), (c, c_out)))
    ]
    for copy in copies:
        copy.start()
    for copy in copies:
        copy.wait()


def local_by_heads(qkv_codes, block_scales, home_segments, kept_rows, pack_list, w_out, cotangent):
    groups = lax.axis_size("dp")
    rows = qkv_codes.shape[2]
    width = qkv_codes.shape[4]
    model = w_out.shape[1]
    share = w_out.shape[0]
    slot = rows // 8
    feats = 3 * width
    vmem = pl.BlockSpec(memory_space=pltpu.VMEM)
    hbm = pl.BlockSpec(memory_space=pltpu.HBM)
    smem = pl.BlockSpec(memory_space=pltpu.SMEM)
    dma = pltpu.SemaphoreType.DMA
    out, grads, gw = pl.pallas_call(
        functools.partial(heads_kernel, groups, share, width),
        out_shape=(
            pltpu.VMEM((rows, model), BF),
            pltpu.VMEM((3, rows, width), BF),
            pltpu.VMEM((share, model), F32),
        ),
        in_specs=[smem, smem, vmem, vmem, hbm, hbm, hbm],
        out_specs=(vmem, vmem, vmem),
        scratch_shapes=[
            pltpu.VMEM((3, rows, width), BF),
            pltpu.VMEM((128, rows), F32),
            pltpu.VMEM((rows, 128), BF),
            pltpu.VMEM((4 * slot, feats + 128), BF),
            pltpu.VMEM((4 * slot, feats + 128), BF),
            pltpu.VMEM((4, PAIR, model), BF),
            pltpu.VMEM((4, rows, model), BF),
            pltpu.VMEM((rows, feats + 128), BF),
            pltpu.VMEM((12, rows, PAIR), BF),
            pltpu.VMEM((12, rows, PAIR), BF),
            pltpu.VMEM((4, 2 * rows, rows), F32),
            pltpu.VMEM((4, rows, PAIR), BF),
            pltpu.VMEM((4, rows, PAIR), BF),
            pltpu.VMEM((12, rows, PAIR), BF),
            pltpu.VMEM((rows, feats), BF),
            pltpu.VMEM((4 * slot, feats), BF),
            pltpu.VMEM((4 * slot, feats), BF),
            dma((3,)), dma((3,)), dma((3,)), dma((2,)), dma((2,)), dma((4,)), dma((4,)),
            dma((4,)), dma((4,)), dma((4,)), dma((4,)),
            dma, dma, dma((8,)), dma((8,)), dma((32,)), dma((8,)), dma((8,)), dma((8,)),
        ],
        compiler_params=pltpu.CompilerParams(
            collective_id=0, has_side_effects=True, vmem_limit_bytes=58 * 1024 * 1024
        ),
        cost_estimate=pl.CostEstimate(
            flops=8 * rows * width * model, bytes_accessed=8 * 1024 * 1024, transcendentals=0
        ),
        name="attention_by_heads",
    )(
        jnp.transpose(pack_list[:, 0], (2, 1, 0)),
        kept_rows,
        home_segments[0],
        jnp.transpose(block_scales[0, 0], (1, 2, 0)),
        jnp.transpose(qkv_codes[0, 0], (1, 0, 2)),
        w_out,
        cotangent[0, 0],
    )
    results = (out, grads, gw)
    out, grads, gw = pl.pallas_call(
        write_out,
        out_shape=tuple(jax.ShapeDtypeStruct(a.shape, a.dtype) for a in results),
        in_specs=[vmem] * 3,
        out_specs=(hbm,) * 3,
        scratch_shapes=[dma((3,))],
        compiler_params=pltpu.CompilerParams(vmem_limit_bytes=4 * 1024 * 1024),
        name="write_out",
    )(*results)
    return (out[None, None], jnp.transpose(grads, (1, 0, 2))[None, None], gw[None])


def solution(mesh):
    fast = mesh.shape["fsdp"] == 4 and mesh.shape["dp"] % 4 == 0
    return jax.shard_map(
        local_by_heads if fast else local,
        mesh=mesh,
        in_specs=(
            P("dp", "fsdp", None, None, None),
            P("dp", "fsdp", None, None, None),
            P("dp", "fsdp", None),
            P("dp", "fsdp"),
            P(None, "fsdp", None, None),
            P("fsdp", None),
            P("dp", "fsdp", None, None),
        ),
        out_specs=(
            P("dp", "fsdp", None, None),
            P("dp", "fsdp", None, None, None),
            P("dp", "fsdp", None),
        ),
        check_vma=False,
    )
```

```python
import functools
import math

import jax
import jax.numpy as jnp
from jax import lax
from jax.experimental import pallas as pl
from jax.experimental.pallas import tpu as pltpu
from jax.sharding import PartitionSpec as P

HEADS = 8


offsets = (1, -1, 2, -2)


def shifted(block, axis, distance):
    devices = range(lax.axis_size(axis))
    route = [(i - distance, i) for i in devices if i - distance in devices]
    return lax.ppermute(block, axis, route)


def dequantize(codes, scales):
    count = codes.shape[0]
    blocks = scales.shape[-1]
    scaled = (
        codes.astype(jnp.float32).reshape(count, 3, blocks, -1)
        * scales.astype(jnp.float32)[..., None]
    )
    return scaled.reshape(count, 3, -1).astype(jnp.bfloat16)


def local_layer(codes, scales, labels, w_full, grad_out):
    count = codes.shape[0]
    width = w_full.shape[0]
    head_size = width // HEADS
    factor = 1.0 / math.sqrt(head_size)
    values = dequantize(codes, scales)
    query = values[:, 0].reshape(count, HEADS, head_size)
    keys = values[:, 1].reshape(count, HEADS, head_size)
    value_rows = values[:, 2].reshape(count, HEADS, head_size)
    scores = jnp.einsum("qhd,khd->hqk", query, keys, preferred_element_type=jnp.float32) * factor
    same = labels[:, None] == labels[None, :]
    scores = jnp.where(same[None], scores, -jnp.inf)
    top = jnp.max(scores, axis=-1, keepdims=True)
    weights = jnp.exp(scores - top)
    probs = weights / jnp.sum(weights, axis=-1, keepdims=True)
    probs_b = probs.astype(jnp.bfloat16)
    context = jnp.einsum("hqk,khd->qhd", probs_b, value_rows, preferred_element_type=jnp.float32)
    context = context.reshape(count, width).astype(jnp.bfloat16)
    output = jnp.dot(context, w_full, preferred_element_type=jnp.float32).astype(jnp.bfloat16)
    grad_context = lax.dot_general(
        grad_out, w_full, (((1,), (1,)), ((), ())), preferred_element_type=jnp.float32
    )
    grad_context = grad_context.astype(jnp.bfloat16).reshape(count, HEADS, head_size)
    grad_probs = jnp.einsum(
        "qhd,khd->hqk", grad_context, value_rows, preferred_element_type=jnp.float32
    )
    total = jnp.sum(probs * grad_probs, axis=-1, keepdims=True)
    grad_scores = (probs * (grad_probs - total) * factor).astype(jnp.bfloat16)
    grad_query = jnp.einsum("hqk,khd->qhd", grad_scores, keys, preferred_element_type=jnp.float32)
    grad_keys = jnp.einsum("hqk,qhd->khd", grad_scores, query, preferred_element_type=jnp.float32)
    grad_values = jnp.einsum(
        "hqk,qhd->khd", probs_b, grad_context, preferred_element_type=jnp.float32
    )
    grads = jnp.stack([grad_query, grad_keys, grad_values], axis=1).reshape(count, 3, -1)
    blocks = scales.shape[-1]
    grads = (grads.reshape(count, 3, blocks, -1) * scales.astype(jnp.float32)[..., None]).reshape(
        count, 3, -1
    )
    return (output, grads.astype(jnp.bfloat16), context)


def pad_rows(array, extra_rows, fill):
    extra = jnp.full((extra_rows,) + array.shape[1:], fill, array.dtype)
    return jnp.concatenate([array, extra], axis=0)


def cut_rows(buffer, at_row, length, slot):
    piece = lax.dynamic_slice_in_dim(buffer, at_row, slot, 0)
    present = (jnp.arange(slot) < length).reshape((slot,) + (1,) * (buffer.ndim - 1))
    return jnp.where(present, piece, jnp.zeros_like(piece))


def put_rows(buffer, piece, at_row, length):
    slot = piece.shape[0]
    old = lax.dynamic_slice_in_dim(buffer, at_row, slot, 0)
    present = (jnp.arange(slot) < length).reshape((slot,) + (1,) * (buffer.ndim - 1))
    return lax.dynamic_update_slice_in_dim(buffer, jnp.where(present, piece, old), at_row, 0)


def local(qkv_codes, block_scales, home_segments, kept_rows, pack_list, w_out, cotangent):
    position = lax.axis_index("dp")
    group_size = lax.axis_size("dp")
    codes = qkv_codes[0, 0]
    scales = block_scales[0, 0]
    segments = home_segments[0, 0]
    kept = kept_rows[0, 0]
    table = pack_list[:, 0]
    grad_out = cotangent[0, 0]
    row_count = codes.shape[0]
    slot = row_count // 8
    w_full = lax.all_gather(w_out, "fsdp", axis=0, tiled=True)
    inside = jnp.arange(row_count) < kept
    own_entries = lax.dynamic_index_in_dim(table, position, 0, keepdims=False)
    home_codes = pad_rows(codes, slot, 0)
    home_scales = pad_rows(scales, slot, 0)
    sent_codes = [
        cut_rows(home_codes, own_entries[route, 0], own_entries[route, 1], slot)
        for route in range(4)
    ]
    sent_scales = [
        cut_rows(home_scales, own_entries[route, 0], own_entries[route, 1], slot)
        for route in range(4)
    ]
    received = [
        shifted((sent_codes[route], sent_scales[route]), "dp", offsets[route]) for route in range(4)
    ]
    landing = []
    arrived = []
    for route in range(4):
        source = position - offsets[route]
        allowed = (source >= 0) & (source < group_size)
        entries = lax.dynamic_index_in_dim(
            table, jnp.clip(source, 0, group_size - 1), 0, keepdims=False
        )
        arrived.append(jnp.where(allowed, entries[route, 1], 0))
        landing.append(entries[route, 2])
    bal_codes = pad_rows(jnp.where(inside[:, None, None], codes, jnp.zeros_like(codes)), slot, 0)
    bal_scales = pad_rows(jnp.where(inside[:, None, None], scales, jnp.zeros_like(scales)), slot, 0)
    labels = pad_rows(jnp.where(inside, segments, -1), slot, -1)
    for route in range(4):
        bal_codes = put_rows(bal_codes, received[route][0], landing[route], arrived[route])
        bal_scales = put_rows(bal_scales, received[route][1], landing[route], arrived[route])
        marks = jnp.full((slot,), 100000 + route, jnp.int32)
        labels = put_rows(labels, marks, landing[route], arrived[route])
    output, grads, context = local_layer(
        bal_codes[:row_count], bal_scales[:row_count], labels[:row_count], w_full, grad_out
    )
    grads_padded = pad_rows(grads, slot, 0)
    going_back = [
        cut_rows(grads_padded, landing[route], arrived[route], slot) for route in range(4)
    ]
    returned = [shifted(going_back[route], "dp", -offsets[route]) for route in range(4)]
    home_grads = pad_rows(jnp.where(inside[:, None, None], grads, jnp.zeros_like(grads)), slot, 0)
    for route in range(4):
        home_grads = put_rows(
            home_grads, returned[route], own_entries[route, 0], own_entries[route, 1]
        )
    grad_codes = home_grads[:row_count]
    term = lax.dot_general(
        context, grad_out, (((0,), (0,)), ((), ())), preferred_element_type=jnp.float32
    )
    grad_w = lax.psum_scatter(
        term.astype(jnp.bfloat16), "fsdp", scatter_dimension=0, tiled=True
    ).astype(jnp.float32)
    return (output[None, None], grad_codes[None, None], grad_w[None])


BF = jnp.bfloat16
F32 = jnp.float32
PAIR = 256


def iota(shape, dim):
    return lax.broadcasted_iota(jnp.int32, shape, dim)


def hot(mask):
    return mask.astype(F32).astype(BF)


def mm(a, b, dims=((1,), (0,))):
    return lax.dot_general(a, b, (dims, ((), ())), preferred_element_type=F32)


def window(block, share):
    low = block * share // 128 * 128
    high = -(-(block + 1) * share // 128) * 128
    return low, high


def heads_kernel(
    groups, share, width,
    table, kept_ref, seg_ref, scales_ref, codes_hbm, w_hbm, cot_hbm,
    out_ref, grad_ref, gw_ref,
    codes, tall, scal, img_send, img_recv, w_all, cot_all, bal, qkv, scl, probs,
    out_acc, ctx_own, ctx_all, packed, nat, back_send, back_recv,
    load_s, cot_s, cot_r, fwd_s, fwd_r, img_s, img_r, ctx_s, ctx_r, back_s, back_r,
    wsib_s, wsib_r, wx_s, wx_r, wq_s, wq_r, wf_s, wf_r,
):
    pos = lax.axis_index("dp")
    me = lax.axis_index("fsdp")
    sib = me + 1 - 2 * (me % 2)
    cross = (me + 2) % 4
    diag = (sib + 2) % 4
    peer = (me, sib, cross, diag)
    quad = pos % 4
    rows = cot_hbm.shape[0]
    slot = img_send.shape[0] // 4
    feats = 3 * width
    model = cot_hbm.shape[1]
    head = width // HEADS
    factor = 1.0 / math.sqrt(head)

    def remote(src, dst, s, r, where):
        return pltpu.make_async_remote_copy(
            src_ref=src, dst_ref=dst, send_sem=s, recv_sem=r,
            device_id=where, device_id_type=pl.DeviceIdType.MESH,
        )

    def at_dp(index):
        return (index, me)

    def at_fsdp(index):
        return (pos, index)

    loads = [
        pltpu.make_async_copy(codes_hbm, codes, load_s.at[0]),
        pltpu.make_async_copy(w_hbm, w_all.at[0, pl.ds(0, share)], load_s.at[1]),
        pltpu.make_async_copy(cot_hbm, cot_all.at[0], load_s.at[2]),
    ]
    for load in loads:
        load.start()
    img_recv[...] = jnp.zeros_like(img_recv)
    back_recv[...] = jnp.zeros_like(back_recv)

    barrier = pltpu.get_barrier_semaphore()
    for r in (1, 2, 3):
        pl.semaphore_signal(barrier, inc=1, device_id=at_fsdp(peer[r]),
                            device_id_type=pl.DeviceIdType.MESH)
    valid_to = [(pos + o >= 0) & (pos + o < groups) for o in offsets]
    valid_from = [(pos - o >= 0) & (pos - o < groups) for o in offsets]
    for d in range(4):
        @pl.when(valid_to[d])
        def _(d=d):
            pl.semaphore_signal(barrier, inc=1, device_id=at_dp(pos + offsets[d]),
                                device_id_type=pl.DeviceIdType.MESH)
    far = pos + 3 - 2 * quad
    outer = (quad == 0) | (quad == 3)

    @pl.when(outer)
    def _():
        pl.semaphore_signal(barrier, inc=1, device_id=at_dp(far),
                            device_id_type=pl.DeviceIdType.MESH)
    pl.semaphore_wait(barrier, 3 + jnp.minimum(pos, 2) + jnp.minimum(groups - 1 - pos, 2)
                      + outer.astype(jnp.int32))

    tiles = model // 128
    cuts = [tiles * i // 4 * 128 for i in range(5)]

    split = share // 2 // 16 * 16
    bands = ((0, split), (split, share - split))
    pieces = [(i, c) for i in range(4) for c in range(2)]

    def columns(ref, i, c):
        return ref.at[pl.ds(*bands[c]), pl.ds(cuts[i], cuts[i + 1] - cuts[i])]

    w_sib = remote(w_hbm, w_all.at[1, pl.ds(0, share)], wsib_s, wsib_r, at_fsdp(sib))
    w_cross = {
        (i, c): remote(columns(w_hbm, i, c), columns(w_all.at[2], i, c),
                       wx_s.at[2 * i + c], wx_r.at[2 * i + c], at_fsdp(cross))
        for i, c in pieces
    }
    w_quad = {
        (i, c, p): remote(columns(w_all.at[2], i, c), columns(w_all.at[2], i, c),
                          wq_s.at[8 * i + 4 * c + p], wq_r.at[2 * i + c], at_dp(pos - quad + p))
        for i, c in pieces for p in range(4)
    }
    w_fwd = {
        (i, c): remote(columns(w_all.at[2], i, c), columns(w_all.at[3], i, c),
                       wf_s.at[2 * i + c], wf_r.at[2 * i + c], at_fsdp(sib))
        for i, c in pieces
    }
    for i in range(4):
        @pl.when(quad == i)
        def _(i=i):
            w_cross[i, 0].start()
            w_cross[i, 1].start()
    w_sib.start()

    hr = rows // 2
    cot_out = [
        remote(cot_hbm.at[pl.ds(c * hr, hr)], cot_all.at[2, pl.ds(c * hr, hr)],
               cot_s.at[c], cot_r.at[c], at_fsdp(cross))
        for c in range(2)
    ]
    cot_sib = remote(cot_hbm, cot_all.at[1], cot_s.at[2], cot_r.at[2], at_fsdp(sib))
    forward = [
        remote(cot_all.at[2, pl.ds(c * hr, hr)], cot_all.at[3, pl.ds(c * hr, hr)],
               fwd_s.at[c], fwd_r.at[c], at_fsdp(sib))
        for c in range(2)
    ]

    kept = kept_ref[0, 0]
    r64 = iota((4 * slot, rows), 0)
    c64 = iota((4 * slot, rows), 1)

    def selection(starts, lengths):
        mask = jnp.zeros((4 * slot, rows), F32)
        for d in range(4):
            step = r64 - d * slot
            ok = (step >= 0) & (step < lengths[d]) & (step < slot) & (c64 == starts[d] + step)
            mask = mask + ok.astype(F32)
        return mask.astype(BF)

    own_start = [table[0, d, pos] for d in range(4)]
    own_len = [table[1, d, pos] for d in range(4)]
    landing, arrived = [], []
    for d in range(4):
        src = jnp.clip(pos - offsets[d], 0, groups - 1)
        landing.append(table[2, d, src])
        arrived.append(jnp.where(valid_from[d], table[1, d, src], 0))
    tall[...] = jnp.zeros_like(tall)
    for m in range(3):
        tall[m * 8:m * 8 + scales_ref.shape[1]] = scales_ref[m].astype(F32)
    rr = iota((rows, rows), 0)
    cc = iota((rows, rows), 1)
    scal[...] = mm(hot(rr == cc), tall[...].astype(BF), ((1,), (1,))).astype(BF)
    loads[0].wait()
    chosen = selection(own_start, own_len)
    for m in range(3):
        img_send[:, m * width:(m + 1) * width] = mm(chosen, codes[m]).astype(BF)
    img_send[:, feats:] = mm(chosen, scal[...]).astype(BF)
    images = []
    for d in range(4):
        part = pl.ds(d * slot, slot)
        images.append(remote(img_send.at[part], img_recv.at[part], img_s.at[d], img_r.at[d],
                             at_dp(jnp.clip(pos + offsets[d], 0, groups - 1))))

        @pl.when(valid_to[d])
        def _(d=d):
            images[d].start()

    def hand_on(c):
        for i in range(4):
            @pl.when(quad == i)
            def _(i=i):
                w_cross[i, c].wait_recv()
                for step in (1, 2, 3):
                    w_quad[i, c, i ^ step].start()
                w_fwd[i, c].start()

    hand_on(0)

    loads[1].wait()
    loads[2].wait()
    for r in range(4):
        w_all[r, share:PAIR] = jnp.zeros((PAIR - share, model), BF)
    gc_own = mm(cot_all[0], w_all[0], ((1,), (1,))).astype(BF)

    keep = iota((rows, 1), 0) < kept
    lanes = iota((1, PAIR), 1)
    first = hot(lanes < head)
    second = hot(lanes >= head)
    picks = []
    spreads = [None] * 12
    for j in range(4):
        low, high = window(j, share)
        picks.append(hot((iota((high - low, PAIR), 0) + low
                          == iota((high - low, PAIR), 1) + j * share)
                         & (iota((high - low, PAIR), 1) < share)))
        block = jnp.where(lanes < share, (lanes + j * share) // 128, -128)
        for m in range(3):
            spreads[m * 4 + j] = hot(iota((128, PAIR), 0) == block + m * 8)

    def placing(starts, lengths):
        r_ = iota((rows, 4 * slot), 0)
        c_ = iota((rows, 4 * slot), 1)
        mask = jnp.zeros((rows, 4 * slot), F32)
        for d in range(4):
            step = c_ - d * slot
            ok = (step >= 0) & (step < lengths[d]) & (step < slot) & (r_ == starts[d] + step)
            mask = mask + ok.astype(F32)
        return mask.astype(BF)

    row_id = iota((1, rows), 1)
    marks = jnp.where(row_id < kept, seg_ref[...], -1)
    for d in range(4):
        here = (row_id >= landing[d]) & (row_id < landing[d] + arrived[d])
        marks = jnp.where(here, 100000 + d, marks)
    marks_row = jnp.broadcast_to(marks.astype(F32), (rows, rows))
    marks_col = jnp.sum(jnp.where(rr == cc, marks_row, 0.0), axis=1, keepdims=True)
    same = marks_col == marks_row
    bias = jnp.where(same, 0.0, -jnp.inf)
    bias2 = jnp.concatenate([bias, bias], axis=0)

    hand_on(1)
    for copy in cot_out + [cot_sib]:
        copy.start()

    for d in range(4):
        @pl.when(valid_from[d])
        def _(d=d):
            images[d].wait_recv()
    place = placing(landing, arrived)
    for m in range(3):
        part = slice(m * width, (m + 1) * width)
        bal[:, part] = jnp.where(keep, codes[m], mm(place, img_recv[:, part]).astype(BF))
    bal[:, feats:] = jnp.where(keep, scal[...], mm(place, img_recv[:, feats:]).astype(BF))

    for j in range(4):
        low, high = window(j, share)
        for m in range(3):
            values = mm(bal[:, m * width + low:m * width + high], picks[j])
            scale = mm(bal[:, feats:feats + 128], spreads[m * 4 + j])
            scl[m * 4 + j] = scale.astype(BF)
            qkv[m * 4 + j] = (values * scale).astype(BF)

    def stack(x):
        return jnp.concatenate([x * first, x * second], axis=0)

    def wide(x):
        return jnp.concatenate([x[:rows], x[rows:]], axis=1)

    w_sib.wait_recv()
    ctx_out = [None] * 4
    for r in range(4):
        j = peer[r]
        scores = mm(stack(qkv[j]), qkv[4 + j], ((1,), (1,))) * factor + bias2
        top = jnp.max(scores, axis=-1, keepdims=True)
        weights = jnp.exp(scores - top)
        p = weights / jnp.sum(weights, axis=-1, keepdims=True)
        probs[r] = p
        ctx = mm(wide(p.astype(BF)), stack(qkv[8 + j])).astype(BF)
        ctx_own[r] = ctx
        if r == 0:
            ctx_all[0] = ctx
        else:
            ctx_out[r] = remote(ctx_own.at[r], ctx_all.at[r], ctx_s.at[r], ctx_r.at[r],
                                at_fsdp(j))

    def backward(r, gc):
        j = peer[r]
        p = probs[r]
        gstack = stack(gc)
        gp = mm(gstack, qkv[8 + j], ((1,), (1,)))
        total = jnp.sum(p * gp, axis=-1, keepdims=True)
        gs = (p * (gp - total) * factor).astype(BF)
        gq = mm(wide(gs), stack(qkv[4 + j]))
        gk = mm(gs, stack(qkv[j]), ((0,), (0,)))
        gv = mm(p.astype(BF), gstack, ((0,), (0,)))
        for m, g in enumerate((gq, gk, gv)):
            packed[m * 4 + j] = (g * scl[m * 4 + j].astype(F32)).astype(BF)

    def gradient(r):
        return mm(cot_all[0], w_all[r], ((1,), (1,))).astype(BF)

    backward(0, gc_own)
    backward(1, gradient(1))
    for r in (1, 2, 3):
        ctx_out[r].start()

    def projected(r):
        return mm(jnp.concatenate([ctx_own[r], ctx_own[r + 1]], axis=1),
                  w_all[r:r + 2].reshape(2 * PAIR, model))

    def weight_terms(r):
        return mm(ctx_all[r:r + 2].reshape(2 * rows, PAIR),
                  cot_all[r:r + 2].reshape(2 * rows, model), ((0,), (0,)))[:share]

    out_acc[...] = projected(0)
    cot_sib.wait_recv()
    ctx_out[1].wait_recv()
    gw_ref[...] = weight_terms(0)
    for i, c in sorted(pieces, key=lambda piece: piece[1]):
        @pl.when(quad != i)
        def _(i=i, c=c):
            w_quad[i, c, i].wait_recv()
            w_fwd[i, c].start()
    for piece in pieces:
        w_fwd[piece].wait_recv()
    backward(2, gradient(2))
    backward(3, gradient(3))
    for m in range(3):
        blocks = [None] * (width // 128)
        for j in range(4):
            low, high = window(j, share)
            spread = hot((iota((PAIR, high - low), 1) + low
                          == iota((PAIR, high - low), 0) + j * share)
                         & (iota((PAIR, high - low), 0) < share))
            piece = mm(packed[m * 4 + j], spread)
            for b in range((high - low) // 128):
                add = piece[:, b * 128:(b + 1) * 128]
                at = low // 128 + b
                blocks[at] = add if blocks[at] is None else blocks[at] + add
        for b in range(width // 128):
            nat[:, m * width + b * 128:m * width + (b + 1) * 128] = blocks[b].astype(BF)

    back_send[...] = mm(selection(landing, arrived), nat[...]).astype(BF)
    returns = []
    for d in range(4):
        part = pl.ds(d * slot, slot)
        returns.append(remote(back_send.at[part], back_recv.at[part], back_s.at[d], back_r.at[d],
                              at_dp(jnp.clip(pos - offsets[d], 0, groups - 1))))

        @pl.when(valid_from[d])
        def _(d=d):
            returns[d].start()

    out_ref[...] = (out_acc[...] + projected(2)).astype(BF)

    for c in range(2):
        cot_out[c].wait_recv()
        forward[c].start()
    for r in (2, 3):
        ctx_out[r].wait_recv()
    for c in range(2):
        forward[c].wait_recv()
    gw_ref[...] += weight_terms(2)

    for d in range(4):
        @pl.when(valid_to[d])
        def _(d=d):
            returns[d].wait_recv()
    place = placing(own_start, own_len)
    for m in range(3):
        part = slice(m * width, (m + 1) * width)
        grad_ref[m] = jnp.where(keep, nat[:, part], mm(place, back_recv[:, part]).astype(BF))

    for copy in cot_out + [cot_sib, w_sib] + forward + list(w_fwd.values()) + ctx_out[1:]:
        copy.wait_send()
    for i in range(4):
        @pl.when(quad == i)
        def _(i=i):
            for c in range(2):
                w_cross[i, c].wait_send()
                for p in range(4):
                    if p != i:
                        w_quad[i, c, p].wait_send()
    for d in range(4):
        @pl.when(valid_to[d])
        def _(d=d):
            images[d].wait_send()

        @pl.when(valid_from[d])
        def _(d=d):
            returns[d].wait_send()


def write_out(a, b, c, a_out, b_out, c_out, sems):
    copies = [
        pltpu.make_async_copy(src, dst, sems.at[i])
        for i, (src, dst) in enumerate(((a, a_out), (b, b_out), (c, c_out)))
    ]
    for copy in copies:
        copy.start()
    for copy in copies:
        copy.wait()


def local_by_heads(qkv_codes, block_scales, home_segments, kept_rows, pack_list, w_out, cotangent):
    groups = lax.axis_size("dp")
    rows = qkv_codes.shape[2]
    width = qkv_codes.shape[4]
    model = w_out.shape[1]
    share = w_out.shape[0]
    slot = rows // 8
    feats = 3 * width
    vmem = pl.BlockSpec(memory_space=pltpu.VMEM)
    hbm = pl.BlockSpec(memory_space=pltpu.HBM)
    smem = pl.BlockSpec(memory_space=pltpu.SMEM)
    dma = pltpu.SemaphoreType.DMA
    out, grads, gw = pl.pallas_call(
        functools.partial(heads_kernel, groups, share, width),
        out_shape=(
            pltpu.VMEM((rows, model), BF),
            pltpu.VMEM((3, rows, width), BF),
            pltpu.VMEM((share, model), F32),
        ),
        in_specs=[smem, smem, vmem, vmem, hbm, hbm, hbm],
        out_specs=(vmem, vmem, vmem),
        scratch_shapes=[
            pltpu.VMEM((3, rows, width), BF),
            pltpu.VMEM((128, rows), F32),
            pltpu.VMEM((rows, 128), BF),
            pltpu.VMEM((4 * slot, feats + 128), BF),
            pltpu.VMEM((4 * slot, feats + 128), BF),
            pltpu.VMEM((4, PAIR, model), BF),
            pltpu.VMEM((4, rows, model), BF),
            pltpu.VMEM((rows, feats + 128), BF),
            pltpu.VMEM((12, rows, PAIR), BF),
            pltpu.VMEM((12, rows, PAIR), BF),
            pltpu.VMEM((4, 2 * rows, rows), F32),
            pltpu.VMEM((rows, model), F32),
            pltpu.VMEM((4, rows, PAIR), BF),
            pltpu.VMEM((4, rows, PAIR), BF),
            pltpu.VMEM((12, rows, PAIR), BF),
            pltpu.VMEM((rows, feats), BF),
            pltpu.VMEM((4 * slot, feats), BF),
            pltpu.VMEM((4 * slot, feats), BF),
            dma((3,)), dma((3,)), dma((3,)), dma((2,)), dma((2,)), dma((4,)), dma((4,)),
            dma((4,)), dma((4,)), dma((4,)), dma((4,)),
            dma, dma, dma((8,)), dma((8,)), dma((32,)), dma((8,)), dma((8,)), dma((8,)),
        ],
        compiler_params=pltpu.CompilerParams(
            collective_id=0, has_side_effects=True, vmem_limit_bytes=58 * 1024 * 1024
        ),
        cost_estimate=pl.CostEstimate(
            flops=8 * rows * width * model, bytes_accessed=8 * 1024 * 1024, transcendentals=0
        ),
        name="attention_by_heads",
    )(
        jnp.transpose(pack_list[:, 0], (2, 1, 0)),
        kept_rows,
        home_segments[0],
        jnp.transpose(block_scales[0, 0], (1, 2, 0)),
        jnp.transpose(qkv_codes[0, 0], (1, 0, 2)),
        w_out,
        cotangent[0, 0],
    )
    results = (out, grads, gw)
    out, grads, gw = pl.pallas_call(
        write_out,
        out_shape=tuple(jax.ShapeDtypeStruct(a.shape, a.dtype) for a in results),
        in_specs=[vmem] * 3,
        out_specs=(hbm,) * 3,
        scratch_shapes=[dma((3,))],
        compiler_params=pltpu.CompilerParams(vmem_limit_bytes=4 * 1024 * 1024),
        name="write_out",
    )(*results)
    return (out[None, None], jnp.transpose(grads, (1, 0, 2))[None, None], gw[None])


def solution(mesh):
    fast = mesh.shape["fsdp"] == 4 and mesh.shape["dp"] % 4 == 0
    return jax.shard_map(
        local_by_heads if fast else local,
        mesh=mesh,
        in_specs=(
            P("dp", "fsdp", None, None, None),
            P("dp", "fsdp", None, None, None),
            P("dp", "fsdp", None),
            P("dp", "fsdp"),
            P(None, "fsdp", None, None),
            P("fsdp", None),
            P("dp", "fsdp", None, None),
        ),
        out_specs=(
            P("dp", "fsdp", None, None),
            P("dp", "fsdp", None, None, None),
            P("dp", "fsdp", None),
        ),
        check_vma=False,
    )
```

```python
import functools
import math

import jax
import jax.numpy as jnp
from jax import lax
from jax.experimental import pallas as pl
from jax.experimental.pallas import tpu as pltpu
from jax.sharding import PartitionSpec as P

HEADS = 8


offsets = (1, -1, 2, -2)


def shifted(block, axis, distance):
    devices = range(lax.axis_size(axis))
    route = [(i - distance, i) for i in devices if i - distance in devices]
    return lax.ppermute(block, axis, route)


def dequantize(codes, scales):
    count = codes.shape[0]
    blocks = scales.shape[-1]
    scaled = (
        codes.astype(jnp.float32).reshape(count, 3, blocks, -1)
        * scales.astype(jnp.float32)[..., None]
    )
    return scaled.reshape(count, 3, -1).astype(jnp.bfloat16)


def local_layer(codes, scales, labels, w_full, grad_out):
    count = codes.shape[0]
    width = w_full.shape[0]
    head_size = width // HEADS
    factor = 1.0 / math.sqrt(head_size)
    values = dequantize(codes, scales)
    query = values[:, 0].reshape(count, HEADS, head_size)
    keys = values[:, 1].reshape(count, HEADS, head_size)
    value_rows = values[:, 2].reshape(count, HEADS, head_size)
    scores = jnp.einsum("qhd,khd->hqk", query, keys, preferred_element_type=jnp.float32) * factor
    same = labels[:, None] == labels[None, :]
    scores = jnp.where(same[None], scores, -jnp.inf)
    top = jnp.max(scores, axis=-1, keepdims=True)
    weights = jnp.exp(scores - top)
    probs = weights / jnp.sum(weights, axis=-1, keepdims=True)
    probs_b = probs.astype(jnp.bfloat16)
    context = jnp.einsum("hqk,khd->qhd", probs_b, value_rows, preferred_element_type=jnp.float32)
    context = context.reshape(count, width).astype(jnp.bfloat16)
    output = jnp.dot(context, w_full, preferred_element_type=jnp.float32).astype(jnp.bfloat16)
    grad_context = lax.dot_general(
        grad_out, w_full, (((1,), (1,)), ((), ())), preferred_element_type=jnp.float32
    )
    grad_context = grad_context.astype(jnp.bfloat16).reshape(count, HEADS, head_size)
    grad_probs = jnp.einsum(
        "qhd,khd->hqk", grad_context, value_rows, preferred_element_type=jnp.float32
    )
    total = jnp.sum(probs * grad_probs, axis=-1, keepdims=True)
    grad_scores = (probs * (grad_probs - total) * factor).astype(jnp.bfloat16)
    grad_query = jnp.einsum("hqk,khd->qhd", grad_scores, keys, preferred_element_type=jnp.float32)
    grad_keys = jnp.einsum("hqk,qhd->khd", grad_scores, query, preferred_element_type=jnp.float32)
    grad_values = jnp.einsum(
        "hqk,qhd->khd", probs_b, grad_context, preferred_element_type=jnp.float32
    )
    grads = jnp.stack([grad_query, grad_keys, grad_values], axis=1).reshape(count, 3, -1)
    blocks = scales.shape[-1]
    grads = (grads.reshape(count, 3, blocks, -1) * scales.astype(jnp.float32)[..., None]).reshape(
        count, 3, -1
    )
    return (output, grads.astype(jnp.bfloat16), context)


def pad_rows(array, extra_rows, fill):
    extra = jnp.full((extra_rows,) + array.shape[1:], fill, array.dtype)
    return jnp.concatenate([array, extra], axis=0)


def cut_rows(buffer, at_row, length, slot):
    piece = lax.dynamic_slice_in_dim(buffer, at_row, slot, 0)
    present = (jnp.arange(slot) < length).reshape((slot,) + (1,) * (buffer.ndim - 1))
    return jnp.where(present, piece, jnp.zeros_like(piece))


def put_rows(buffer, piece, at_row, length):
    slot = piece.shape[0]
    old = lax.dynamic_slice_in_dim(buffer, at_row, slot, 0)
    present = (jnp.arange(slot) < length).reshape((slot,) + (1,) * (buffer.ndim - 1))
    return lax.dynamic_update_slice_in_dim(buffer, jnp.where(present, piece, old), at_row, 0)


def local(qkv_codes, block_scales, home_segments, kept_rows, pack_list, w_out, cotangent):
    position = lax.axis_index("dp")
    group_size = lax.axis_size("dp")
    codes = qkv_codes[0, 0]
    scales = block_scales[0, 0]
    segments = home_segments[0, 0]
    kept = kept_rows[0, 0]
    table = pack_list[:, 0]
    grad_out = cotangent[0, 0]
    row_count = codes.shape[0]
    slot = row_count // 8
    w_full = lax.all_gather(w_out, "fsdp", axis=0, tiled=True)
    inside = jnp.arange(row_count) < kept
    own_entries = lax.dynamic_index_in_dim(table, position, 0, keepdims=False)
    home_codes = pad_rows(codes, slot, 0)
    home_scales = pad_rows(scales, slot, 0)
    sent_codes = [
        cut_rows(home_codes, own_entries[route, 0], own_entries[route, 1], slot)
        for route in range(4)
    ]
    sent_scales = [
        cut_rows(home_scales, own_entries[route, 0], own_entries[route, 1], slot)
        for route in range(4)
    ]
    received = [
        shifted((sent_codes[route], sent_scales[route]), "dp", offsets[route]) for route in range(4)
    ]
    landing = []
    arrived = []
    for route in range(4):
        source = position - offsets[route]
        allowed = (source >= 0) & (source < group_size)
        entries = lax.dynamic_index_in_dim(
            table, jnp.clip(source, 0, group_size - 1), 0, keepdims=False
        )
        arrived.append(jnp.where(allowed, entries[route, 1], 0))
        landing.append(entries[route, 2])
    bal_codes = pad_rows(jnp.where(inside[:, None, None], codes, jnp.zeros_like(codes)), slot, 0)
    bal_scales = pad_rows(jnp.where(inside[:, None, None], scales, jnp.zeros_like(scales)), slot, 0)
    labels = pad_rows(jnp.where(inside, segments, -1), slot, -1)
    for route in range(4):
        bal_codes = put_rows(bal_codes, received[route][0], landing[route], arrived[route])
        bal_scales = put_rows(bal_scales, received[route][1], landing[route], arrived[route])
        marks = jnp.full((slot,), 100000 + route, jnp.int32)
        labels = put_rows(labels, marks, landing[route], arrived[route])
    output, grads, context = local_layer(
        bal_codes[:row_count], bal_scales[:row_count], labels[:row_count], w_full, grad_out
    )
    grads_padded = pad_rows(grads, slot, 0)
    going_back = [
        cut_rows(grads_padded, landing[route], arrived[route], slot) for route in range(4)
    ]
    returned = [shifted(going_back[route], "dp", -offsets[route]) for route in range(4)]
    home_grads = pad_rows(jnp.where(inside[:, None, None], grads, jnp.zeros_like(grads)), slot, 0)
    for route in range(4):
        home_grads = put_rows(
            home_grads, returned[route], own_entries[route, 0], own_entries[route, 1]
        )
    grad_codes = home_grads[:row_count]
    term = lax.dot_general(
        context, grad_out, (((0,), (0,)), ((), ())), preferred_element_type=jnp.float32
    )
    grad_w = lax.psum_scatter(
        term.astype(jnp.bfloat16), "fsdp", scatter_dimension=0, tiled=True
    ).astype(jnp.float32)
    return (output[None, None], grad_codes[None, None], grad_w[None])


BF = jnp.bfloat16
F32 = jnp.float32
PAIR = 256


def iota(shape, dim):
    return lax.broadcasted_iota(jnp.int32, shape, dim)


def hot(mask):
    return mask.astype(F32).astype(BF)


def mm(a, b, dims=((1,), (0,))):
    return lax.dot_general(a, b, (dims, ((), ())), preferred_element_type=F32)


def window(block, share):
    low = block * share // 128 * 128
    high = -(-(block + 1) * share // 128) * 128
    return low, high


def heads_kernel(
    groups, share, width,
    table, kept_ref, seg_ref, scales_ref, codes_hbm, w_hbm, cot_hbm,
    out_ref, grad_ref, gw_ref,
    codes, tall, scal, img_send, img_recv, w_all, cot_all, bal, qkv, scl, probs,
    out_acc, ctx_own, ctx_all, packed, back_send, back_recv,
    load_s, cot_s, cot_r, fwd_s, fwd_r, img_s, img_r, ctx_s, ctx_r, back_s, back_r,
    wsib_s, wsib_r, wx_s, wx_r, wq_s, wq_r, wf_s, wf_r,
):
    pos = lax.axis_index("dp")
    me = lax.axis_index("fsdp")
    sib = me + 1 - 2 * (me % 2)
    cross = (me + 2) % 4
    diag = (sib + 2) % 4
    peer = (me, sib, cross, diag)
    quad = pos % 4
    rows = cot_hbm.shape[0]
    slot = img_send.shape[0] // 4
    feats = 3 * width
    model = cot_hbm.shape[1]
    head = width // HEADS
    factor = 1.0 / math.sqrt(head)

    def remote(src, dst, s, r, where):
        return pltpu.make_async_remote_copy(
            src_ref=src, dst_ref=dst, send_sem=s, recv_sem=r,
            device_id=where, device_id_type=pl.DeviceIdType.MESH,
        )

    def at_dp(index):
        return (index, me)

    def at_fsdp(index):
        return (pos, index)

    loads = [
        pltpu.make_async_copy(codes_hbm, codes, load_s.at[0]),
        pltpu.make_async_copy(w_hbm, w_all.at[0, pl.ds(0, share)], load_s.at[1]),
        pltpu.make_async_copy(cot_hbm, cot_all.at[0], load_s.at[2]),
    ]
    for load in loads:
        load.start()
    img_recv[...] = jnp.zeros_like(img_recv)
    back_recv[...] = jnp.zeros_like(back_recv)

    barrier = pltpu.get_barrier_semaphore()
    for r in (1, 2, 3):
        pl.semaphore_signal(barrier, inc=1, device_id=at_fsdp(peer[r]),
                            device_id_type=pl.DeviceIdType.MESH)
    valid_to = [(pos + o >= 0) & (pos + o < groups) for o in offsets]
    valid_from = [(pos - o >= 0) & (pos - o < groups) for o in offsets]
    for d in range(4):
        @pl.when(valid_to[d])
        def _(d=d):
            pl.semaphore_signal(barrier, inc=1, device_id=at_dp(pos + offsets[d]),
                                device_id_type=pl.DeviceIdType.MESH)
    far = pos + 3 - 2 * quad
    outer = (quad == 0) | (quad == 3)

    @pl.when(outer)
    def _():
        pl.semaphore_signal(barrier, inc=1, device_id=at_dp(far),
                            device_id_type=pl.DeviceIdType.MESH)
    pl.semaphore_wait(barrier, 3 + jnp.minimum(pos, 2) + jnp.minimum(groups - 1 - pos, 2)
                      + outer.astype(jnp.int32))

    tiles = model // 128
    cuts = [tiles * i // 4 * 128 for i in range(5)]

    split = share // 2 // 16 * 16
    bands = ((0, split), (split, share - split))
    pieces = [(i, c) for i in range(4) for c in range(2)]

    def columns(ref, i, c):
        return ref.at[pl.ds(*bands[c]), pl.ds(cuts[i], cuts[i + 1] - cuts[i])]

    w_sib = remote(w_hbm, w_all.at[1, pl.ds(0, share)], wsib_s, wsib_r, at_fsdp(sib))
    w_cross = {
        (i, c): remote(columns(w_hbm, i, c), columns(w_all.at[2], i, c),
                       wx_s.at[2 * i + c], wx_r.at[2 * i + c], at_fsdp(cross))
        for i, c in pieces
    }
    w_quad = {
        (i, c, p): remote(columns(w_all.at[2], i, c), columns(w_all.at[2], i, c),
                          wq_s.at[8 * i + 4 * c + p], wq_r.at[2 * i + c], at_dp(pos - quad + p))
        for i, c in pieces for p in range(4)
    }
    w_fwd = {
        (i, c): remote(columns(w_all.at[2], i, c), columns(w_all.at[3], i, c),
                       wf_s.at[2 * i + c], wf_r.at[2 * i + c], at_fsdp(sib))
        for i, c in pieces
    }
    for i in range(4):
        @pl.when(quad == i)
        def _(i=i):
            w_cross[i, 0].start()
            w_cross[i, 1].start()
    w_sib.start()

    hr = rows // 2
    cot_out = [
        remote(cot_hbm.at[pl.ds(c * hr, hr)], cot_all.at[2, pl.ds(c * hr, hr)],
               cot_s.at[c], cot_r.at[c], at_fsdp(cross))
        for c in range(2)
    ]
    cot_sib = remote(cot_hbm, cot_all.at[1], cot_s.at[2], cot_r.at[2], at_fsdp(sib))
    forward = [
        remote(cot_all.at[2, pl.ds(c * hr, hr)], cot_all.at[3, pl.ds(c * hr, hr)],
               fwd_s.at[c], fwd_r.at[c], at_fsdp(sib))
        for c in range(2)
    ]

    kept = kept_ref[0, 0]
    r64 = iota((4 * slot, rows), 0)
    c64 = iota((4 * slot, rows), 1)

    def selection(starts, lengths):
        mask = jnp.zeros((4 * slot, rows), F32)
        for d in range(4):
            step = r64 - d * slot
            ok = (step >= 0) & (step < lengths[d]) & (step < slot) & (c64 == starts[d] + step)
            mask = mask + ok.astype(F32)
        return mask.astype(BF)

    own_start = [table[0, d, pos] for d in range(4)]
    own_len = [table[1, d, pos] for d in range(4)]
    landing, arrived = [], []
    for d in range(4):
        src = jnp.clip(pos - offsets[d], 0, groups - 1)
        landing.append(table[2, d, src])
        arrived.append(jnp.where(valid_from[d], table[1, d, src], 0))
    tall[...] = jnp.zeros_like(tall)
    for m in range(3):
        tall[m * 8:m * 8 + scales_ref.shape[1]] = scales_ref[m].astype(F32)
    rr = iota((rows, rows), 0)
    cc = iota((rows, rows), 1)
    scal[...] = mm(hot(rr == cc), tall[...].astype(BF), ((1,), (1,))).astype(BF)
    loads[0].wait()
    chosen = selection(own_start, own_len)
    for m in range(3):
        img_send[:, m * width:(m + 1) * width] = mm(chosen, codes[m]).astype(BF)
    img_send[:, feats:] = mm(chosen, scal[...]).astype(BF)
    images = []
    for d in range(4):
        part = pl.ds(d * slot, slot)
        images.append(remote(img_send.at[part], img_recv.at[part], img_s.at[d], img_r.at[d],
                             at_dp(jnp.clip(pos + offsets[d], 0, groups - 1))))

        @pl.when(valid_to[d])
        def _(d=d):
            images[d].start()

    def hand_on(c):
        for i in range(4):
            @pl.when(quad == i)
            def _(i=i):
                w_cross[i, c].wait_recv()
                for step in (1, 2, 3):
                    w_quad[i, c, i ^ step].start()
                w_fwd[i, c].start()

    hand_on(0)

    loads[1].wait()
    loads[2].wait()
    for r in range(4):
        w_all[r, share:PAIR] = jnp.zeros((PAIR - share, model), BF)
    gc_own = mm(cot_all[0], w_all[0], ((1,), (1,))).astype(BF)

    keep = iota((rows, 1), 0) < kept
    lanes = iota((1, PAIR), 1)
    first = hot(lanes < head)
    second = hot(lanes >= head)
    picks = []
    spreads = [None] * 12
    for j in range(4):
        low, high = window(j, share)
        picks.append(hot((iota((high - low, PAIR), 0) + low
                          == iota((high - low, PAIR), 1) + j * share)
                         & (iota((high - low, PAIR), 1) < share)))
        block = jnp.where(lanes < share, (lanes + j * share) // 128, -128)
        for m in range(3):
            spreads[m * 4 + j] = hot(iota((128, PAIR), 0) == block + m * 8)

    def placing(starts, lengths):
        r_ = iota((rows, 4 * slot), 0)
        c_ = iota((rows, 4 * slot), 1)
        mask = jnp.zeros((rows, 4 * slot), F32)
        for d in range(4):
            step = c_ - d * slot
            ok = (step >= 0) & (step < lengths[d]) & (step < slot) & (r_ == starts[d] + step)
            mask = mask + ok.astype(F32)
        return mask.astype(BF)

    row_id = iota((1, rows), 1)
    marks = jnp.where(row_id < kept, seg_ref[...], -1)
    for d in range(4):
        here = (row_id >= landing[d]) & (row_id < landing[d] + arrived[d])
        marks = jnp.where(here, 100000 + d, marks)
    marks_row = jnp.broadcast_to(marks.astype(F32), (rows, rows))
    marks_col = jnp.sum(jnp.where(rr == cc, marks_row, 0.0), axis=1, keepdims=True)
    same = marks_col == marks_row
    bias = jnp.where(same, 0.0, -jnp.inf)
    bias2 = jnp.concatenate([bias, bias], axis=0)

    hand_on(1)
    for copy in cot_out + [cot_sib]:
        copy.start()

    for d in range(4):
        @pl.when(valid_from[d])
        def _(d=d):
            images[d].wait_recv()
    place = placing(landing, arrived)
    for m in range(3):
        part = slice(m * width, (m + 1) * width)
        bal[:, part] = jnp.where(keep, codes[m], mm(place, img_recv[:, part]).astype(BF))
    bal[:, feats:] = jnp.where(keep, scal[...], mm(place, img_recv[:, feats:]).astype(BF))

    for j in range(4):
        low, high = window(j, share)
        for m in range(3):
            values = mm(bal[:, m * width + low:m * width + high], picks[j])
            scale = mm(bal[:, feats:feats + 128], spreads[m * 4 + j])
            scl[m * 4 + j] = scale.astype(BF)
            qkv[m * 4 + j] = (values * scale).astype(BF)

    def stack(x):
        return jnp.concatenate([x * first, x * second], axis=0)

    def wide(x):
        return jnp.concatenate([x[:rows], x[rows:]], axis=1)

    w_sib.wait_recv()
    ctx_out = [None] * 4
    for r in range(4):
        j = peer[r]
        scores = mm(stack(qkv[j]), qkv[4 + j], ((1,), (1,))) * factor + bias2
        top = jnp.max(scores, axis=-1, keepdims=True)
        weights = jnp.exp(scores - top)
        p = weights / jnp.sum(weights, axis=-1, keepdims=True)
        probs[r] = p
        ctx = mm(wide(p.astype(BF)), stack(qkv[8 + j])).astype(BF)
        ctx_own[r] = ctx
        if r == 0:
            ctx_all[0] = ctx
        else:
            ctx_out[r] = remote(ctx_own.at[r], ctx_all.at[r], ctx_s.at[r], ctx_r.at[r],
                                at_fsdp(j))

    def backward(r, gc):
        j = peer[r]
        p = probs[r]
        gstack = stack(gc)
        gp = mm(gstack, qkv[8 + j], ((1,), (1,)))
        total = jnp.sum(p * gp, axis=-1, keepdims=True)
        gs = (p * (gp - total) * factor).astype(BF)
        gq = mm(wide(gs), stack(qkv[4 + j]))
        gk = mm(gs, stack(qkv[j]), ((0,), (0,)))
        gv = mm(p.astype(BF), gstack, ((0,), (0,)))
        for m, g in enumerate((gq, gk, gv)):
            packed[m * 4 + j] = (g * scl[m * 4 + j].astype(F32)).astype(BF)

    def gradient(r):
        return mm(cot_all[0], w_all[r], ((1,), (1,))).astype(BF)

    going = selection(landing, arrived)
    returns = {
        (h, d): remote(back_send.at[h, pl.ds(d * slot, slot)],
                       back_recv.at[h, pl.ds(d * slot, slot)],
                       back_s.at[4 * h + d], back_r.at[4 * h + d],
                       at_dp(jnp.clip(pos - offsets[d], 0, groups - 1)))
        for h in range(2) for d in range(4)
    }
    parts = [(m, k, slice((2 * m + k) * PAIR, (2 * m + k + 1) * PAIR))
             for m in range(3) for k in range(2)]

    def send_back(h):
        for m, k, cols in parts:
            back_send[h, :, cols] = mm(going, packed[m * 4 + peer[2 * h + k]]).astype(BF)
        for d in range(4):
            @pl.when(valid_from[d])
            def _(d=d):
                returns[h, d].start()

    def bring_home(h):
        for d in range(4):
            @pl.when(valid_to[d])
            def _(d=d):
                returns[h, d].wait_recv()
        for m, k, cols in parts:
            at = m * 4 + peer[2 * h + k]
            placed = mm(home, back_recv[h, :, cols]).astype(BF)
            packed[at] = jnp.where(keep, packed[at], placed)

    backward(0, gc_own)
    backward(1, gradient(1))
    for r in (1, 2, 3):
        ctx_out[r].start()
    send_back(0)

    def projected(r):
        return mm(jnp.concatenate([ctx_own[r], ctx_own[r + 1]], axis=1),
                  w_all[r:r + 2].reshape(2 * PAIR, model))

    def weight_terms(r):
        return mm(ctx_all[r:r + 2].reshape(2 * rows, PAIR),
                  cot_all[r:r + 2].reshape(2 * rows, model), ((0,), (0,)))[:share]

    out_acc[...] = projected(0)
    cot_sib.wait_recv()
    ctx_out[1].wait_recv()
    gw_ref[...] = weight_terms(0)
    for i, c in sorted(pieces, key=lambda piece: piece[1]):
        @pl.when(quad != i)
        def _(i=i, c=c):
            w_quad[i, c, i].wait_recv()
            w_fwd[i, c].start()
    for piece in pieces:
        w_fwd[piece].wait_recv()
    backward(2, gradient(2))
    backward(3, gradient(3))
    send_back(1)

    out_ref[...] = (out_acc[...] + projected(2)).astype(BF)

    home = placing(own_start, own_len)
    bring_home(0)

    for c in range(2):
        cot_out[c].wait_recv()
        forward[c].start()
    for r in (2, 3):
        ctx_out[r].wait_recv()
    for c in range(2):
        forward[c].wait_recv()
    gw_ref[...] += weight_terms(2)

    bring_home(1)
    for m in range(3):
        blocks = [None] * (width // 128)
        for j in range(4):
            low, high = window(j, share)
            spread = hot((iota((PAIR, high - low), 1) + low
                          == iota((PAIR, high - low), 0) + j * share)
                         & (iota((PAIR, high - low), 0) < share))
            piece = mm(packed[m * 4 + j], spread)
            for b in range((high - low) // 128):
                add = piece[:, b * 128:(b + 1) * 128]
                at = low // 128 + b
                blocks[at] = add if blocks[at] is None else blocks[at] + add
        for b in range(width // 128):
            grad_ref[m, :, b * 128:(b + 1) * 128] = blocks[b].astype(BF)

    for copy in cot_out + [cot_sib, w_sib] + forward + list(w_fwd.values()) + ctx_out[1:]:
        copy.wait_send()
    for i in range(4):
        @pl.when(quad == i)
        def _(i=i):
            for c in range(2):
                w_cross[i, c].wait_send()
                for p in range(4):
                    if p != i:
                        w_quad[i, c, p].wait_send()
    for d in range(4):
        @pl.when(valid_to[d])
        def _(d=d):
            images[d].wait_send()

        @pl.when(valid_from[d])
        def _(d=d):
            returns[0, d].wait_send()
            returns[1, d].wait_send()


def write_out(a, b, c, a_out, b_out, c_out, sems):
    copies = [
        pltpu.make_async_copy(src, dst, sems.at[i])
        for i, (src, dst) in enumerate(((a, a_out), (b, b_out), (c, c_out)))
    ]
    for copy in copies:
        copy.start()
    for copy in copies:
        copy.wait()


def local_by_heads(qkv_codes, block_scales, home_segments, kept_rows, pack_list, w_out, cotangent):
    groups = lax.axis_size("dp")
    rows = qkv_codes.shape[2]
    width = qkv_codes.shape[4]
    model = w_out.shape[1]
    share = w_out.shape[0]
    slot = rows // 8
    feats = 3 * width
    vmem = pl.BlockSpec(memory_space=pltpu.VMEM)
    hbm = pl.BlockSpec(memory_space=pltpu.HBM)
    smem = pl.BlockSpec(memory_space=pltpu.SMEM)
    dma = pltpu.SemaphoreType.DMA
    out, grads, gw = pl.pallas_call(
        functools.partial(heads_kernel, groups, share, width),
        out_shape=(
            pltpu.VMEM((rows, model), BF),
            pltpu.VMEM((3, rows, width), BF),
            pltpu.VMEM((share, model), F32),
        ),
        in_specs=[smem, smem, vmem, vmem, hbm, hbm, hbm],
        out_specs=(vmem, vmem, vmem),
        scratch_shapes=[
            pltpu.VMEM((3, rows, width), BF),
            pltpu.VMEM((128, rows), F32),
            pltpu.VMEM((rows, 128), BF),
            pltpu.VMEM((4 * slot, feats + 128), BF),
            pltpu.VMEM((4 * slot, feats + 128), BF),
            pltpu.VMEM((4, PAIR, model), BF),
            pltpu.VMEM((4, rows, model), BF),
            pltpu.VMEM((rows, feats + 128), BF),
            pltpu.VMEM((12, rows, PAIR), BF),
            pltpu.VMEM((12, rows, PAIR), BF),
            pltpu.VMEM((4, 2 * rows, rows), F32),
            pltpu.VMEM((rows, model), F32),
            pltpu.VMEM((4, rows, PAIR), BF),
            pltpu.VMEM((4, rows, PAIR), BF),
            pltpu.VMEM((12, rows, PAIR), BF),
            pltpu.VMEM((2, 4 * slot, 6 * PAIR), BF),
            pltpu.VMEM((2, 4 * slot, 6 * PAIR), BF),
            dma((3,)), dma((3,)), dma((3,)), dma((2,)), dma((2,)), dma((4,)), dma((4,)),
            dma((4,)), dma((4,)), dma((8,)), dma((8,)),
            dma, dma, dma((8,)), dma((8,)), dma((32,)), dma((8,)), dma((8,)), dma((8,)),
        ],
        compiler_params=pltpu.CompilerParams(
            collective_id=0, has_side_effects=True, vmem_limit_bytes=58 * 1024 * 1024
        ),
        cost_estimate=pl.CostEstimate(
            flops=8 * rows * width * model, bytes_accessed=8 * 1024 * 1024, transcendentals=0
        ),
        name="attention_by_heads",
    )(
        jnp.transpose(pack_list[:, 0], (2, 1, 0)),
        kept_rows,
        home_segments[0],
        jnp.transpose(block_scales[0, 0], (1, 2, 0)),
        jnp.transpose(qkv_codes[0, 0], (1, 0, 2)),
        w_out,
        cotangent[0, 0],
    )
    results = (out, grads, gw)
    out, grads, gw = pl.pallas_call(
        write_out,
        out_shape=tuple(jax.ShapeDtypeStruct(a.shape, a.dtype) for a in results),
        in_specs=[vmem] * 3,
        out_specs=(hbm,) * 3,
        scratch_shapes=[dma((3,))],
        compiler_params=pltpu.CompilerParams(vmem_limit_bytes=4 * 1024 * 1024),
        name="write_out",
    )(*results)
    return (out[None, None], jnp.transpose(grads, (1, 0, 2))[None, None], gw[None])


def solution(mesh):
    fast = mesh.shape["fsdp"] == 4 and mesh.shape["dp"] % 4 == 0
    return jax.shard_map(
        local_by_heads if fast else local,
        mesh=mesh,
        in_specs=(
            P("dp", "fsdp", None, None, None),
            P("dp", "fsdp", None, None, None),
            P("dp", "fsdp", None),
            P("dp", "fsdp"),
            P(None, "fsdp", None, None),
            P("fsdp", None),
            P("dp", "fsdp", None, None),
        ),
        out_specs=(
            P("dp", "fsdp", None, None),
            P("dp", "fsdp", None, None, None),
            P("dp", "fsdp", None),
        ),
        check_vma=False,
    )
```

```python
import functools
import math

import jax
import jax.numpy as jnp
from jax import lax
from jax.experimental import pallas as pl
from jax.experimental.pallas import tpu as pltpu
from jax.sharding import PartitionSpec as P

HEADS = 8


offsets = (1, -1, 2, -2)


def shifted(block, axis, distance):
    devices = range(lax.axis_size(axis))
    route = [(i - distance, i) for i in devices if i - distance in devices]
    return lax.ppermute(block, axis, route)


def dequantize(codes, scales):
    count = codes.shape[0]
    blocks = scales.shape[-1]
    scaled = (
        codes.astype(jnp.float32).reshape(count, 3, blocks, -1)
        * scales.astype(jnp.float32)[..., None]
    )
    return scaled.reshape(count, 3, -1).astype(jnp.bfloat16)


def local_layer(codes, scales, labels, w_full, grad_out):
    count = codes.shape[0]
    width = w_full.shape[0]
    head_size = width // HEADS
    factor = 1.0 / math.sqrt(head_size)
    values = dequantize(codes, scales)
    query = values[:, 0].reshape(count, HEADS, head_size)
    keys = values[:, 1].reshape(count, HEADS, head_size)
    value_rows = values[:, 2].reshape(count, HEADS, head_size)
    scores = jnp.einsum("qhd,khd->hqk", query, keys, preferred_element_type=jnp.float32) * factor
    same = labels[:, None] == labels[None, :]
    scores = jnp.where(same[None], scores, -jnp.inf)
    top = jnp.max(scores, axis=-1, keepdims=True)
    weights = jnp.exp(scores - top)
    probs = weights / jnp.sum(weights, axis=-1, keepdims=True)
    probs_b = probs.astype(jnp.bfloat16)
    context = jnp.einsum("hqk,khd->qhd", probs_b, value_rows, preferred_element_type=jnp.float32)
    context = context.reshape(count, width).astype(jnp.bfloat16)
    output = jnp.dot(context, w_full, preferred_element_type=jnp.float32).astype(jnp.bfloat16)
    grad_context = lax.dot_general(
        grad_out, w_full, (((1,), (1,)), ((), ())), preferred_element_type=jnp.float32
    )
    grad_context = grad_context.astype(jnp.bfloat16).reshape(count, HEADS, head_size)
    grad_probs = jnp.einsum(
        "qhd,khd->hqk", grad_context, value_rows, preferred_element_type=jnp.float32
    )
    total = jnp.sum(probs * grad_probs, axis=-1, keepdims=True)
    grad_scores = (probs * (grad_probs - total) * factor).astype(jnp.bfloat16)
    grad_query = jnp.einsum("hqk,khd->qhd", grad_scores, keys, preferred_element_type=jnp.float32)
    grad_keys = jnp.einsum("hqk,qhd->khd", grad_scores, query, preferred_element_type=jnp.float32)
    grad_values = jnp.einsum(
        "hqk,qhd->khd", probs_b, grad_context, preferred_element_type=jnp.float32
    )
    grads = jnp.stack([grad_query, grad_keys, grad_values], axis=1).reshape(count, 3, -1)
    blocks = scales.shape[-1]
    grads = (grads.reshape(count, 3, blocks, -1) * scales.astype(jnp.float32)[..., None]).reshape(
        count, 3, -1
    )
    return (output, grads.astype(jnp.bfloat16), context)


def pad_rows(array, extra_rows, fill):
    extra = jnp.full((extra_rows,) + array.shape[1:], fill, array.dtype)
    return jnp.concatenate([array, extra], axis=0)


def cut_rows(buffer, at_row, length, slot):
    piece = lax.dynamic_slice_in_dim(buffer, at_row, slot, 0)
    present = (jnp.arange(slot) < length).reshape((slot,) + (1,) * (buffer.ndim - 1))
    return jnp.where(present, piece, jnp.zeros_like(piece))


def put_rows(buffer, piece, at_row, length):
    slot = piece.shape[0]
    old = lax.dynamic_slice_in_dim(buffer, at_row, slot, 0)
    present = (jnp.arange(slot) < length).reshape((slot,) + (1,) * (buffer.ndim - 1))
    return lax.dynamic_update_slice_in_dim(buffer, jnp.where(present, piece, old), at_row, 0)


def local(qkv_codes, block_scales, home_segments, kept_rows, pack_list, w_out, cotangent):
    position = lax.axis_index("dp")
    group_size = lax.axis_size("dp")
    codes = qkv_codes[0, 0]
    scales = block_scales[0, 0]
    segments = home_segments[0, 0]
    kept = kept_rows[0, 0]
    table = pack_list[:, 0]
    grad_out = cotangent[0, 0]
    row_count = codes.shape[0]
    slot = row_count // 8
    w_full = lax.all_gather(w_out, "fsdp", axis=0, tiled=True)
    inside = jnp.arange(row_count) < kept
    own_entries = lax.dynamic_index_in_dim(table, position, 0, keepdims=False)
    home_codes = pad_rows(codes, slot, 0)
    home_scales = pad_rows(scales, slot, 0)
    sent_codes = [
        cut_rows(home_codes, own_entries[route, 0], own_entries[route, 1], slot)
        for route in range(4)
    ]
    sent_scales = [
        cut_rows(home_scales, own_entries[route, 0], own_entries[route, 1], slot)
        for route in range(4)
    ]
    received = [
        shifted((sent_codes[route], sent_scales[route]), "dp", offsets[route]) for route in range(4)
    ]
    landing = []
    arrived = []
    for route in range(4):
        source = position - offsets[route]
        allowed = (source >= 0) & (source < group_size)
        entries = lax.dynamic_index_in_dim(
            table, jnp.clip(source, 0, group_size - 1), 0, keepdims=False
        )
        arrived.append(jnp.where(allowed, entries[route, 1], 0))
        landing.append(entries[route, 2])
    bal_codes = pad_rows(jnp.where(inside[:, None, None], codes, jnp.zeros_like(codes)), slot, 0)
    bal_scales = pad_rows(jnp.where(inside[:, None, None], scales, jnp.zeros_like(scales)), slot, 0)
    labels = pad_rows(jnp.where(inside, segments, -1), slot, -1)
    for route in range(4):
        bal_codes = put_rows(bal_codes, received[route][0], landing[route], arrived[route])
        bal_scales = put_rows(bal_scales, received[route][1], landing[route], arrived[route])
        marks = jnp.full((slot,), 100000 + route, jnp.int32)
        labels = put_rows(labels, marks, landing[route], arrived[route])
    output, grads, context = local_layer(
        bal_codes[:row_count], bal_scales[:row_count], labels[:row_count], w_full, grad_out
    )
    grads_padded = pad_rows(grads, slot, 0)
    going_back = [
        cut_rows(grads_padded, landing[route], arrived[route], slot) for route in range(4)
    ]
    returned = [shifted(going_back[route], "dp", -offsets[route]) for route in range(4)]
    home_grads = pad_rows(jnp.where(inside[:, None, None], grads, jnp.zeros_like(grads)), slot, 0)
    for route in range(4):
        home_grads = put_rows(
            home_grads, returned[route], own_entries[route, 0], own_entries[route, 1]
        )
    grad_codes = home_grads[:row_count]
    term = lax.dot_general(
        context, grad_out, (((0,), (0,)), ((), ())), preferred_element_type=jnp.float32
    )
    grad_w = lax.psum_scatter(
        term.astype(jnp.bfloat16), "fsdp", scatter_dimension=0, tiled=True
    ).astype(jnp.float32)
    return (output[None, None], grad_codes[None, None], grad_w[None])


BF = jnp.bfloat16
F32 = jnp.float32
PAIR = 256


def iota(shape, dim):
    return lax.broadcasted_iota(jnp.int32, shape, dim)


def hot(mask):
    return mask.astype(F32).astype(BF)


def mm(a, b, dims=((1,), (0,))):
    return lax.dot_general(a, b, (dims, ((), ())), preferred_element_type=F32)


def window(block, share):
    low = block * share // 128 * 128
    high = -(-(block + 1) * share // 128) * 128
    return low, high


def heads_kernel(
    groups, share, width,
    table, kept_ref, seg_ref, scales_ref, codes_hbm, w_hbm, cot_hbm,
    out_ref, grad_ref, gw_ref,
    codes, tall, scal, img_send, img_recv, w_all, cot_all, bal, qkv, scl, probs,
    out_acc, ctx_own, ctx_all, packed, back_send, back_recv,
    load_s, cot_s, cot_r, fwd_s, fwd_r, img_s, img_r, ctx_s, ctx_r, back_s, back_r,
    wsib_s, wsib_r, wx_s, wx_r, wq_s, wq_r, wf_s, wf_r,
):
    pos = lax.axis_index("dp")
    me = lax.axis_index("fsdp")
    sib = me + 1 - 2 * (me % 2)
    cross = (me + 2) % 4
    diag = (sib + 2) % 4
    peer = (me, sib, cross, diag)
    quad = pos % 4
    rows = cot_hbm.shape[0]
    slot = img_send.shape[0] // 4
    feats = 3 * width
    model = cot_hbm.shape[1]
    head = width // HEADS
    factor = 1.0 / math.sqrt(head)

    def remote(src, dst, s, r, where):
        return pltpu.make_async_remote_copy(
            src_ref=src, dst_ref=dst, send_sem=s, recv_sem=r,
            device_id=where, device_id_type=pl.DeviceIdType.MESH,
        )

    def at_dp(index):
        return (index, me)

    def at_fsdp(index):
        return (pos, index)

    loads = [
        pltpu.make_async_copy(codes_hbm, codes, load_s.at[0]),
        pltpu.make_async_copy(w_hbm, w_all.at[0, pl.ds(0, share)], load_s.at[1]),
        pltpu.make_async_copy(cot_hbm, cot_all.at[0], load_s.at[2]),
    ]
    for load in loads:
        load.start()
    img_recv[...] = jnp.zeros_like(img_recv)
    back_recv[...] = jnp.zeros_like(back_recv)

    barrier = pltpu.get_barrier_semaphore()
    for r in (1, 2, 3):
        pl.semaphore_signal(barrier, inc=1, device_id=at_fsdp(peer[r]),
                            device_id_type=pl.DeviceIdType.MESH)
    valid_to = [(pos + o >= 0) & (pos + o < groups) for o in offsets]
    valid_from = [(pos - o >= 0) & (pos - o < groups) for o in offsets]
    for d in range(4):
        @pl.when(valid_to[d])
        def _(d=d):
            pl.semaphore_signal(barrier, inc=1, device_id=at_dp(pos + offsets[d]),
                                device_id_type=pl.DeviceIdType.MESH)
    far = pos + 3 - 2 * quad
    outer = (quad == 0) | (quad == 3)

    @pl.when(outer)
    def _():
        pl.semaphore_signal(barrier, inc=1, device_id=at_dp(far),
                            device_id_type=pl.DeviceIdType.MESH)
    pl.semaphore_wait(barrier, 3 + jnp.minimum(pos, 2) + jnp.minimum(groups - 1 - pos, 2)
                      + outer.astype(jnp.int32))

    tiles = model // 128
    cuts = [tiles * i // 4 * 128 for i in range(5)]

    split = share // 2 // 16 * 16
    bands = ((0, split), (split, share - split))
    pieces = [(i, c) for i in range(4) for c in range(2)]

    def columns(ref, i, c):
        return ref.at[pl.ds(*bands[c]), pl.ds(cuts[i], cuts[i + 1] - cuts[i])]

    w_sib = remote(w_hbm, w_all.at[1, pl.ds(0, share)], wsib_s, wsib_r, at_fsdp(sib))
    w_cross = {
        (i, c): remote(columns(w_hbm, i, c), columns(w_all.at[2], i, c),
                       wx_s.at[2 * i + c], wx_r.at[2 * i + c], at_fsdp(cross))
        for i, c in pieces
    }
    w_quad = {
        (i, c, p): remote(columns(w_all.at[2], i, c), columns(w_all.at[2], i, c),
                          wq_s.at[8 * i + 4 * c + p], wq_r.at[2 * i + c], at_dp(pos - quad + p))
        for i, c in pieces for p in range(4)
    }
    w_fwd = {
        (i, c): remote(columns(w_all.at[2], i, c), columns(w_all.at[3], i, c),
                       wf_s.at[2 * i + c], wf_r.at[2 * i + c], at_fsdp(sib))
        for i, c in pieces
    }
    for i in range(4):
        @pl.when(quad == i)
        def _(i=i):
            w_cross[i, 0].start()
            w_cross[i, 1].start()
    w_sib.start()

    hr = rows // 2
    cot_out = [
        remote(cot_hbm.at[pl.ds(c * hr, hr)], cot_all.at[2, pl.ds(c * hr, hr)],
               cot_s.at[c], cot_r.at[c], at_fsdp(cross))
        for c in range(2)
    ]
    cot_sib = remote(cot_hbm, cot_all.at[1], cot_s.at[2], cot_r.at[2], at_fsdp(sib))
    forward = [
        remote(cot_all.at[2, pl.ds(c * hr, hr)], cot_all.at[3, pl.ds(c * hr, hr)],
               fwd_s.at[c], fwd_r.at[c], at_fsdp(sib))
        for c in range(2)
    ]

    kept = kept_ref[0, 0]
    r64 = iota((4 * slot, rows), 0)
    c64 = iota((4 * slot, rows), 1)

    def selection(starts, lengths):
        mask = jnp.zeros((4 * slot, rows), F32)
        for d in range(4):
            step = r64 - d * slot
            ok = (step >= 0) & (step < lengths[d]) & (step < slot) & (c64 == starts[d] + step)
            mask = mask + ok.astype(F32)
        return mask.astype(BF)

    own_start = [table[0, d, pos] for d in range(4)]
    own_len = [table[1, d, pos] for d in range(4)]
    landing, arrived = [], []
    for d in range(4):
        src = jnp.clip(pos - offsets[d], 0, groups - 1)
        landing.append(table[2, d, src])
        arrived.append(jnp.where(valid_from[d], table[1, d, src], 0))
    tall[...] = jnp.zeros_like(tall)
    for m in range(3):
        tall[m * 8:m * 8 + scales_ref.shape[1]] = scales_ref[m].astype(F32)
    rr = iota((rows, rows), 0)
    cc = iota((rows, rows), 1)
    scal[...] = mm(hot(rr == cc), tall[...].astype(BF), ((1,), (1,))).astype(BF)
    loads[0].wait()
    chosen = selection(own_start, own_len)
    for m in range(3):
        img_send[:, m * width:(m + 1) * width] = mm(chosen, codes[m]).astype(BF)
    img_send[:, feats:] = mm(chosen, scal[...]).astype(BF)
    images = []
    for d in range(4):
        part = pl.ds(d * slot, slot)
        images.append(remote(img_send.at[part], img_recv.at[part], img_s.at[d], img_r.at[d],
                             at_dp(jnp.clip(pos + offsets[d], 0, groups - 1))))

        @pl.when(valid_to[d])
        def _(d=d):
            images[d].start()

    def hand_on(c):
        for i in range(4):
            @pl.when(quad == i)
            def _(i=i):
                w_cross[i, c].wait_recv()
                for step in (1, 2, 3):
                    w_quad[i, c, i ^ step].start()
                w_fwd[i, c].start()

    hand_on(0)

    loads[1].wait()
    loads[2].wait()
    for r in range(4):
        w_all[r, share:PAIR] = jnp.zeros((PAIR - share, model), BF)
    gc_own = mm(cot_all[0], w_all[0], ((1,), (1,))).astype(BF)

    keep = iota((rows, 1), 0) < kept
    lanes = iota((1, PAIR), 1)
    first = hot(lanes < head)
    second = hot(lanes >= head)
    picks = []
    spreads = [None] * 12
    for j in range(4):
        low, high = window(j, share)
        picks.append(hot((iota((high - low, PAIR), 0) + low
                          == iota((high - low, PAIR), 1) + j * share)
                         & (iota((high - low, PAIR), 1) < share)))
        block = jnp.where(lanes < share, (lanes + j * share) // 128, -128)
        for m in range(3):
            spreads[m * 4 + j] = hot(iota((128, PAIR), 0) == block + m * 8)

    def placing(starts, lengths):
        r_ = iota((rows, 4 * slot), 0)
        c_ = iota((rows, 4 * slot), 1)
        mask = jnp.zeros((rows, 4 * slot), F32)
        for d in range(4):
            step = c_ - d * slot
            ok = (step >= 0) & (step < lengths[d]) & (step < slot) & (r_ == starts[d] + step)
            mask = mask + ok.astype(F32)
        return mask.astype(BF)

    row_id = iota((1, rows), 1)
    marks = jnp.where(row_id < kept, seg_ref[...], -1)
    for d in range(4):
        here = (row_id >= landing[d]) & (row_id < landing[d] + arrived[d])
        marks = jnp.where(here, 100000 + d, marks)
    marks_row = jnp.broadcast_to(marks.astype(F32), (rows, rows))
    marks_col = jnp.sum(jnp.where(rr == cc, marks_row, 0.0), axis=1, keepdims=True)
    same = marks_col == marks_row
    bias = jnp.where(same, 0.0, -jnp.inf)
    bias2 = jnp.concatenate([bias, bias], axis=0)

    hand_on(1)
    for copy in cot_out + [cot_sib]:
        copy.start()

    for d in range(4):
        @pl.when(valid_from[d])
        def _(d=d):
            images[d].wait_recv()
    place = placing(landing, arrived)
    for m in range(3):
        part = slice(m * width, (m + 1) * width)
        bal[:, part] = jnp.where(keep, codes[m], mm(place, img_recv[:, part]).astype(BF))
    bal[:, feats:] = jnp.where(keep, scal[...], mm(place, img_recv[:, feats:]).astype(BF))

    for j in range(4):
        low, high = window(j, share)
        for m in range(3):
            values = mm(bal[:, m * width + low:m * width + high], picks[j])
            scale = mm(bal[:, feats:feats + 128], spreads[m * 4 + j])
            scl[m * 4 + j] = scale.astype(BF)
            qkv[m * 4 + j] = (values * scale).astype(BF)

    def stack(x):
        return jnp.concatenate([x * first, x * second], axis=0)

    def wide(x):
        return jnp.concatenate([x[:rows], x[rows:]], axis=1)

    w_sib.wait_recv()
    ctx_out = [None] * 4
    for r in range(4):
        j = peer[r]
        scores = mm(stack(qkv[j]), qkv[4 + j], ((1,), (1,))) * factor + bias2
        top = jnp.max(scores, axis=-1, keepdims=True)
        weights = jnp.exp(scores - top)
        p = weights / jnp.sum(weights, axis=-1, keepdims=True)
        probs[r] = p
        ctx = mm(wide(p.astype(BF)), stack(qkv[8 + j])).astype(BF)
        ctx_own[r] = ctx
        if r == 0:
            ctx_all[0] = ctx
        else:
            ctx_out[r] = remote(ctx_own.at[r], ctx_all.at[r], ctx_s.at[r], ctx_r.at[r],
                                at_fsdp(j))

    for r in (1, 2, 3):
        ctx_out[r].start()

    def backward(r, gc):
        j = peer[r]
        p = probs[r]
        gstack = stack(gc)
        gp = mm(gstack, qkv[8 + j], ((1,), (1,)))
        total = jnp.sum(p * gp, axis=-1, keepdims=True)
        gs = (p * (gp - total) * factor).astype(BF)
        gq = mm(wide(gs), stack(qkv[4 + j]))
        gk = mm(gs, stack(qkv[j]), ((0,), (0,)))
        gv = mm(p.astype(BF), gstack, ((0,), (0,)))
        for m, g in enumerate((gq, gk, gv)):
            packed[m * 4 + j] = (g * scl[m * 4 + j].astype(F32)).astype(BF)

    def gradient(r):
        return mm(cot_all[0], w_all[r], ((1,), (1,))).astype(BF)

    going = selection(landing, arrived)
    returns = {
        (h, d): remote(back_send.at[h, pl.ds(d * slot, slot)],
                       back_recv.at[h, pl.ds(d * slot, slot)],
                       back_s.at[4 * h + d], back_r.at[4 * h + d],
                       at_dp(jnp.clip(pos - offsets[d], 0, groups - 1)))
        for h in range(2) for d in range(4)
    }
    parts = [(m, k, slice((2 * m + k) * PAIR, (2 * m + k + 1) * PAIR))
             for m in range(3) for k in range(2)]

    def send_back(h):
        for m, k, cols in parts:
            back_send[h, :, cols] = mm(going, packed[m * 4 + peer[2 * h + k]]).astype(BF)
        for d in range(4):
            @pl.when(valid_from[d])
            def _(d=d):
                returns[h, d].start()

    def bring_home(h):
        for d in range(4):
            @pl.when(valid_to[d])
            def _(d=d):
                returns[h, d].wait_recv()
        for m, k, cols in parts:
            at = m * 4 + peer[2 * h + k]
            placed = mm(home, back_recv[h, :, cols]).astype(BF)
            packed[at] = jnp.where(keep, packed[at], placed)

    backward(0, gc_own)
    backward(1, gradient(1))
    send_back(0)

    def projected(r):
        return mm(jnp.concatenate([ctx_own[r], ctx_own[r + 1]], axis=1),
                  w_all[r:r + 2].reshape(2 * PAIR, model))

    def weight_terms(r):
        return mm(ctx_all[r:r + 2].reshape(2 * rows, PAIR),
                  cot_all[r:r + 2].reshape(2 * rows, model), ((0,), (0,)))[:share]

    out_acc[...] = projected(0)
    cot_sib.wait_recv()
    ctx_out[1].wait_recv()
    gw_ref[...] = weight_terms(0)
    for i, c in sorted(pieces, key=lambda piece: piece[1]):
        @pl.when(quad != i)
        def _(i=i, c=c):
            w_quad[i, c, i].wait_recv()
            w_fwd[i, c].start()
    for piece in pieces:
        w_fwd[piece].wait_recv()
    backward(2, gradient(2))
    backward(3, gradient(3))
    send_back(1)

    out_ref[...] = (out_acc[...] + projected(2)).astype(BF)

    home = placing(own_start, own_len)
    bring_home(0)

    for c in range(2):
        cot_out[c].wait_recv()
        forward[c].start()
    for r in (2, 3):
        ctx_out[r].wait_recv()
    for c in range(2):
        forward[c].wait_recv()
    gw_ref[...] += weight_terms(2)

    bring_home(1)
    for m in range(3):
        blocks = [None] * (width // 128)
        for j in range(4):
            low, high = window(j, share)
            spread = hot((iota((PAIR, high - low), 1) + low
                          == iota((PAIR, high - low), 0) + j * share)
                         & (iota((PAIR, high - low), 0) < share))
            piece = mm(packed[m * 4 + j], spread)
            for b in range((high - low) // 128):
                add = piece[:, b * 128:(b + 1) * 128]
                at = low // 128 + b
                blocks[at] = add if blocks[at] is None else blocks[at] + add
        for b in range(width // 128):
            grad_ref[m, :, b * 128:(b + 1) * 128] = blocks[b].astype(BF)

    for copy in cot_out + [cot_sib, w_sib] + forward + list(w_fwd.values()) + ctx_out[1:]:
        copy.wait_send()
    for i in range(4):
        @pl.when(quad == i)
        def _(i=i):
            for c in range(2):
                w_cross[i, c].wait_send()
                for p in range(4):
                    if p != i:
                        w_quad[i, c, p].wait_send()
    for d in range(4):
        @pl.when(valid_to[d])
        def _(d=d):
            images[d].wait_send()

        @pl.when(valid_from[d])
        def _(d=d):
            returns[0, d].wait_send()
            returns[1, d].wait_send()


def write_out(a, b, c, a_out, b_out, c_out, sems):
    copies = [
        pltpu.make_async_copy(src, dst, sems.at[i])
        for i, (src, dst) in enumerate(((a, a_out), (b, b_out), (c, c_out)))
    ]
    for copy in copies:
        copy.start()
    for copy in copies:
        copy.wait()


def local_by_heads(qkv_codes, block_scales, home_segments, kept_rows, pack_list, w_out, cotangent):
    groups = lax.axis_size("dp")
    rows = qkv_codes.shape[2]
    width = qkv_codes.shape[4]
    model = w_out.shape[1]
    share = w_out.shape[0]
    slot = rows // 8
    feats = 3 * width
    vmem = pl.BlockSpec(memory_space=pltpu.VMEM)
    hbm = pl.BlockSpec(memory_space=pltpu.HBM)
    smem = pl.BlockSpec(memory_space=pltpu.SMEM)
    dma = pltpu.SemaphoreType.DMA
    out, grads, gw = pl.pallas_call(
        functools.partial(heads_kernel, groups, share, width),
        out_shape=(
            pltpu.VMEM((rows, model), BF),
            pltpu.VMEM((3, rows, width), BF),
            pltpu.VMEM((share, model), F32),
        ),
        in_specs=[smem, smem, vmem, vmem, hbm, hbm, hbm],
        out_specs=(vmem, vmem, vmem),
        scratch_shapes=[
            pltpu.VMEM((3, rows, width), BF),
            pltpu.VMEM((128, rows), F32),
            pltpu.VMEM((rows, 128), BF),
            pltpu.VMEM((4 * slot, feats + 128), BF),
            pltpu.VMEM((4 * slot, feats + 128), BF),
            pltpu.VMEM((4, PAIR, model), BF),
            pltpu.VMEM((4, rows, model), BF),
            pltpu.VMEM((rows, feats + 128), BF),
            pltpu.VMEM((12, rows, PAIR), BF),
            pltpu.VMEM((12, rows, PAIR), BF),
            pltpu.VMEM((4, 2 * rows, rows), F32),
            pltpu.VMEM((rows, model), F32),
            pltpu.VMEM((4, rows, PAIR), BF),
            pltpu.VMEM((4, rows, PAIR), BF),
            pltpu.VMEM((12, rows, PAIR), BF),
            pltpu.VMEM((2, 4 * slot, 6 * PAIR), BF),
            pltpu.VMEM((2, 4 * slot, 6 * PAIR), BF),
            dma((3,)), dma((3,)), dma((3,)), dma((2,)), dma((2,)), dma((4,)), dma((4,)),
            dma((4,)), dma((4,)), dma((8,)), dma((8,)),
            dma, dma, dma((8,)), dma((8,)), dma((32,)), dma((8,)), dma((8,)), dma((8,)),
        ],
        compiler_params=pltpu.CompilerParams(
            collective_id=0, has_side_effects=True, vmem_limit_bytes=58 * 1024 * 1024
        ),
        cost_estimate=pl.CostEstimate(
            flops=8 * rows * width * model, bytes_accessed=8 * 1024 * 1024, transcendentals=0
        ),
        name="attention_by_heads",
    )(
        jnp.transpose(pack_list[:, 0], (2, 1, 0)),
        kept_rows,
        home_segments[0],
        jnp.transpose(block_scales[0, 0], (1, 2, 0)),
        jnp.transpose(qkv_codes[0, 0], (1, 0, 2)),
        w_out,
        cotangent[0, 0],
    )
    results = (out, grads, gw)
    out, grads, gw = pl.pallas_call(
        write_out,
        out_shape=tuple(jax.ShapeDtypeStruct(a.shape, a.dtype) for a in results),
        in_specs=[vmem] * 3,
        out_specs=(hbm,) * 3,
        scratch_shapes=[dma((3,))],
        compiler_params=pltpu.CompilerParams(vmem_limit_bytes=4 * 1024 * 1024),
        name="write_out",
    )(*results)
    return (out[None, None], jnp.transpose(grads, (1, 0, 2))[None, None], gw[None])


def solution(mesh):
    fast = mesh.shape["fsdp"] == 4 and mesh.shape["dp"] % 4 == 0
    return jax.shard_map(
        local_by_heads if fast else local,
        mesh=mesh,
        in_specs=(
            P("dp", "fsdp", None, None, None),
            P("dp", "fsdp", None, None, None),
            P("dp", "fsdp", None),
            P("dp", "fsdp"),
            P(None, "fsdp", None, None),
            P("fsdp", None),
            P("dp", "fsdp", None, None),
        ),
        out_specs=(
            P("dp", "fsdp", None, None),
            P("dp", "fsdp", None, None, None),
            P("dp", "fsdp", None),
        ),
        check_vma=False,
    )
```
